32 devices in a mesh: ctx: 4 (over z), fsdp: 8 (over y, x, core).
Axes of the slice: x: 2, y: 2, z: 4, core: 2. Of those that a mesh axis runs over, the one named last changes fastest.
Arguments:
- layer_input: bfloat16 [8, 1280, 2048], P('fsdp', 'ctx'), may hold values from -6 to 6
- grad_output: bfloat16 [8, 1280, 2048], P('fsdp', 'ctx'), may hold values from -6 to 6
- routes: int32 [8, 1280, 6], P('fsdp', 'ctx'), may hold values from 0 to 15, all different within a row
- continuation_prompt: int32 [8, 2], P('fsdp'), may hold values from 0 to 1
- block_order: int32 [8], replicated, may hold values from 0 to 7, each once
- query_weight: bfloat16 [2048, 3072], P('fsdp'), may hold values from -0.125 to 0.125
- latent_down: bfloat16 [2048, 576], P('fsdp'), may hold values from -0.125 to 0.125
- latent_up: bfloat16 [512, 4096], P('fsdp'), may hold values from -0.25 to 0.25
- output_weight: bfloat16 [2048, 2048], P('fsdp'), may hold values from -1 to 1
- router_weight: bfloat16 [2048, 16], P('fsdp'), may hold values from -0.0625 to 0.0625
- shared_gate: bfloat16 [2048, 2816], P('fsdp'), may hold values from -0.125 to 0.125
- shared_up: bfloat16 [2048, 2816], P('fsdp'), may hold values from -0.125 to 0.125
- shared_down: bfloat16 [2816, 2048], P('fsdp'), may hold values from -0.109375 to 0.109375
- attn_gain: bfloat16 [2048], P('fsdp'), may hold values from 0.5 to 1.5
- latent_gain: bfloat16 [512], P('fsdp'), may hold values from 0.5 to 1.5
- ffn_gain: bfloat16 [2048], P('fsdp'), may hold values from 0.5 to 1.5
- expert_gate: bfloat16 [32, 2048, 704], P(('ctx', 'fsdp')), may hold values from -0.125 to 0.125
- expert_up: bfloat16 [32, 2048, 704], P(('ctx', 'fsdp')), may hold values from -0.125 to 0.125
- expert_down: bfloat16 [32, 704, 2048], P(('ctx', 'fsdp')), may hold values from -0.15625 to 0.15625
Outputs:
- layer_output: bfloat16 [8, 1280, 2048], P('fsdp', 'ctx')
- grad_input: bfloat16 [8, 1280, 2048], P('fsdp', 'ctx')
- grad_query_weight: float32 [2048, 3072], P('fsdp')
- grad_latent_down: float32 [2048, 576], P('fsdp')
- grad_latent_up: float32 [512, 4096], P('fsdp')
- grad_output_weight: float32 [2048, 2048], P('fsdp')
- grad_router_weight: float32 [2048, 16], P('fsdp')
- grad_shared_gate: float32 [2048, 2816], P('fsdp')
- grad_shared_up: float32 [2048, 2816], P('fsdp')
- grad_shared_down: float32 [2816, 2048], P('fsdp')
- grad_attn_gain: float32 [2048], P('fsdp')
- grad_latent_gain: float32 [512], P('fsdp')
- grad_ffn_gain: float32 [2048], P('fsdp')
- grad_expert_gate: float32 [32, 2048, 704], P(('ctx', 'fsdp'))
- grad_expert_up: float32 [32, 2048, 704], P(('ctx', 'fsdp'))
- grad_expert_down: float32 [32, 704, 2048], P(('ctx', 'fsdp'))
The draws below stay inside these ranges and needn't reach their ends.
Inputs may be any that keep to these rules, and one draw needn't show every extreme that they name: `routes`: within a row the 6 experts are distinct. `block_order`: each of the 8 prompt block numbers appears once.
All inputs are finite; a program needn't handle non-finite values.
Results may differ from the reference program's by a relative error of at most 0.023.
Values may be sent and summed in bfloat16 or wider, within the bound.
No kernel may reach another device: no remote copies, remote signals or barrier semaphores. Data moves between devices by JAX's collectives and lax.ppermute only.
A program may use at most 576 MiB of HBM per device.

```python
import jax
import jax.numpy as jnp
from jax import lax

D = 2048
HEADS = 16
NOPE = 128
ROPE = 64
VDIM = 128
KV_RANK = 512
MOE_FF = 1408
SH_FF = 2816
TOP = 6
PROMPT = 512
PROMPTS = 2
CONT_LEN = 128
CONTS = 2
EXPERTS = 16
HALF_FF = 704
GROUP_TOK = 1280
TOK_DEV = 320
GROUPS = 8
PB = 64
C_DEV = 64
CAP = 150
N_CTX = 4


def set_ends(drawn, rng, low, high):
    shape = drawn.shape
    index_at = [jax.random.randint(jax.random.fold_in(rng, axis), (), 0, shape[axis]) for axis in range(len(shape))]
    drawn = drawn.at[tuple(index_at)].set(low)
    longest = shape.index(max(shape))
    index_at[longest] = (index_at[longest] + 1) % shape[longest]
    return drawn.at[tuple(index_at)].set(high)


def block_scale(key, extent, shards, least, largest):
    level = 1.0
    for axis_at, parts in shards:
        steps = jax.random.uniform(jax.random.fold_in(jax.random.fold_in(key, 6), axis_at), (parts,), jnp.float32, least / len(shards), largest / len(shards))
        level = level * jnp.repeat(jnp.exp(steps), extent[axis_at] // parts).reshape((-1,) + (1,) * (len(extent) - 1 - axis_at))
    return level


def choose_distinct(stream_key, rows, number_of, top, lift):
    ranking = jax.random.permutation(jax.random.fold_in(stream_key, 1), number_of)
    favour = ranking
    for power in range(3):
        favour = favour * favour // number_of
    favour = favour * lift // number_of
    tickets = jax.random.randint(jax.random.fold_in(stream_key, 2), (rows, number_of), 0, 4096) + favour
    sure = jax.random.permutation(jax.random.fold_in(stream_key, 3), rows)[jnp.arange(number_of) % rows]
    tickets = jnp.where(jnp.arange(rows)[:, None] == sure[None, :], 1 << 14, tickets)
    score = tickets * number_of + jnp.arange(number_of)
    return lax.top_k(score.astype(jnp.int32), top)[1].astype(jnp.int32)


def bell_draw(key, shape, scale, most, split=(), kind=jnp.bfloat16):
    drawn = scale * jax.random.normal(key, shape, jnp.float32)
    if split:
        drawn = drawn * block_scale(key, shape, split, -0.22, 0.18)
    return jnp.clip(drawn, -most, most).astype(kind)


def setup_inputs(seed: int = 0) -> dict:
    key_list = jax.random.split(jax.random.key(seed), 20)
    layer_input = bell_draw(key_list[0], (GROUPS, GROUP_TOK, D), 1.0, 6.0, ((0, 8), (1, 4)))
    grad_output = bell_draw(key_list[1], (GROUPS, GROUP_TOK, D), 1.0, 6.0, ((0, 8), (1, 4)))
    routes = choose_distinct(key_list[2], GROUPS * GROUP_TOK, EXPERTS, TOP, 3072).reshape((GROUPS, GROUP_TOK, TOP))
    continuation_prompt = set_ends(jax.random.randint(key_list[3], (GROUPS, CONTS), 0, PROMPTS), jax.random.fold_in(key_list[3], 1), 0, PROMPTS - 1).astype(jnp.int32)
    block_order = jax.random.permutation(key_list[4], 2 * N_CTX).astype(jnp.int32)
    query_weight = bell_draw(key_list[5], (D, HEADS * (NOPE + ROPE)), D ** -0.5, 0.125, ((0, 8),))
    latent_down = bell_draw(key_list[6], (D, KV_RANK + ROPE), D ** -0.5, 0.125, ((0, 8),))
    latent_up = bell_draw(key_list[7], (KV_RANK, HEADS * (NOPE + VDIM)), KV_RANK ** -0.5, 0.25, ((0, 8),))
    output_weight = bell_draw(key_list[8], (HEADS * VDIM, D), (HEADS * VDIM // 64) ** -0.5, 1.0, ((0, 8),))
    router_weight = bell_draw(key_list[9], (D, EXPERTS), (4 * D) ** -0.5, 0.0625, ((0, 8),))
    shared_gate = bell_draw(key_list[10], (D, SH_FF), D ** -0.5, 0.125, ((0, 8),))
    shared_up = bell_draw(key_list[11], (D, SH_FF), D ** -0.5, 0.125, ((0, 8),))
    shared_down = bell_draw(key_list[12], (SH_FF, D), SH_FF ** -0.5, 0.109375, ((0, 8),))
    attn_gain = jnp.clip(1.0 + 0.1 * jax.random.normal(key_list[13], (D,), jnp.float32), 0.5, 1.5).astype(jnp.bfloat16)
    latent_gain = jnp.clip(1.0 + 0.1 * jax.random.normal(key_list[14], (KV_RANK,), jnp.float32), 0.5, 1.5).astype(jnp.bfloat16)
    ffn_gain = jnp.clip(1.0 + 0.1 * jax.random.normal(key_list[15], (D,), jnp.float32), 0.5, 1.5).astype(jnp.bfloat16)
    expert_gate = bell_draw(key_list[16], (2 * EXPERTS, D, HALF_FF), D ** -0.5, 0.125, ((0, 32),))
    expert_up = bell_draw(key_list[17], (2 * EXPERTS, D, HALF_FF), D ** -0.5, 0.125, ((0, 32),))
    expert_down = bell_draw(key_list[18], (2 * EXPERTS, HALF_FF, D), MOE_FF ** -0.5, 0.15625, ((0, 32),))
    return {"layer_input": layer_input, "grad_output": grad_output, "routes": routes, "continuation_prompt": continuation_prompt, "block_order": block_order, "query_weight": query_weight, "latent_down": latent_down, "latent_up": latent_up, "output_weight": output_weight, "router_weight": router_weight, "shared_gate": shared_gate, "shared_up": shared_up, "shared_down": shared_down, "attn_gain": attn_gain, "latent_gain": latent_gain, "ffn_gain": ffn_gain, "expert_gate": expert_gate, "expert_up": expert_up, "expert_down": expert_down}


@jax.custom_vjp
def low(v):
    return lax.optimization_barrier(v.astype(jnp.bfloat16)).astype(jnp.float32)

@jax.custom_vjp
def low_back(v):
    return v

def low_keep(v):
    return (low(v), None)

def low_pass(kept, grad):
    return (grad,)

def back_keep(v):
    return (v, None)

def back_low(kept, grad):
    return (low(grad),)
low.defvjp(low_keep, low_pass)
low_back.defvjp(back_keep, back_low)
epsilon = 1e-06
masked_score = -1e+30
highest = lax.Precision.HIGHEST

def product(left, right):
    return jnp.dot(left, right, preferred_element_type=jnp.float32, precision=highest)

def rms_norm(values, gain):
    inverse = lax.rsqrt(lax.optimization_barrier(jnp.mean(values * values, axis=-1, keepdims=True)) + epsilon)
    return values * inverse * gain

def rotary_tables(positions):
    exponent = jnp.arange(ROPE // 2, dtype=jnp.float32) * (2.0 / ROPE)
    frequency = jnp.exp(-jnp.log(10000.0) * exponent)
    angles = positions[:, None] * frequency[None, :]
    return (jnp.cos(angles), jnp.sin(angles))

def rotate(values, cos_table, sin_table):
    half_width = values.shape[-1] // 2
    first_half = values[..., :half_width]
    second = values[..., half_width:]
    return jnp.concatenate([first_half * cos_table - second * sin_table, second * cos_table + first_half * sin_table], axis=-1)

def lookup(table_values, wanted):
    matches = wanted[:, None] == jnp.arange(table_values.shape[0], dtype=jnp.int32)[None, :]
    return lax.optimization_barrier(jnp.sum(jnp.where(matches, table_values[None, :], 0), axis=1)).astype(jnp.int32)

def row_layout(device, local_row, block_order, link_table, block_len, cont_dev):
    prompt_rows = PROMPTS * 2 * block_len
    in_prompt = local_row < prompt_rows
    prompt_id = local_row // (2 * block_len)
    half_slot = local_row // block_len % 2
    prompt_pos = lookup(block_order, 2 * device + half_slot) * block_len + local_row % block_len
    cont_index = device * cont_dev + jnp.maximum(local_row - prompt_rows, 0)
    cont_id = jnp.minimum(cont_index // CONT_LEN, CONTS - 1)
    cont_pos = cont_index % CONT_LEN
    sequence = jnp.where(in_prompt, prompt_id, PROMPTS + cont_id).astype(jnp.int32)
    position = jnp.where(in_prompt, prompt_pos, cont_pos).astype(jnp.int32)
    linked = jnp.where(in_prompt, -1, lookup(link_table, cont_id)).astype(jnp.int32)
    rotary = jnp.where(in_prompt, prompt_pos, PROMPT + cont_pos).astype(jnp.int32)
    return (sequence, position, linked, rotary)

def slot_tables(route_block, experts, capacity):
    flat_routes = route_block.reshape(-1)
    onehot = (flat_routes[:, None] == jnp.arange(experts, dtype=jnp.int32)[None, :]).astype(jnp.int32)
    slot_rank = lax.optimization_barrier(jnp.sum((jnp.cumsum(onehot, axis=0, dtype=jnp.int32) - onehot) * onehot, axis=1)).astype(jnp.int32)
    kept_pairs = slot_rank < capacity
    target = jnp.where(kept_pairs, flat_routes * capacity + slot_rank, experts * capacity).astype(jnp.int32)
    pair_count = flat_routes.shape[0]
    slot_owner = jnp.full((experts * capacity + 1,), pair_count, jnp.int32).at[target].set(jnp.arange(pair_count, dtype=jnp.int32))
    return (kept_pairs, target, slot_owner[:experts * capacity])

def block_tables(route_block):
    return slot_tables(route_block, EXPERTS, CAP)

def take_rows(rows_table, wanted):
    return rows_table[wanted]

def routed_experts(ffn_in, route_group, gate_values, expert_gate, expert_up, expert_down):
    kept_pairs, target, slot_owner = jax.vmap(block_tables)(route_group.reshape(N_CTX, TOK_DEV, TOP))
    padded = jnp.concatenate([ffn_in.reshape(N_CTX, TOK_DEV, D), jnp.zeros((N_CTX, 1, D), jnp.float32)], axis=1)
    slot_rows = jax.vmap(take_rows)(padded, slot_owner // TOP)
    slot_rows = slot_rows.reshape(N_CTX, EXPERTS, CAP, D).transpose(1, 0, 2, 3).reshape(EXPERTS, N_CTX * CAP, D)
    gate_pieces = expert_gate.reshape(EXPERTS, 2, D, HALF_FF)
    up_pieces = expert_up.reshape(EXPERTS, 2, D, HALF_FF)
    down_pieces = expert_down.reshape(EXPERTS, 2, HALF_FF, D)
    halves = []
    for half_index in range(2):
        inputs = low_back(slot_rows)
        gate_pre = low_back(jnp.einsum('erd,edf->erf', inputs, gate_pieces[:, half_index], precision=highest))
        up_pre = low_back(jnp.einsum('erd,edf->erf', inputs, up_pieces[:, half_index], precision=highest))
        activation = low(jax.nn.silu(gate_pre) * up_pre)
        halves.append(low(low_back(jnp.einsum('erf,efd->erd', activation, down_pieces[:, half_index], precision=highest))))
    expert_out = halves[0] + halves[1]
    expert_out = expert_out.reshape(EXPERTS, N_CTX, CAP, D).transpose(1, 0, 2, 3).reshape(N_CTX, EXPERTS * CAP, D)
    padded_out = jnp.concatenate([expert_out, jnp.zeros((N_CTX, 1, D), jnp.float32)], axis=1)
    pair_out = jax.vmap(take_rows)(padded_out, target).reshape(GROUP_TOK, TOP, D)
    pair_weight = gate_values * kept_pairs.reshape(GROUP_TOK, TOP).astype(jnp.float32)
    return lax.optimization_barrier(jnp.sum(pair_out * pair_weight[:, :, None], axis=1))

def group_forward(params, x_group, route_group, link_group, block_order):
    query_weight, latent_down, latent_up, output_weight, router_weight, shared_gate, shared_up, shared_down, attn_gain, latent_gain, ffn_gain, expert_gate, expert_up, expert_down = params
    row_index = jnp.arange(GROUP_TOK, dtype=jnp.int32)
    sequence, position, linked, rotary = row_layout(row_index // TOK_DEV, row_index % TOK_DEV, block_order, link_group, PB, C_DEV)
    allowed = (sequence[None, :] == sequence[:, None]) & (position[None, :] <= position[:, None]) | (sequence[None, :] == linked[:, None])
    cos_table, sin_table = rotary_tables(rotary.astype(jnp.float32))
    normed = low(rms_norm(x_group, attn_gain))
    query_pre = low_back(product(normed, query_weight))
    query_nope = low(query_pre[:, :HEADS * NOPE].reshape(GROUP_TOK, HEADS, NOPE))
    query_rope = low(rotate(query_pre[:, HEADS * NOPE:].reshape(GROUP_TOK, HEADS, ROPE), cos_table[:, None, :], sin_table[:, None, :]))
    latent_pre = low_back(product(normed, latent_down))
    latent = low(rms_norm(latent_pre[:, :KV_RANK], latent_gain))
    key_rope = low(rotate(latent_pre[:, KV_RANK:], cos_table, sin_table))
    kv_all = low(product(latent, latent_up))
    score_scale = (NOPE + ROPE) ** (-0.5)
    attended_blocks = []
    for block_index in range(N_CTX):
        rows_start = block_index * TOK_DEV
        kv_copy = low_back(kv_all)
        key_nope = kv_copy[:, :HEADS * NOPE].reshape(GROUP_TOK, HEADS, NOPE)
        values = kv_copy[:, HEADS * NOPE:].reshape(GROUP_TOK, HEADS, VDIM)
        block_nope = query_nope[rows_start:rows_start + TOK_DEV]
        block_rope = query_rope[rows_start:rows_start + TOK_DEV]
        block_allowed = allowed[rows_start:rows_start + TOK_DEV]
        raw_scores = jnp.einsum('qhd,khd->hqk', block_nope, key_nope, precision=highest) + jnp.einsum('qhd,kd->hqk', block_rope, key_rope, precision=highest)
        scores = jnp.where(block_allowed[None], low_back(raw_scores * score_scale), masked_score)
        top_score = lax.optimization_barrier(jnp.max(scores, axis=2, keepdims=True))
        exps = jnp.exp(scores - top_score)
        attn_probs = exps / lax.optimization_barrier(jnp.sum(exps, axis=2, keepdims=True))
        attended_blocks.append(jnp.einsum('hqk,khd->qhd', low(attn_probs), values, precision=highest))
    attended = jnp.concatenate(attended_blocks, axis=0)
    attended = low(low_back(attended.reshape(GROUP_TOK, HEADS * VDIM)))
    hidden = x_group + low_back(product(attended, output_weight))
    ffn_in = low(rms_norm(hidden, ffn_gain))
    logits = low_back(product(ffn_in, router_weight))
    router_exps = jnp.exp(logits - lax.optimization_barrier(jnp.max(logits, axis=1, keepdims=True)))
    router = router_exps / lax.optimization_barrier(jnp.sum(router_exps, axis=1, keepdims=True))
    chosen = jnp.take_along_axis(router, route_group, axis=1)
    gate_values = chosen / lax.optimization_barrier(jnp.sum(chosen, axis=1, keepdims=True))
    shared_gate_pre = low_back(product(ffn_in, shared_gate))
    shared_up_pre = low_back(product(ffn_in, shared_up))
    shared_out = low_back(product(low(jax.nn.silu(shared_gate_pre) * shared_up_pre), shared_down))
    routed = routed_experts(ffn_in, route_group, gate_values, expert_gate, expert_up, expert_down)
    return hidden + shared_out + routed

def reference(layer_input, grad_output, routes, continuation_prompt, block_order, query_weight, latent_down, latent_up, output_weight, router_weight, shared_gate, shared_up, shared_down, attn_gain, latent_gain, ffn_gain, expert_gate, expert_up, expert_down):
    weights = tuple((weight_arg.astype(jnp.float32) for weight_arg in (query_weight, latent_down, latent_up, output_weight, router_weight, shared_gate, shared_up, shared_down, attn_gain, latent_gain, ffn_gain, expert_gate, expert_up, expert_down)))

    def forward(params, inputs):

        def one_group(carried):
            return group_forward(params, carried[0], carried[1], carried[2], block_order)
        return lax.map(jax.checkpoint(one_group), (inputs, routes, continuation_prompt))
    outputs, pullback = jax.vjp(forward, weights, layer_input.astype(jnp.float32))
    grad_weights, grad_inputs = pullback(grad_output.astype(jnp.float32))
    return (outputs.astype(jnp.bfloat16), grad_inputs.astype(jnp.bfloat16), grad_weights[0], grad_weights[1], grad_weights[2], grad_weights[3], grad_weights[4], grad_weights[5], grad_weights[6], grad_weights[7], grad_weights[8], grad_weights[9], grad_weights[10], grad_weights[11], grad_weights[12], grad_weights[13])
```

```python
import jax
import jax.numpy as jnp
from jax import lax
from jax.sharding import PartitionSpec as P

HEADS = 16
NOPE = 128
ROPE = 64
VDIM = 128
KV_RANK = 512
TOP = 6
PROMPT = 512
PROMPTS = 2
CONT_LEN = 128
CONTS = 2


epsilon = 1e-06
masked_score = -1e30
bfloat = jnp.bfloat16
single = jnp.float32


def matmul(left, right):
    return jnp.dot(left, right, preferred_element_type=single)


def rms_forward(values, gain):
    inverse = lax.rsqrt(jnp.mean(values * values, axis=-1, keepdims=True) + epsilon)
    normal_part = values * inverse
    return (normal_part * gain, normal_part, inverse)


def rms_backward(grad_out, normal_part, inverse, gain):
    grad_normal = grad_out * gain
    grad_gain = jnp.sum(grad_out * normal_part, axis=0)
    grad_in = inverse * (
        grad_normal - normal_part * jnp.mean(grad_normal * normal_part, axis=-1, keepdims=True)
    )
    return (grad_in, grad_gain)


def rotary_tables(positions):
    exponent = jnp.arange(ROPE // 2, dtype=jnp.float32) * (2.0 / ROPE)
    frequency = jnp.exp(-jnp.log(10000.0) * exponent)
    angles = positions[:, None] * frequency[None, :]
    return (jnp.cos(angles), jnp.sin(angles))


def rotate(values, cos_table, sin_table):
    half_width = values.shape[-1] // 2
    first_half = values[..., :half_width]
    second = values[..., half_width:]
    return jnp.concatenate(
        [first_half * cos_table - second * sin_table, second * cos_table + first_half * sin_table],
        axis=-1,
    )


def lookup(table_values, wanted):
    matches = wanted[:, None] == jnp.arange(table_values.shape[0], dtype=jnp.int32)[None, :]
    return jnp.sum(jnp.where(matches, table_values[None, :], 0), axis=1)


def row_layout(device, local_row, block_order, link_table, block_len, cont_dev):
    prompt_rows = PROMPTS * 2 * block_len
    in_prompt = local_row < prompt_rows
    prompt_id = local_row // (2 * block_len)
    half_slot = local_row // block_len % 2
    prompt_pos = lookup(block_order, 2 * device + half_slot) * block_len + local_row % block_len
    cont_index = device * cont_dev + jnp.maximum(local_row - prompt_rows, 0)
    cont_id = jnp.minimum(cont_index // CONT_LEN, CONTS - 1)
    cont_pos = cont_index % CONT_LEN
    sequence = jnp.where(in_prompt, prompt_id, PROMPTS + cont_id)
    position = jnp.where(in_prompt, prompt_pos, cont_pos)
    linked = jnp.where(in_prompt, -1, lookup(link_table, cont_id))
    rotary = jnp.where(in_prompt, prompt_pos, PROMPT + cont_pos)
    return (sequence, position, linked, rotary)


def silu_grads(grad_act, gate_pre, up_pre):
    sigmoid_gate = jax.nn.sigmoid(gate_pre)
    grad_gate = (grad_act * up_pre * sigmoid_gate * (1.0 + gate_pre * (1.0 - sigmoid_gate))).astype(
        bfloat
    )
    grad_up = (grad_act * gate_pre * sigmoid_gate).astype(bfloat)
    return (grad_gate, grad_up)


def attention_scores(query_nope, query_rope, key_nope, key_rope, allowed, score_scale):
    raw_scores = jnp.einsum(
        "qhd,khd->hqk", query_nope, key_nope, preferred_element_type=single
    ) + jnp.einsum("qhd,kd->hqk", query_rope, key_rope, preferred_element_type=single)
    return jnp.where(allowed[None], raw_scores * score_scale, masked_score)


def ring_next(value):
    size = lax.axis_size("ctx")
    return lax.ppermute(value, "ctx", [(i, (i + 1) % size) for i in range(size)])


def to_chip(value, offset):
    if offset == 0:
        return value
    size = lax.axis_size("fsdp")
    return lax.ppermute(
        value, "fsdp", [(i, ((i // 2) ^ offset) * 2 + i % 2) for i in range(size)]
    )


def to_core(value):
    size = lax.axis_size("fsdp")
    return lax.ppermute(value, "fsdp", [(i, i ^ 1) for i in range(size)])


def gather_rows(value):
    return lax.all_gather(value, "fsdp", axis=0, tiled=True)


def scatter_rows(value):
    return lax.psum_scatter(value.astype(bfloat), "fsdp", scatter_dimension=0, tiled=True)


def sum_ctx(value):
    part = lax.psum_scatter(value, "ctx", scatter_dimension=0, tiled=True)
    return lax.all_gather(part, "ctx", axis=0, tiled=True).astype(single)


def rank_table(route_block, experts, capacity):
    tokens = route_block.shape[0]
    expert_ids = jnp.arange(experts, dtype=jnp.int32)
    named = jnp.any(route_block[:, :, None] == expert_ids[None, None, :], axis=1)
    order = jnp.arange(tokens, dtype=jnp.int32)
    earlier = (order[:, None] > order[None, :]).astype(bfloat)
    rank = matmul(earlier, named.astype(bfloat)).astype(jnp.int32)
    return jnp.where(named & (rank < capacity), rank, -1)


def dispatch(rows, chips):
    mine = [to_chip(rows[j], j) for j in range(chips)]
    theirs = [to_core(piece) for piece in mine]
    return jnp.concatenate(mine + theirs, axis=0)


def send_back(results, chips, kind):
    pieces = results.reshape((2 * chips, results.shape[0] // (2 * chips)) + results.shape[1:])
    other = to_core(pieces[chips:])
    total = (pieces[:chips].astype(single) + other.astype(single)).astype(kind)
    return jnp.stack([to_chip(total[j], j) for j in range(chips)])


def local(
    layer_input,
    grad_output,
    routes,
    continuation_prompt,
    block_order,
    query_weight,
    latent_down,
    latent_up,
    output_weight,
    router_weight,
    shared_gate,
    shared_up,
    shared_down,
    attn_gain,
    latent_gain,
    ffn_gain,
    expert_gate,
    expert_up,
    expert_down,
):
    ctx_size = lax.axis_size("ctx")
    fsdp_size = lax.axis_size("fsdp")
    chips = fsdp_size // 2
    device = lax.axis_index("ctx")
    chip = lax.axis_index("fsdp") // 2
    tokens = layer_input.shape[1]
    model_width = layer_input.shape[2]
    experts = router_weight.shape[1]
    group_tok = tokens * ctx_size
    block_len = PROMPT // (2 * ctx_size)
    cont_dev = CONTS * CONT_LEN // ctx_size
    capacity = (5 * tokens * TOP + 4 * experts - 1) // (4 * experts)
    slots = (capacity + 7) // 8 * 8
    score_scale = (NOPE + ROPE) ** (-0.5)
    shard_rows = latent_down.shape[0]
    down_width = latent_down.shape[1]
    hidden_dev = shared_down.shape[0] // ctx_size

    packed = gather_rows(
        jnp.concatenate(
            [
                latent_down,
                router_weight,
                attn_gain[:, None],
                ffn_gain[:, None],
                jnp.pad(latent_gain, (0, shard_rows - latent_gain.shape[0]))[:, None],
            ],
            axis=1,
        )
    )
    full_down = packed[:, :down_width]
    full_router = packed[:, down_width : down_width + experts]
    gain_attn = packed[:, down_width + experts].astype(single)
    gain_ffn = packed[:, down_width + experts + 1].astype(single)
    gain_latent = (
        packed[:, down_width + experts + 2]
        .reshape(fsdp_size, shard_rows)[:, : latent_gain.shape[0]]
        .reshape(-1)
        .astype(single)
    )
    full_query = gather_rows(query_weight)
    full_up = gather_rows(latent_up)
    full_output = gather_rows(output_weight)

    def hidden_columns(weight):
        parts = weight.reshape(shard_rows, fsdp_size, ctx_size, hidden_dev)
        return lax.dynamic_index_in_dim(parts, device, axis=2, keepdims=False).reshape(
            shard_rows, fsdp_size * hidden_dev
        )

    part_gate = gather_rows(hidden_columns(shared_gate))
    part_up = gather_rows(hidden_columns(shared_up))
    part_down = gather_rows(
        lax.dynamic_slice_in_dim(shared_down, device * hidden_dev, hidden_dev, axis=0)
    )

    own_rows = jnp.arange(tokens, dtype=jnp.int32)
    link_table = continuation_prompt[0]
    own_seq, own_pos, own_link, own_rotary = row_layout(
        device, own_rows, block_order, link_table, block_len, cont_dev
    )
    group_rows = jnp.arange(group_tok, dtype=jnp.int32)
    key_seq, key_pos, key_link, key_rotary = row_layout(
        group_rows // tokens, group_rows % tokens, block_order, link_table, block_len, cont_dev
    )
    allowed = (key_seq[None, :] == own_seq[:, None]) & (key_pos[None, :] <= own_pos[:, None]) | (
        key_seq[None, :] == own_link[:, None]
    )
    cos_table, sin_table = rotary_tables(own_rotary.astype(single))

    route_ring = [routes[0]]
    grad_ring = [grad_output[0]]
    for _ in range(ctx_size - 1):
        route_ring.append(ring_next(route_ring[-1]))
        grad_ring.append(ring_next(grad_ring[-1]))
    plane_experts = device * chips + (chip ^ jnp.arange(chips, dtype=jnp.int32))
    chosen_here = plane_experts[:, None] == jnp.arange(experts, dtype=jnp.int32)[None, :]
    rank_ring = [rank_table(block, experts, capacity) for block in route_ring]

    def here(table):
        return jnp.sum(jnp.where(chosen_here[:, None, :], table[None], 0), axis=2)

    slot_ids = jnp.arange(slots, dtype=jnp.int32)
    slot_match = [
        here(ranks)[:, None, :] == slot_ids[None, :, None] for ranks in rank_ring
    ]
    slot_pick = [match.astype(bfloat) for match in slot_match]

    def pick_rows(step, rows):
        return jnp.einsum(
            "jrt,td->jrd", slot_pick[step], rows, preferred_element_type=single
        ).astype(bfloat)

    def put_rows(step, results):
        return jnp.einsum("jrt,jrd->td", slot_pick[step], results, preferred_element_type=single)

    inputs_full = layer_input[0].astype(single)
    normed, attn_normal, attn_inverse = rms_forward(inputs_full, gain_attn)
    normed_low = normed.astype(bfloat)
    latent_pre = matmul(normed_low, full_down)
    latent, latent_normal, latent_inverse = rms_forward(latent_pre[:, :KV_RANK], gain_latent)
    latent_low = latent.astype(bfloat)
    key_rope_own = rotate(latent_pre[:, KV_RANK:], cos_table, sin_table).astype(bfloat)
    key_group = lax.all_gather(
        jnp.concatenate([latent_low, key_rope_own], axis=1), "ctx", axis=0, tiled=True
    )
    latent_group = key_group[:, :KV_RANK]
    rope_group = key_group[:, KV_RANK:]
    query_pre = matmul(normed_low, full_query)
    query_nope = query_pre[:, : HEADS * NOPE].reshape(tokens, HEADS, NOPE).astype(bfloat)
    query_rope = rotate(
        query_pre[:, HEADS * NOPE :].reshape(tokens, HEADS, ROPE),
        cos_table[:, None, :],
        sin_table[:, None, :],
    ).astype(bfloat)
    kv_group = matmul(latent_group, full_up).astype(bfloat)
    key_nope = kv_group[:, : HEADS * NOPE].reshape(group_tok, HEADS, NOPE)
    values = kv_group[:, HEADS * NOPE :].reshape(group_tok, HEADS, VDIM)
    scores = attention_scores(query_nope, query_rope, key_nope, rope_group, allowed, score_scale)
    top_score = jnp.max(scores, axis=2, keepdims=True)
    exps = jnp.exp(scores - top_score)
    row_total = jnp.sum(exps, axis=2, keepdims=True)
    log_total = top_score + jnp.log(row_total)
    probs_low = (exps / row_total).astype(bfloat)
    attended = jnp.einsum("hqk,khd->qhd", probs_low, values, preferred_element_type=single)
    attended_low = attended.reshape(tokens, HEADS * VDIM).astype(bfloat)
    hidden = inputs_full + matmul(attended_low, full_output)
    ffn_in, ffn_normal, ffn_inverse = rms_forward(hidden, gain_ffn)
    ffn_low = ffn_in.astype(bfloat)

    grad_rows_ring = [
        dispatch(pick_rows(step, grad_ring[step]), chips) for step in range(ctx_size)
    ]

    logits = matmul(ffn_low, full_router)
    router_exps = jnp.exp(logits - jnp.max(logits, axis=1, keepdims=True))
    router = router_exps / jnp.sum(router_exps, axis=1, keepdims=True)
    route_match = jnp.any(
        routes[0][:, :, None] == jnp.arange(experts, dtype=jnp.int32)[None, None, :], axis=1
    )
    chosen_total = jnp.sum(jnp.where(route_match, router, 0.0), axis=1, keepdims=True)
    gates = jnp.where(route_match, router, 0.0) / chosen_total
    pair_weight = jnp.where(rank_ring[0] >= 0, gates, 0.0)

    ffn_ring = [ffn_low]
    weight_ring = [pair_weight]
    for _ in range(ctx_size - 1):
        weight_ring.append(ring_next(weight_ring[-1]))
        ffn_ring.append(ring_next(ffn_ring[-1]))

    expert_steps = []
    grad_parts = []
    gate_parts = []
    shared_steps = []
    for step in range(ctx_size):
        slot_weight = jnp.sum(
            jnp.where(slot_match[step], here(weight_ring[step])[:, None, :], 0.0), axis=2
        )
        slot_weight = dispatch(slot_weight, chips)
        rows = dispatch(pick_rows(step, ffn_ring[step]), chips)
        grad_rows = grad_rows_ring[step]
        gate_pre = matmul(rows, expert_gate[0])
        up_pre = matmul(rows, expert_up[0])
        grad_act = jnp.einsum("rd,fd->rf", grad_rows, expert_down[0], preferred_element_type=single)
        sigmoid_gate = jax.nn.sigmoid(gate_pre)
        act = gate_pre * sigmoid_gate * up_pre
        grad_weight = jnp.sum(act.astype(bfloat).astype(single) * grad_act, axis=1)
        act_low = (act * slot_weight[:, None]).astype(bfloat)
        grad_gate_low, grad_up_low = silu_grads(grad_act * slot_weight[:, None], gate_pre, up_pre)
        grad_back = (
            jnp.einsum("rf,df->rd", grad_gate_low, expert_gate[0], preferred_element_type=single)
            + jnp.einsum("rf,df->rd", grad_up_low, expert_up[0], preferred_element_type=single)
        ).astype(bfloat)
        expert_steps.append((rows, grad_rows, act_low, grad_gate_low, grad_up_low))
        back_weight = send_back(grad_weight, chips, single)
        back_rows = send_back(grad_back, chips, bfloat)

        sh_gate_pre = matmul(ffn_ring[step], part_gate)
        sh_up_pre = matmul(ffn_ring[step], part_up)
        shared_act = (jax.nn.silu(sh_gate_pre) * sh_up_pre).astype(bfloat)
        grad_sh_act = jnp.einsum(
            "td,fd->tf", grad_ring[step], part_down, preferred_element_type=single
        )
        grad_sh_gate, grad_sh_up = silu_grads(grad_sh_act, sh_gate_pre, sh_up_pre)
        shared_steps.append((shared_act, grad_sh_gate, grad_sh_up))
        grad_parts.append(
            put_rows(step, back_rows)
            + jnp.einsum("tf,df->td", grad_sh_gate, part_gate, preferred_element_type=single)
            + jnp.einsum("tf,df->td", grad_sh_up, part_up, preferred_element_type=single)
        )
        token_weight = jnp.sum(
            jnp.where(slot_match[step], back_weight[:, :, None], 0.0), axis=1
        )
        gate_parts.append(
            jnp.sum(jnp.where(chosen_here[:, None, :], token_weight[:, :, None], 0.0), axis=0)
        )

    def ring_sum(parts, kind):
        moving = parts[1].astype(kind)
        for step in range(2, ctx_size):
            moving = (ring_next(moving).astype(single) + parts[step]).astype(kind)
        return ring_next(moving).astype(single) + parts[0]

    grad_gate_pair = jnp.where(rank_ring[0] >= 0, ring_sum(gate_parts, single), 0.0)
    grad_ffn = ring_sum(grad_parts, bfloat)

    grad_low = grad_output[0]
    grad_top = grad_low.astype(single)
    grad_chosen = (
        grad_gate_pair - jnp.sum(grad_gate_pair * gates, axis=1, keepdims=True)
    ) / chosen_total
    grad_router = jnp.where(route_match, grad_chosen, 0.0)
    grad_logits = (
        router * (grad_router - jnp.sum(router * grad_router, axis=1, keepdims=True))
    ).astype(bfloat)
    grad_w_router = jnp.einsum("td,te->de", ffn_low, grad_logits, preferred_element_type=single)
    grad_ffn = grad_ffn + jnp.einsum(
        "te,de->td", grad_logits, full_router, preferred_element_type=single
    )
    grad_hidden_norm, grad_gain_ffn = rms_backward(grad_ffn, ffn_normal, ffn_inverse, gain_ffn)
    grad_hidden = grad_top + grad_hidden_norm
    grad_attn_low = grad_hidden.astype(bfloat)

    out_parts = []
    for step in range(ctx_size):
        part_low = matmul(expert_steps[step][2], expert_down[0]).astype(bfloat)
        back_out = send_back(part_low, chips, bfloat)
        out_parts.append(put_rows(step, back_out) + matmul(shared_steps[step][0], part_down))
    layer_output = (hidden + ring_sum(out_parts, bfloat)).astype(bfloat)

    def over_steps(pairs):
        total = None
        for left, right in pairs:
            part = jnp.einsum("ra,rb->ab", left, right, preferred_element_type=single)
            total = part if total is None else total + part
        return total

    grad_piece_down = over_steps([(e[2], e[1]) for e in expert_steps])
    grad_piece_gate = over_steps([(e[0], e[3]) for e in expert_steps])
    grad_piece_up = over_steps([(e[0], e[4]) for e in expert_steps])
    grad_w_sh_down = over_steps([(s[0], g) for s, g in zip(shared_steps, grad_ring)])
    grad_w_sh_gate = over_steps([(x, s[1]) for s, x in zip(shared_steps, ffn_ring)])
    grad_w_sh_up = over_steps([(x, s[2]) for s, x in zip(shared_steps, ffn_ring)])

    grad_w_output = jnp.einsum(
        "tv,td->vd", attended_low, grad_attn_low, preferred_element_type=single
    )
    grad_attended = (
        jnp.einsum("td,vd->tv", grad_attn_low, full_output, preferred_element_type=single)
        .astype(bfloat)
        .reshape(tokens, HEADS, VDIM)
    )
    scores_again = attention_scores(
        query_nope, query_rope, key_nope, rope_group, allowed, score_scale
    )
    probs_again = jnp.exp(scores_again - log_total)
    grad_probs = jnp.einsum("qhd,khd->hqk", grad_attended, values, preferred_element_type=single)
    row_delta = jnp.sum(probs_again * grad_probs, axis=2, keepdims=True)
    grad_scores = (probs_again * (grad_probs - row_delta)).astype(bfloat)
    grad_query_nope = (
        jnp.einsum("hqk,khd->qhd", grad_scores, key_nope, preferred_element_type=single)
        * score_scale
    )
    grad_query_rope = (
        jnp.einsum("hqk,kd->qhd", grad_scores, rope_group, preferred_element_type=single)
        * score_scale
    )
    grad_key_nope = (
        jnp.einsum("hqk,qhd->khd", grad_scores, query_nope, preferred_element_type=single)
        * score_scale
    )
    grad_key_rope = (
        jnp.einsum("hqk,qhd->kd", grad_scores, query_rope, preferred_element_type=single)
        * score_scale
    )
    grad_values = jnp.einsum(
        "hqk,qhd->khd", probs_low, grad_attended, preferred_element_type=single
    )
    grad_kv_part = jnp.concatenate(
        [grad_key_nope.reshape(group_tok, -1), grad_values.reshape(group_tok, -1)], axis=1
    )
    grad_kv_block = grad_kv_part.astype(bfloat)
    grad_w_up = jnp.einsum("tc,tk->ck", latent_group, grad_kv_block, preferred_element_type=single)
    grad_latent_group = jnp.einsum(
        "tk,ck->tc", grad_kv_block, full_up, preferred_element_type=single
    )
    grad_keys_own = lax.psum_scatter(
        jnp.concatenate([grad_latent_group, grad_key_rope], axis=1).astype(bfloat),
        "ctx",
        scatter_dimension=0,
        tiled=True,
    ).astype(single)
    grad_latent = grad_keys_own[:, :KV_RANK]
    grad_rope_own = grad_keys_own[:, KV_RANK:]
    grad_latent_in, grad_gain_latent = rms_backward(
        grad_latent, latent_normal, latent_inverse, gain_latent
    )
    grad_rope_in = rotate(grad_rope_own, cos_table, -sin_table)
    grad_latent_pre = jnp.concatenate([grad_latent_in, grad_rope_in], axis=1).astype(bfloat)
    grad_rope_query = rotate(grad_query_rope, cos_table[:, None, :], -sin_table[:, None, :])
    grad_query_pre = jnp.concatenate(
        [grad_query_nope.reshape(tokens, -1), grad_rope_query.reshape(tokens, -1)], axis=1
    ).astype(bfloat)
    grad_w_query = jnp.einsum(
        "td,tq->dq", normed_low, grad_query_pre, preferred_element_type=single
    )
    grad_w_down = jnp.einsum(
        "td,tk->dk", normed_low, grad_latent_pre, preferred_element_type=single
    )
    grad_normed = jnp.einsum(
        "tq,dq->td", grad_query_pre, full_query, preferred_element_type=single
    ) + jnp.einsum("tk,dk->td", grad_latent_pre, full_down, preferred_element_type=single)
    grad_x_norm, grad_gain_attn = rms_backward(grad_normed, attn_normal, attn_inverse, gain_attn)
    grad_input = (grad_hidden + grad_x_norm).astype(bfloat)

    sum_output = sum_ctx(scatter_rows(grad_w_output))
    sum_up = sum_ctx(scatter_rows(grad_w_up))
    sum_query = sum_ctx(scatter_rows(grad_w_query))
    padded_latent = jnp.pad(
        grad_gain_latent.reshape(fsdp_size, -1),
        ((0, 0), (0, shard_rows - latent_gain.shape[0])),
    ).reshape(-1)
    sum_packed = sum_ctx(
        scatter_rows(
            jnp.concatenate(
                [
                    grad_w_down,
                    grad_w_router,
                    grad_gain_attn[:, None],
                    grad_gain_ffn[:, None],
                    padded_latent[:, None],
                ],
                axis=1,
            )
        )
    )
    sum_down = sum_packed[:, :down_width]
    sum_router = sum_packed[:, down_width : down_width + experts]
    sum_gain_attn = sum_packed[:, down_width + experts]
    sum_gain_ffn = sum_packed[:, down_width + experts + 1]
    sum_gain_latent = sum_packed[: latent_gain.shape[0], down_width + experts + 2]

    def all_columns(part):
        blocks = lax.all_gather(scatter_rows(part), "ctx", axis=0)
        blocks = blocks.reshape(ctx_size, shard_rows, fsdp_size, hidden_dev)
        return blocks.transpose(1, 2, 0, 3).reshape(shard_rows, -1).astype(single)

    sum_sh_gate = all_columns(grad_w_sh_gate)
    sum_sh_up = all_columns(grad_w_sh_up)
    sum_sh_down = lax.all_gather(
        scatter_rows(grad_w_sh_down), "ctx", axis=0, tiled=True
    ).astype(single)
    return (
        layer_output[None],
        grad_input[None],
        sum_query,
        sum_down,
        sum_up,
        sum_output,
        sum_router,
        sum_sh_gate,
        sum_sh_up,
        sum_sh_down,
        sum_gain_attn,
        sum_gain_latent,
        sum_gain_ffn,
        grad_piece_gate[None],
        grad_piece_up[None],
        grad_piece_down[None],
    )


def solution(mesh):
    in_specs = (
        P("fsdp", "ctx", None),
        P("fsdp", "ctx", None),
        P("fsdp", "ctx", None),
        P("fsdp", None),
        P(),
        P("fsdp", None),
        P("fsdp", None),
        P("fsdp", None),
        P("fsdp", None),
        P("fsdp", None),
        P("fsdp", None),
        P("fsdp", None),
        P("fsdp", None),
        P("fsdp"),
        P("fsdp"),
        P("fsdp"),
        P(("ctx", "fsdp"), None, None),
        P(("ctx", "fsdp"), None, None),
        P(("ctx", "fsdp"), None, None),
    )
    out_specs = (
        P("fsdp", "ctx", None),
        P("fsdp", "ctx", None),
        P("fsdp", None),
        P("fsdp", None),
        P("fsdp", None),
        P("fsdp", None),
        P("fsdp", None),
        P("fsdp", None),
        P("fsdp", None),
        P("fsdp", None),
        P("fsdp"),
        P("fsdp"),
        P("fsdp"),
        P(("ctx", "fsdp"), None, None),
        P(("ctx", "fsdp"), None, None),
        P(("ctx", "fsdp"), None, None),
    )
    return jax.shard_map(local, mesh=mesh, in_specs=in_specs, out_specs=out_specs, check_vma=False)
```

```python
import functools

import jax
import jax.numpy as jnp
from jax import lax
from jax.experimental import pallas as pl
from jax.experimental.layout import Layout, with_layout_constraint
from jax.experimental.pallas import tpu as pltpu
from jax.sharding import PartitionSpec as P

HEADS = 16
NOPE = 128
ROPE = 64
VDIM = 128
KV_RANK = 512
TOP = 6
PROMPT = 512
PROMPTS = 2
CONT_LEN = 128
CONTS = 2


epsilon = 1e-06
masked_score = -1e30
bfloat = jnp.bfloat16
single = jnp.float32


EXTRA = 128
by_rows = Layout(major_to_minor=(0, 1))


def matmul(left, right):
    return jnp.dot(left, right, preferred_element_type=single)


def rms_forward(values, gain):
    inverse = lax.rsqrt(jnp.mean(values * values, axis=-1, keepdims=True) + epsilon)
    normal_part = values * inverse
    return (normal_part * gain, normal_part, inverse)


def rms_backward(grad_out, normal_part, inverse, gain):
    grad_normal = grad_out * gain
    grad_gain = jnp.sum(grad_out * normal_part, axis=0)
    grad_in = inverse * (
        grad_normal - normal_part * jnp.mean(grad_normal * normal_part, axis=-1, keepdims=True)
    )
    return (grad_in, grad_gain)


def rotary_tables(positions):
    exponent = jnp.arange(ROPE // 2, dtype=jnp.float32) * (2.0 / ROPE)
    frequency = jnp.exp(-jnp.log(10000.0) * exponent)
    angles = positions[:, None] * frequency[None, :]
    return (jnp.cos(angles), jnp.sin(angles))


def rotate(values, cos_table, sin_table):
    half_width = values.shape[-1] // 2
    first_half = values[..., :half_width]
    second = values[..., half_width:]
    return jnp.concatenate(
        [first_half * cos_table - second * sin_table, second * cos_table + first_half * sin_table],
        axis=-1,
    )


def lookup(table_values, wanted):
    matches = wanted[:, None] == jnp.arange(table_values.shape[0], dtype=jnp.int32)[None, :]
    return jnp.sum(jnp.where(matches, table_values[None, :], 0), axis=1)


def row_layout(device, local_row, block_order, link_table, block_len, cont_dev):
    prompt_rows = PROMPTS * 2 * block_len
    in_prompt = local_row < prompt_rows
    prompt_id = local_row // (2 * block_len)
    half_slot = local_row // block_len % 2
    prompt_pos = lookup(block_order, 2 * device + half_slot) * block_len + local_row % block_len
    cont_index = device * cont_dev + jnp.maximum(local_row - prompt_rows, 0)
    cont_id = jnp.minimum(cont_index // CONT_LEN, CONTS - 1)
    cont_pos = cont_index % CONT_LEN
    sequence = jnp.where(in_prompt, prompt_id, PROMPTS + cont_id)
    position = jnp.where(in_prompt, prompt_pos, cont_pos)
    linked = jnp.where(in_prompt, -1, lookup(link_table, cont_id))
    rotary = jnp.where(in_prompt, prompt_pos, PROMPT + cont_pos)
    return (sequence, position, linked, rotary)


def silu_grads(grad_act, gate_pre, up_pre):
    sigmoid_gate = jax.nn.sigmoid(gate_pre)
    grad_gate = (grad_act * up_pre * sigmoid_gate * (1.0 + gate_pre * (1.0 - sigmoid_gate))).astype(
        bfloat
    )
    grad_up = (grad_act * gate_pre * sigmoid_gate).astype(bfloat)
    return (grad_gate, grad_up)


NT = (((1,), (1,)), ((), ()))
TN = (((0,), (0,)), ((), ()))


def product(left, right, dims):
    return lax.dot_general(left, right, dims, preferred_element_type=single)


def half_swap(values):
    width = values.shape[1]
    lane = lax.broadcasted_iota(jnp.int32, values.shape, 1)
    ahead = pltpu.roll(values, width - ROPE // 2, 1)
    behind = pltpu.roll(values, ROPE // 2, 1)
    return jnp.where(lane % ROPE < ROPE // 2, ahead, behind)


def head_query(nope, rotated, which):
    lane = lax.broadcasted_iota(jnp.int32, rotated.shape, 1)
    kept = jnp.where((lane >= ROPE) == (which == 1), rotated, 0.0)
    return jnp.concatenate(
        [nope[:, which * NOPE : (which + 1) * NOPE].astype(bfloat), kept.astype(bfloat)], axis=1
    )


def attend_kernel(
    rows, scale, link, nope, rope, cos, sin, keys, values, key_rope, prompt_mask, cont_mask, out, lse
):
    pair = pl.program_id(0)
    prompt_rows, cont_rows = rows
    first = prompt_rows * PROMPTS
    linked = pl.multiple_of(link[0] * PROMPT, PROMPT)
    rotated = rope[...] * cos[...] + half_swap(rope[...]) * sin[...]
    nopes = nope[...]

    @pl.when(pair == 0)
    def _():
        lse[...] = jnp.zeros_like(lse)

    def key_part(start, count, which):
        return jnp.concatenate(
            [keys[pl.ds(start, count), which * NOPE : (which + 1) * NOPE], key_rope[pl.ds(start, count), :]],
            axis=1,
        )

    def value_part(start, count, which):
        return values[pl.ds(start, count), which * VDIM : (which + 1) * VDIM]

    for which in range(2):
        query = head_query(nopes, rotated, which)
        outs = []
        logs = []
        for prompt in range(PROMPTS):
            part = query[prompt * prompt_rows : (prompt + 1) * prompt_rows]
            scores = product(part, key_part(prompt * PROMPT, PROMPT, which), NT) * scale
            scores = scores + prompt_mask[...]
            top = jnp.max(scores, axis=1, keepdims=True)
            exps = jnp.exp(scores - top)
            total = jnp.sum(exps, axis=1, keepdims=True)
            probs = (exps / total).astype(bfloat)
            outs.append(matmul(probs, value_part(prompt * PROMPT, PROMPT, which)))
            logs.append(top + jnp.log(total))
        part = query[first:]
        cont_keys = CONTS * CONT_LEN
        scores = product(part, key_part(linked, PROMPT, which), NT) * scale
        near = product(part, key_part(PROMPTS * PROMPT, cont_keys, which), NT) * scale
        near = near + cont_mask[...]
        top = jnp.maximum(
            jnp.max(scores, axis=1, keepdims=True), jnp.max(near, axis=1, keepdims=True)
        )
        exps = jnp.exp(scores - top)
        near_exps = jnp.exp(near - top)
        total = jnp.sum(exps, axis=1, keepdims=True) + jnp.sum(near_exps, axis=1, keepdims=True)
        outs.append(
            matmul((exps / total).astype(bfloat), value_part(linked, PROMPT, which))
            + matmul(
                (near_exps / total).astype(bfloat), value_part(PROMPTS * PROMPT, cont_keys, which)
            )
        )
        logs.append(top + jnp.log(total))
        out[:, which * VDIM : (which + 1) * VDIM] = jnp.concatenate(outs, axis=0).astype(bfloat)
        lane = lax.broadcasted_iota(jnp.int32, lse.shape, 1)
        lse[...] = jnp.where(lane == 2 * pair + which, jnp.concatenate(logs, axis=0), lse[...])


def attend_back_kernel(
    rows,
    scale,
    link,
    nope,
    rope,
    cos,
    sin,
    keys,
    values,
    key_rope,
    prompt_mask,
    cont_mask,
    lse,
    grad,
    grad_nope,
    grad_rope,
    grad_keys,
    grad_values,
    grad_key_rope,
    key_sum,
    value_sum,
    rope_sum,
):
    pair = pl.program_id(0)
    prompt_rows, cont_rows = rows
    first = prompt_rows * PROMPTS
    linked = pl.multiple_of(link[0] * PROMPT, PROMPT)
    cont_start = PROMPTS * PROMPT
    cont_keys = CONTS * CONT_LEN
    rotated = rope[...] * cos[...] + half_swap(rope[...]) * sin[...]
    nopes = nope[...]

    @pl.when(pair == 0)
    def _():
        rope_sum[...] = jnp.zeros_like(rope_sum)

    rope_grads = []
    for which in range(2):
        query = head_query(nopes, rotated, which)
        log_row = lse[which : which + 1, :]
        query_grads = []

        def one(lo, hi, start, count, mask):
            part = query[lo:hi]
            key_cat = jnp.concatenate(
                [
                    keys[pl.ds(start, count), which * NOPE : (which + 1) * NOPE],
                    key_rope[pl.ds(start, count), :],
                ],
                axis=1,
            )
            value = values[pl.ds(start, count), which * VDIM : (which + 1) * VDIM]
            grad_part = grad[lo:hi, which * VDIM : (which + 1) * VDIM]
            scores = product(key_cat, part, NT) * scale
            if mask is not None:
                scores = scores + mask
            probs = jnp.exp(scores - log_row[:, lo:hi])
            grad_probs = product(value, grad_part, NT)
            return part, key_cat, grad_part, probs, grad_probs

        def finish(parts, delta):
            part, key_cat, grad_part, probs, grad_probs = parts
            grad_scores = (probs * (grad_probs - delta)).astype(bfloat)
            query_grad = product(grad_scores, key_cat, TN)
            key_grad = matmul(grad_scores, part) * scale
            value_grad = matmul(probs.astype(bfloat), grad_part)
            return query_grad, key_grad, value_grad

        def delta_of(parts):
            return jnp.sum(parts[3] * parts[4], axis=0, keepdims=True)

        for prompt in range(PROMPTS):
            lo, hi = prompt * prompt_rows, (prompt + 1) * prompt_rows
            start = prompt * PROMPT
            parts = one(lo, hi, start, PROMPT, prompt_mask[...])
            query_grad, key_grad, value_grad = finish(parts, delta_of(parts))
            query_grads.append(query_grad)
            key_sum[start : start + PROMPT, :] = key_grad[:, :NOPE]
            value_sum[start : start + PROMPT, :] = value_grad
            rope_sum[start : start + PROMPT, :] += key_grad[:, NOPE:]
        far = one(first, first + cont_rows, linked, PROMPT, None)
        near = one(first, first + cont_rows, cont_start, cont_keys, cont_mask[...])
        delta = delta_of(far) + delta_of(near)
        far_query, far_key, far_value = finish(far, delta)
        near_query, near_key, near_value = finish(near, delta)
        query_grads.append(far_query + near_query)
        span = pl.ds(linked, PROMPT)
        key_sum[span, :] += far_key[:, :NOPE]
        value_sum[span, :] += far_value
        rope_sum[span, :] += far_key[:, NOPE:]
        key_sum[cont_start:, :] = near_key[:, :NOPE]
        value_sum[cont_start:, :] = near_value
        rope_sum[cont_start:, :] += near_key[:, NOPE:]
        query_grad = jnp.concatenate(query_grads, axis=0) * scale
        grad_nope[:, which * NOPE : (which + 1) * NOPE] = query_grad[:, :NOPE].astype(bfloat)
        rope_grads.append(query_grad[:, NOPE:])
        grad_keys[:, which * NOPE : (which + 1) * NOPE] = key_sum[...].astype(bfloat)
        grad_values[:, which * VDIM : (which + 1) * VDIM] = value_sum[...].astype(bfloat)
    lane = lax.broadcasted_iota(jnp.int32, rope_grads[0].shape, 1)
    both = jnp.where(lane < ROPE, rope_grads[0], rope_grads[1])
    grad_rope[...] = (both * cos[...] - half_swap(both) * sin[...]).astype(bfloat)
    grad_key_rope[...] = rope_sum[...]


def whole(shape):
    return pl.BlockSpec(shape, lambda pair: (0,) * len(shape))


def pair_specs(tokens, key_rows, prompt_mask, cont_mask):
    nope_blocks = HEADS * NOPE // (2 * ROPE)
    return [
        pl.BlockSpec(memory_space=pltpu.SMEM),
        pl.BlockSpec((tokens, 2 * NOPE), lambda pair: (0, pair)),
        pl.BlockSpec((tokens, 2 * ROPE), lambda pair: (0, nope_blocks + pair)),
        whole((tokens, 2 * ROPE)),
        whole((tokens, 2 * ROPE)),
        pl.BlockSpec((key_rows, 2 * NOPE), lambda pair: (0, pair)),
        pl.BlockSpec((key_rows, 2 * VDIM), lambda pair: (0, HEADS // 2 + pair)),
        whole((key_rows, 2 * ROPE)),
        whole(prompt_mask),
        whole(cont_mask),
    ]


def attend(rows, scale, link, query_pre, cos, sin, kv, key_rope, prompt_mask, cont_mask):
    tokens = query_pre.shape[0]
    key_rows = kv.shape[0]
    work = 2 * (rows[0] * PROMPT * PROMPTS + rows[1] * (PROMPT + CONTS * CONT_LEN)) * HEADS
    return pl.pallas_call(
        functools.partial(attend_kernel, rows, scale),
        grid=(HEADS // 2,),
        in_specs=pair_specs(tokens, key_rows, prompt_mask.shape, cont_mask.shape),
        out_specs=[
            pl.BlockSpec((tokens, 2 * VDIM), lambda pair: (0, pair)),
            whole((tokens, 128)),
        ],
        out_shape=[
            jax.ShapeDtypeStruct((tokens, HEADS * VDIM), bfloat),
            jax.ShapeDtypeStruct((tokens, 128), single),
        ],
        compiler_params=pltpu.CompilerParams(vmem_limit_bytes=40 * 2**20),
        cost_estimate=pl.CostEstimate(
            flops=work * 384, bytes_accessed=2 * kv.size + 6 * query_pre.size, transcendentals=work // 2
        ),
    )(link, query_pre, query_pre, cos, sin, kv, kv, key_rope, prompt_mask, cont_mask)


def attend_back(
    rows, scale, link, query_pre, cos, sin, kv, key_rope, prompt_mask, cont_mask, lse, grad
):
    tokens = query_pre.shape[0]
    key_rows = kv.shape[0]
    work = 2 * (rows[0] * PROMPT * PROMPTS + rows[1] * (PROMPT + CONTS * CONT_LEN)) * HEADS
    return pl.pallas_call(
        functools.partial(attend_back_kernel, rows, scale),
        grid=(HEADS // 2,),
        in_specs=pair_specs(tokens, key_rows, prompt_mask.shape, cont_mask.shape)
        + [
            pl.BlockSpec((None, 2, tokens), lambda pair: (pair, 0, 0)),
            pl.BlockSpec((tokens, 2 * VDIM), lambda pair: (0, pair)),
        ],
        out_specs=[
            pl.BlockSpec((tokens, 2 * NOPE), lambda pair: (0, pair)),
            pl.BlockSpec((tokens, 2 * ROPE), lambda pair: (0, pair)),
            pl.BlockSpec((key_rows, 2 * NOPE), lambda pair: (0, pair)),
            pl.BlockSpec((key_rows, 2 * VDIM), lambda pair: (0, pair)),
            whole((key_rows, 2 * ROPE)),
        ],
        out_shape=[
            jax.ShapeDtypeStruct((tokens, HEADS * NOPE), bfloat),
            jax.ShapeDtypeStruct((tokens, HEADS * ROPE), bfloat),
            jax.ShapeDtypeStruct((key_rows, HEADS * NOPE), bfloat),
            jax.ShapeDtypeStruct((key_rows, HEADS * VDIM), bfloat),
            jax.ShapeDtypeStruct((key_rows, 2 * ROPE), single),
        ],
        scratch_shapes=[
            pltpu.VMEM((key_rows, NOPE), single),
            pltpu.VMEM((key_rows, VDIM), single),
            pltpu.VMEM((key_rows, 2 * ROPE), single),
        ],
        compiler_params=pltpu.CompilerParams(vmem_limit_bytes=48 * 2**20),
        cost_estimate=pl.CostEstimate(
            flops=work * 1152, bytes_accessed=4 * kv.size + 10 * query_pre.size, transcendentals=work // 2
        ),
    )(link, query_pre, query_pre, cos, sin, kv, kv, key_rope, prompt_mask, cont_mask, lse, grad)


def expert_kernel(
    first_row,
    experts,
    expert,
    mine,
    theirs,
    grad_mine,
    grad_theirs,
    gate,
    up,
    down,
    *refs,
):
    back_mine, back_theirs, out_mine, out_theirs = refs[-21:-17]
    all_rows, all_grads, all_act, all_gate, all_up = refs[-17:-12]
    rows, grads, gate_w, up_w, down_w, act, grad_gate, grad_up, back, out = refs[-12:-2]
    in_sems, out_sems = refs[-2:]
    count = mine.shape[0]
    hidden, width = gate.shape
    lane = lax.broadcasted_iota(jnp.int32, (count, EXTRA), 1)
    here = lane == expert[0]
    loads = [
        pltpu.make_async_copy(source, target, in_sems.at[i])
        for i, (source, target) in enumerate(
            [
                (theirs, rows.at[1]),
                (gate, gate_w),
                (up, up_w),
                (grad_theirs, grads.at[1]),
                (down, down_w),
                (mine, rows.at[0]),
                (grad_mine, grads.at[0]),
            ]
        )
    ]
    for load in loads:
        load.start()

    def stores(half):
        span = pl.ds(first_row + half * count, count)
        pairs = [
            (back.at[half], (back_mine, back_theirs)[half]),
            (out.at[half], (out_mine, out_theirs)[half]),
            (rows.at[half, :, pl.ds(0, width)], all_rows.at[span, :]),
            (grads.at[half], all_grads.at[span, :]),
            (act.at[half], all_act.at[span, :]),
            (grad_gate.at[half], all_gate.at[span, :]),
            (grad_up.at[half], all_up.at[span, :]),
        ]
        return [
            pltpu.make_async_copy(source, target, out_sems.at[half, i])
            for i, (source, target) in enumerate(pairs)
        ]

    def one_half(turn, carry):
        half = 1 - turn

        @pl.when(turn == 0)
        def _():
            for load in loads[:5]:
                load.wait()

        @pl.when(turn == 1)
        def _():
            for load in loads[5:]:
                load.wait()

        extra = rows[half, :, width:].astype(single)
        slot_weight = jnp.sum(
            jnp.where(here | (lane == expert[0] + experts), extra, 0.0), axis=1, keepdims=True
        )
        total = jnp.zeros((count, 1), single)
        for lo in range(0, hidden, 256):
            hi = min(lo + 256, hidden)
            gate_pre = product(rows[half, :, :width], gate_w[lo:hi, :], NT)
            up_pre = product(rows[half, :, :width], up_w[lo:hi, :], NT)
            grad_act = product(grads[half], down_w[lo:hi, :], NT)
            sigmoid = 1.0 / (1.0 + jnp.exp(-gate_pre))
            silu = gate_pre * sigmoid
            value = silu * up_pre
            total = total + jnp.sum(
                value.astype(bfloat).astype(single) * grad_act, axis=1, keepdims=True
            )
            grad_act = grad_act * slot_weight
            act[half, :, lo:hi] = (value * slot_weight).astype(bfloat)
            grad_gate[half, :, lo:hi] = (
                grad_act * up_pre * sigmoid * (1.0 + gate_pre * (1.0 - sigmoid))
            ).astype(bfloat)
            grad_up[half, :, lo:hi] = (grad_act * silu).astype(bfloat)
        back[half, :, width:] = jnp.where(here, total, 0.0).astype(bfloat)
        step = min(512, width)
        for lo in range(0, width, step):
            hi = lo + step
            part = matmul(grad_gate[half], gate_w[:, lo:hi])
            part = part + matmul(grad_up[half], up_w[:, lo:hi])
            back[half, :, lo:hi] = part.astype(bfloat)
        for lo in range(0, width, step):
            hi = lo + step
            out[half, :, lo:hi] = matmul(act[half], down_w[:, lo:hi]).astype(bfloat)

        @pl.when(turn == 0)
        def _():
            for store in stores(1):
                store.start()

        @pl.when(turn == 1)
        def _():
            for store in stores(0):
                store.start()

        return carry

    lax.fori_loop(0, 2, one_half, 0)
    for half in range(2):
        for store in stores(half):
            store.wait()


def expert_call(
    step, steps, experts, expert, mine, theirs, grad_mine, grad_theirs, gate, up, down, kept
):
    count, wide = mine.shape
    hidden, width = gate.shape
    anywhere = pl.BlockSpec(memory_space=pl.ANY)
    back_shape = jax.ShapeDtypeStruct((count, wide), bfloat)
    out_shape = jax.ShapeDtypeStruct((count, width), bfloat)
    kept_shapes = [
        jax.ShapeDtypeStruct((steps * 2 * count, columns), bfloat)
        for columns in (width, width, hidden, hidden, hidden)
    ]
    outs = pl.pallas_call(
        functools.partial(expert_kernel, step * 2 * count, experts),
        in_specs=[pl.BlockSpec(memory_space=pltpu.SMEM)] + [anywhere] * (7 + len(kept)),
        out_specs=[anywhere] * 9,
        out_shape=[back_shape] * 2 + [out_shape] * 2 + kept_shapes,
        input_output_aliases={8 + i: 4 + i for i in range(len(kept))},
        scratch_shapes=[
            pltpu.VMEM((2, count, wide), bfloat),
            pltpu.VMEM((2, count, width), bfloat),
        ]
        + [pltpu.VMEM((hidden, width), bfloat)] * 3
        + [pltpu.VMEM((2, count, hidden), bfloat)] * 3
        + [pltpu.VMEM((2, count, wide), bfloat), pltpu.VMEM((2, count, width), bfloat)]
        + [pltpu.SemaphoreType.DMA((7,)), pltpu.SemaphoreType.DMA((2, 7))],
        compiler_params=pltpu.CompilerParams(vmem_limit_bytes=56 * 2**20),
        cost_estimate=pl.CostEstimate(
            flops=2 * 6 * 2 * count * width * hidden,
            bytes_accessed=2 * (12 * count * width + 3 * hidden * width + 6 * count * hidden),
            transcendentals=2 * count * hidden,
        ),
    )(expert, mine, theirs, grad_mine, grad_theirs, gate, up, down, *kept)
    return outs[:4], list(outs[4:])


def ring_next(value):
    size = lax.axis_size("ctx")
    return lax.ppermute(value, "ctx", [(i, (i + 1) % size) for i in range(size)])


def to_chips(value):
    size = lax.axis_size("fsdp")
    return lax.all_to_all(
        value,
        "fsdp",
        split_axis=0,
        concat_axis=0,
        tiled=True,
        axis_index_groups=[list(range(core, size, 2)) for core in range(2)],
    )


def to_core(value):
    size = lax.axis_size("fsdp")
    return lax.ppermute(value, "fsdp", [(i, i ^ 1) for i in range(size)])


def gather_rows(value):
    return lax.all_gather(value, "fsdp", axis=0, tiled=True)


def scatter_rows(value):
    return lax.psum_scatter(value.astype(bfloat), "fsdp", scatter_dimension=0, tiled=True)


def along_ctx(value, shift):
    size = lax.axis_size("ctx")
    return lax.ppermute(value, "ctx", [(i, (i + shift) % size) for i in range(size)])


def sum_ctx(value):
    size = lax.axis_size("ctx")
    device = lax.axis_index("ctx")
    low = ctx_total(value, device).astype(bfloat)
    pieces = [low] + [along_ctx(low, shift) for shift in range(1, size)]
    return in_order([piece.astype(single) for piece in pieces], device)


def in_order(pieces, device, axis=0):
    size = len(pieces)
    count = pieces[0].shape[axis]
    shape = list(pieces[0].shape)
    shape[axis] = size * count
    result = jnp.zeros(shape, pieces[0].dtype)
    for shift, piece in enumerate(pieces):
        owner = (device - shift + size) % size
        result = lax.dynamic_update_slice_in_dim(result, piece, owner * count, axis=axis)
    return result


def together(*values):
    return lax.optimization_barrier(values)


def ctx_total(group, device):
    size = lax.axis_size("ctx")
    count = group.shape[0] // size

    def share(owner):
        return lax.dynamic_slice_in_dim(group, owner % size * count, count, axis=0)

    total = share(device).astype(single)
    for shift in range(1, size):
        total = total + along_ctx(share(device + shift), shift).astype(single)
    return total


def rank_table(route_block, experts, capacity):
    tokens = route_block.shape[0]
    expert_ids = jnp.arange(experts, dtype=jnp.int32)
    named = jnp.any(route_block[:, :, None] == expert_ids[None, None, :], axis=1)
    order = jnp.arange(tokens, dtype=jnp.int32)
    earlier = (order[:, None] > order[None, :]).astype(bfloat)
    rank = matmul(earlier, named.astype(bfloat)).astype(jnp.int32)
    return jnp.where(named & (rank < capacity), rank, -1)


def dispatch(rows):
    mine = to_chips(rows)
    return mine, to_core(mine)


def add_halves(mine, theirs):
    return (mine.astype(single) + to_core(theirs).astype(single)).astype(bfloat)


def local(
    layer_input,
    grad_output,
    routes,
    continuation_prompt,
    block_order,
    query_weight,
    latent_down,
    latent_up,
    output_weight,
    router_weight,
    shared_gate,
    shared_up,
    shared_down,
    attn_gain,
    latent_gain,
    ffn_gain,
    expert_gate,
    expert_up,
    expert_down,
):
    ctx_size = lax.axis_size("ctx")
    fsdp_size = lax.axis_size("fsdp")
    chips = fsdp_size // 2
    device = lax.axis_index("ctx")
    tokens = layer_input.shape[1]
    model_width = layer_input.shape[2]
    experts = router_weight.shape[1]
    group_tok = tokens * ctx_size
    block_len = PROMPT // (2 * ctx_size)
    cont_dev = CONTS * CONT_LEN // ctx_size
    capacity = (5 * tokens * TOP + 4 * experts - 1) // (4 * experts)
    slots = (capacity + 7) // 8 * 8
    score_scale = (NOPE + ROPE) ** (-0.5)
    shard_rows = latent_down.shape[0]
    down_width = latent_down.shape[1]
    hidden_dev = shared_down.shape[0] // ctx_size

    def hidden_columns(weight):
        parts = weight.reshape(shard_rows, fsdp_size, ctx_size, hidden_dev)
        return lax.dynamic_index_in_dim(parts, device, axis=2, keepdims=False).reshape(
            shard_rows, fsdp_size * hidden_dev
        )

    hidden_part = fsdp_size * hidden_dev
    part_down = lax.dynamic_slice_in_dim(shared_down, device * hidden_dev, hidden_dev, axis=0)
    part_shared = jnp.concatenate(
        [
            hidden_columns(shared_gate),
            hidden_columns(shared_up),
            part_down.reshape(shard_rows, hidden_part),
        ],
        axis=1,
    )

    own_rows = jnp.arange(tokens, dtype=jnp.int32)
    link_table = continuation_prompt[0]
    own_seq, own_pos, own_link, own_rotary = row_layout(
        device, own_rows, block_order, link_table, block_len, cont_dev
    )
    prompt_rows = 2 * block_len
    first_cont = PROMPTS * prompt_rows
    link = lookup(link_table, (device * cont_dev // CONT_LEN)[None])
    key_pos = (block_order[:, None] * block_len + jnp.arange(block_len, dtype=jnp.int32)).reshape(-1)
    prompt_mask = jnp.where(key_pos[None, :] <= own_pos[:prompt_rows, None], 0.0, masked_score)
    cont_rows = device * cont_dev + jnp.arange(cont_dev, dtype=jnp.int32)
    cont_ids = jnp.arange(CONTS * CONT_LEN, dtype=jnp.int32)
    cont_mask = jnp.where(
        (cont_ids[None, :] // CONT_LEN == cont_rows[:, None] // CONT_LEN)
        & (cont_ids[None, :] <= cont_rows[:, None]),
        0.0,
        masked_score,
    )
    cos_table, sin_table = rotary_tables(own_rotary.astype(single))
    pair_cos = jnp.concatenate([cos_table] * 4, axis=1)
    pair_sin = jnp.concatenate([-sin_table, sin_table] * 2, axis=1)

    def by_sequence(group):
        blocks = group.reshape(ctx_size, tokens, -1)
        parts = [
            blocks[:, p * prompt_rows : (p + 1) * prompt_rows].reshape(PROMPT, -1)
            for p in range(PROMPTS)
        ]
        return jnp.concatenate(parts + [blocks[:, first_cont:].reshape(CONTS * CONT_LEN, -1)])

    def by_block(group):
        parts = [
            group[p * PROMPT : (p + 1) * PROMPT].reshape(ctx_size, prompt_rows, -1)
            for p in range(PROMPTS)
        ]
        last = group[PROMPTS * PROMPT :].reshape(ctx_size, cont_dev, -1)
        return jnp.concatenate(parts + [last], axis=1).reshape(group_tok, -1)

    plane_experts = device * chips + jnp.arange(chips, dtype=jnp.int32)
    chosen_here = plane_experts[:, None] == jnp.arange(experts, dtype=jnp.int32)[None, :]
    def here(table):
        return jnp.sum(jnp.where(chosen_here[:, None, :], table[None], 0), axis=2)

    slot_ids = jnp.arange(slots, dtype=jnp.int32)

    def pick_rows(step, rows):
        return jnp.einsum(
            "jrt,td->jrd", slot_pick[step], rows, preferred_element_type=single
        ).astype(bfloat)

    def put_rows(step, results):
        return jnp.einsum("jrt,jrd->td", slot_pick[step], results, preferred_element_type=single)

    def add_slots(route_block):
        ranks = rank_table(route_block, experts, capacity)
        match = here(ranks)[:, None, :] == slot_ids[None, :, None]
        slot_pick.append(match.astype(bfloat))
        return ranks

    slot_pick = []
    own_ranks = add_slots(routes[0])
    packed = gather_rows(
        jnp.concatenate(
            [
                latent_down,
                router_weight,
                attn_gain[:, None],
                ffn_gain[:, None],
                jnp.pad(latent_gain, (0, shard_rows - latent_gain.shape[0]))[:, None],
            ],
            axis=1,
        )
    )
    route_ring = [along_ctx(routes[0], s) for s in range(1, ctx_size)]
    grad_ring = [grad_output[0]]
    grad_next = ring_next(grad_ring[0])
    grad_mine = [to_chips(pick_rows(0, grad_ring[0]))]
    grad_theirs = []
    packed, query_shard, route_ring, grad_next, grad_mine[0] = together(
        packed, query_weight, route_ring, grad_next, grad_mine[0]
    )

    for route_block in route_ring:
        add_slots(route_block)
    full_down = packed[:, :down_width]
    full_router = packed[:, down_width : down_width + experts]
    gain_attn = packed[:, down_width + experts].astype(single)
    gain_ffn = packed[:, down_width + experts + 1].astype(single)
    gain_latent = (
        packed[:, down_width + experts + 2]
        .reshape(fsdp_size, shard_rows)[:, : latent_gain.shape[0]]
        .reshape(-1)
        .astype(single)
    )
    inputs_full = layer_input[0].astype(single)
    normed, attn_normal, attn_inverse = rms_forward(inputs_full, gain_attn)
    normed_low = normed.astype(bfloat)
    latent_pre = matmul(normed_low, full_down)
    latent, latent_normal, latent_inverse = rms_forward(latent_pre[:, :KV_RANK], gain_latent)
    latent_low = latent.astype(bfloat)
    key_rope_own = rotate(latent_pre[:, KV_RANK:], cos_table, sin_table).astype(bfloat)
    key_own = jnp.concatenate([latent_low, key_rope_own], axis=1)

    def more_grad_rows():
        step = len(grad_mine)
        grad_ring.append(grad_next)
        following = ring_next(grad_next) if step + 1 < ctx_size else grad_next
        theirs = to_core(grad_mine[-1])
        return following, theirs, to_chips(pick_rows(step, grad_ring[step]))

    full_query = gather_rows(query_shard)
    key_pieces = [key_own] + [along_ctx(key_own, s) for s in range(1, ctx_size)]
    grad_next, theirs, mine = more_grad_rows()
    full_query, up_shard, key_pieces, grad_next, theirs, mine = together(
        full_query, latent_up, key_pieces, grad_next, theirs, mine
    )
    grad_theirs.append(theirs)
    grad_mine.append(mine)

    full_up = gather_rows(up_shard)
    query_pre = matmul(normed_low, full_query)
    grad_next, theirs, mine = more_grad_rows()
    full_up, output_shard, query_pre, grad_next, theirs, mine = together(
        full_up, output_weight, query_pre, grad_next, theirs, mine
    )
    grad_theirs.append(theirs)
    grad_mine.append(mine)

    full_output = gather_rows(output_shard)
    key_group = by_sequence(in_order(key_pieces, device))
    latent_group = key_group[:, :KV_RANK]
    rope_pair = jnp.concatenate([key_group[:, KV_RANK:]] * 2, axis=1)
    kv_group = matmul(latent_group, full_up).astype(bfloat)
    rows_here = (prompt_rows, cont_dev)
    attended_low, log_total = attend(
        rows_here,
        score_scale,
        link,
        query_pre,
        pair_cos,
        pair_sin,
        kv_group,
        rope_pair,
        prompt_mask,
        cont_mask,
    )
    while len(grad_mine) < ctx_size:
        grad_next, theirs, mine = more_grad_rows()
        grad_theirs.append(theirs)
        grad_mine.append(mine)
    full_output, shared_shard, attended_low, grad_mine, grad_theirs = together(
        full_output, part_shared, attended_low, grad_mine, grad_theirs
    )
    grad_theirs.append(to_core(grad_mine[-1]))

    part_shared = gather_rows(shared_shard)
    hidden = inputs_full + matmul(attended_low, full_output)
    ffn_in, ffn_normal, ffn_inverse = rms_forward(hidden, gain_ffn)
    ffn_low = ffn_in.astype(bfloat)
    logits = matmul(ffn_low, full_router)
    router_exps = jnp.exp(logits - jnp.max(logits, axis=1, keepdims=True))
    router = router_exps / jnp.sum(router_exps, axis=1, keepdims=True)
    route_match = jnp.any(
        routes[0][:, :, None] == jnp.arange(experts, dtype=jnp.int32)[None, None, :], axis=1
    )
    chosen_total = jnp.sum(jnp.where(route_match, router, 0.0), axis=1, keepdims=True)
    gates = jnp.where(route_match, router, 0.0) / chosen_total
    pair_weight = jnp.where(own_ranks >= 0, gates, 0.0)

    weight_high = pair_weight.astype(bfloat)
    weight_low = (pair_weight - weight_high.astype(single)).astype(bfloat)
    ffn_wide = jnp.concatenate(
        [
            ffn_low,
            weight_high,
            weight_low,
            jnp.zeros((tokens, EXTRA - 2 * experts), bfloat),
        ],
        axis=1,
    )
    own_expert = (device * chips + lax.axis_index("fsdp") // 2)[None].astype(jnp.int32)
    kept = []
    out_sends = []

    def flat(rows):
        return rows.reshape(-1, rows.shape[-1])

    def expert_step(step, mine, theirs):
        results, kept[:] = expert_call(
            step,
            ctx_size,
            experts,
            own_expert,
            flat(mine),
            flat(theirs),
            flat(grad_mine[step]),
            flat(grad_theirs[step]),
            expert_gate[0].T,
            expert_up[0].T,
            expert_down[0],
            kept,
        )
        shaped = [rows.reshape(chips, slots, -1) for rows in results]
        out_sends.append(shaped[2:])
        return shaped[:2]

    def shared_step(first):
        rows = jnp.concatenate([block[:, :model_width] for block in ffn_ring[first : first + 2]])
        grads = jnp.concatenate(grad_ring[first : first + 2])
        gate_pre = matmul(rows, part_gate)
        up_pre = matmul(rows, part_up)
        act = (jax.nn.silu(gate_pre) * up_pre).astype(bfloat)
        grad_act = jnp.einsum("td,fd->tf", grads, part_down, preferred_element_type=single)
        grad_gate, grad_up = silu_grads(grad_act, gate_pre, up_pre)
        back = jnp.einsum("tf,df->td", grad_gate, part_gate, preferred_element_type=single)
        back = back + jnp.einsum("tf,df->td", grad_up, part_up, preferred_element_type=single)
        return rows, grads, act, grad_gate, grad_up, back

    def shared_grads():
        rows, grads, act, grad_gate, grad_up = [
            jnp.concatenate([part[i] for part in shared]) for i in range(5)
        ]
        pieces = [
            jnp.einsum("ta,tb->ab", left, right, preferred_element_type=single).astype(bfloat)
            for left, right in ((rows, grad_gate), (rows, grad_up), (act, grads))
        ]
        return jnp.concatenate(pieces[:2] + [pieces[2].reshape(model_width, hidden_part)], axis=1)

    def block_rows(parts, step):
        first = step % 2 * tokens
        return parts[step // 2][first : first + tokens]

    ffn_ring = [ffn_wide]
    shared = []
    mines, backs, added, returned, out_added = {}, {}, {}, {}, {}
    moving = None
    first_part = None

    def block_part(step):
        part = put_rows(step, returned[step])
        return part + jnp.pad(block_rows([p[5] for p in shared], step), ((0, 0), (0, EXTRA)))

    def hop(step):
        part = block_part(step)
        if moving is not None:
            part = part + moving.astype(single)
        return ring_next(part.astype(bfloat))

    for tick in range(ctx_size + 1):
        sent = {}
        if tick < ctx_size:
            sent["mine"] = to_chips(pick_rows(tick, ffn_ring[tick]))
            if tick + 1 < ctx_size:
                sent["ring"] = ring_next(ffn_ring[tick])
        else:
            sent["returned"] = to_chips(added[tick - 2])
        if tick >= 1:
            sent["back"] = expert_step(tick - 1, *mines[tick - 1])
        if 1 <= tick - 3 <= ctx_size - 3:
            sent["moving"] = hop(tick - 3)
        if tick == 0:
            sent["theirs"] = grad_theirs[-1]
        if tick == 1:
            sent["shared"] = part_shared
        names = sorted(sent)
        sent = dict(zip(names, together(*(sent[name] for name in names))))
        if tick + 1 < ctx_size:
            ffn_ring.append(sent["ring"])
        if tick >= 1:
            backs[tick - 1] = sent["back"]
        if tick == ctx_size:
            returned[tick - 2] = sent["returned"]
        moving = sent.get("moving", moving)
        if tick == 0:
            grad_theirs[-1] = sent["theirs"]
        if tick == 1:
            part_gate = sent["shared"][:, :hidden_part]
            part_up = sent["shared"][:, hidden_part : 2 * hidden_part]
            part_down = sent["shared"][:, 2 * hidden_part :].reshape(hidden_part, model_width)

        sends = {}
        if tick < ctx_size:
            sends["theirs"] = to_core(sent["mine"])
            sends["mine"] = sent["mine"]
        if tick >= 1:
            sends["added"] = add_halves(*backs[tick - 1])
        if 2 <= tick < ctx_size:
            sends["returned"] = to_chips(added[tick - 2])
        for pair in range(ctx_size // 2):
            if tick == min(2 * pair + 2, ctx_size - 1):
                shared.append(shared_step(2 * pair))
        if tick == 3:
            sends["first"] = block_part(0)
        if tick == ctx_size:
            sends["returned"] = to_chips(sends["added"])
            sends["moving"] = hop(ctx_size - 2)
            sends["shared_grads"] = shared_grads()
            sends["out"] = add_halves(*out_sends[1])
        names = sorted(sends)
        sends = dict(zip(names, together(*(sends[name] for name in names))))
        if tick < ctx_size:
            mines[tick] = (sends["mine"], sends["theirs"])
        if tick >= 1:
            added[tick - 1] = sends["added"]
        if 2 <= tick < ctx_size:
            returned[tick - 2] = sends["returned"]
        if tick == 3:
            first_part = sends["first"]
        if tick == ctx_size:
            returned[ctx_size - 1] = sends["returned"]
            moving = sends["moving"]
            out_added = sends["out"]

    shared_part = scatter_rows(sends["shared_grads"])
    out_steps = {}

    def next_out(step):
        ahead = (step + 1) % ctx_size
        return to_chips(out_added), add_halves(*out_sends[ahead]) if step else out_added

    moving, (out_steps[1], out_added) = together(hop(ctx_size - 1), next_out(1))
    grad_wide = moving.astype(single) + first_part
    grad_ffn = grad_wide[:, :model_width]
    grad_gate_pair = jnp.where(
        own_ranks >= 0, grad_wide[:, model_width : model_width + experts], 0.0
    )

    grad_low = grad_output[0]
    grad_top = grad_low.astype(single)
    grad_chosen = (
        grad_gate_pair - jnp.sum(grad_gate_pair * gates, axis=1, keepdims=True)
    ) / chosen_total
    grad_router = jnp.where(route_match, grad_chosen, 0.0)
    grad_logits = (
        router * (grad_router - jnp.sum(router * grad_router, axis=1, keepdims=True))
    ).astype(bfloat)
    grad_w_router = jnp.einsum("td,te->de", ffn_low, grad_logits, preferred_element_type=single)
    grad_ffn = grad_ffn + jnp.einsum(
        "te,de->td", grad_logits, full_router, preferred_element_type=single
    )
    grad_hidden_norm, grad_gain_ffn = rms_backward(grad_ffn, ffn_normal, ffn_inverse, gain_ffn)
    grad_hidden = grad_top + grad_hidden_norm
    grad_attn_low = grad_hidden.astype(bfloat)

    def out_hop(step, moving):
        part = put_rows(step, out_steps[step]) + block_rows(shared_out, step)
        if moving is not None:
            part = part + moving.astype(single)
        return ring_next(part.astype(bfloat))

    shared_out = [matmul(part[2], part_down) for part in shared]
    out_next = next_out(2)
    out_moving = out_hop(1, None)
    grad_attended = jnp.einsum(
        "td,vd->tv", grad_attn_low, full_output, preferred_element_type=single
    ).astype(bfloat)
    grad_w_output = jnp.einsum(
        "tv,td->vd", attended_low, grad_attn_low, preferred_element_type=single
    )
    grad_attended, out_next, shared_part, grad_w_output, out_moving = together(
        grad_attended, out_next, shared_part, grad_w_output, out_moving
    )
    out_steps[2], out_added = out_next
    output_part = scatter_rows(grad_w_output)
    shared_ring = [shared_part]

    out_moving = out_hop(2, out_moving)
    shared_next = ring_next(shared_part)

    def weight_grad(left, right):
        return jnp.einsum("ra,rb->ab", left, right, preferred_element_type=single)

    all_rows, all_grads, all_act, all_gate, all_up = kept
    grad_piece_down = weight_grad(all_act, all_grads)
    grad_piece_gate = weight_grad(all_rows, all_gate)
    grad_piece_up = weight_grad(all_rows, all_up)

    log_rows = log_total[:, :HEADS].T.reshape(HEADS // 2, 2, tokens)
    grad_nope, grad_rope, grad_key_part, grad_value_part, rope_pair_grad = attend_back(
        rows_here,
        score_scale,
        link,
        query_pre,
        pair_cos,
        pair_sin,
        kv_group,
        rope_pair,
        prompt_mask.T,
        cont_mask.T,
        log_rows,
        grad_attended,
    )
    out_next = next_out(3)
    (
        grad_nope,
        grad_rope,
        grad_key_part,
        grad_value_part,
        rope_pair_grad,
        out_next,
        out_moving,
        shared_next,
    ) = together(
        grad_nope,
        grad_rope,
        grad_key_part,
        grad_value_part,
        rope_pair_grad,
        out_next,
        out_moving,
        shared_next,
    )
    out_steps[3], out_added = out_next
    shared_ring.append(shared_next)
    shared_next = ring_next(shared_next)
    grad_kv_block = jnp.concatenate([grad_key_part, grad_value_part], axis=1)
    grad_key_rope = rope_pair_grad[:, :ROPE] + rope_pair_grad[:, ROPE:]
    grad_w_up = jnp.einsum("tc,tk->ck", latent_group, grad_kv_block, preferred_element_type=single)
    grad_latent_group = jnp.einsum(
        "tk,ck->tc", grad_kv_block, full_up, preferred_element_type=single
    )
    grad_query_pre = jnp.concatenate([grad_nope, grad_rope], axis=1)
    grad_w_query = jnp.einsum(
        "td,tq->dq", normed_low, grad_query_pre, preferred_element_type=single
    )
    grad_keys_own = ctx_total(
        by_block(jnp.concatenate([grad_latent_group, grad_key_rope], axis=1).astype(bfloat)), device
    )
    out_next = next_out(4 % ctx_size)
    grad_keys_own, output_part, grad_w_query, out_next, shared_next = together(
        grad_keys_own, output_part, grad_w_query, out_next, shared_next
    )
    out_steps[4 % ctx_size], out_added = out_next
    shared_ring.append(shared_next)
    out_moving = out_hop(3, out_moving)
    for step in range(4, ctx_size):
        out_moving = out_hop(step, out_moving)
        out_steps[(step + 1) % ctx_size], out_added = next_out((step + 1) % ctx_size)
    query_part = scatter_rows(grad_w_query)
    sum_output = sum_ctx(output_part)
    while len(shared_ring) < ctx_size:
        shared_ring.append(ring_next(shared_ring[-1]))
    grad_latent = grad_keys_own[:, :KV_RANK]
    grad_rope_own = grad_keys_own[:, KV_RANK:]
    grad_latent_in, grad_gain_latent = rms_backward(
        grad_latent, latent_normal, latent_inverse, gain_latent
    )
    grad_rope_in = rotate(grad_rope_own, cos_table, -sin_table)
    grad_latent_pre = jnp.concatenate([grad_latent_in, grad_rope_in], axis=1).astype(bfloat)
    grad_w_down = jnp.einsum(
        "td,tk->dk",
        normed_low,
        jnp.pad(grad_latent_pre, ((0, 0), (0, -down_width % 128))),
        preferred_element_type=single,
    )
    grad_normed = jnp.einsum(
        "tq,dq->td", grad_query_pre, full_query, preferred_element_type=single
    ) + jnp.einsum("tk,dk->td", grad_latent_pre, full_down, preferred_element_type=single)
    grad_x_norm, grad_gain_attn = rms_backward(grad_normed, attn_normal, attn_inverse, gain_attn)
    grad_input = (grad_hidden + grad_x_norm).astype(bfloat)

    padded_latent = jnp.pad(
        grad_gain_latent.reshape(fsdp_size, -1),
        ((0, 0), (0, shard_rows - latent_gain.shape[0])),
    ).reshape(-1)
    up_width = grad_w_up.size // model_width
    small = jnp.concatenate(
        [
            grad_w_router,
            grad_gain_attn[:, None],
            grad_gain_ffn[:, None],
            padded_latent[:, None],
        ],
        axis=1,
    ).astype(bfloat)
    packed_grads = jnp.concatenate(
        [
            grad_w_up.astype(bfloat).reshape(model_width, up_width),
            grad_w_down.astype(bfloat),
            jnp.pad(small, ((0, 0), (0, -small.shape[1] % 128))),
        ],
        axis=1,
    )
    query_part, out_moving, shared_ring, packed_grads, sum_output = together(
        query_part, out_moving, shared_ring, packed_grads, sum_output
    )
    first_out = put_rows(0, out_steps[0]) + block_rows(shared_out, 0)
    layer_output = (hidden + out_moving.astype(single) + first_out).astype(bfloat)
    packed_part = scatter_rows(with_layout_constraint(packed_grads, by_rows))
    sum_query = sum_ctx(query_part)
    packed_part, sum_query = together(packed_part, sum_query)
    sum_packed = with_layout_constraint(
        sum_ctx(with_layout_constraint(packed_part, by_rows)), by_rows
    )
    sum_up = sum_packed[:, :up_width].reshape(latent_up.shape)
    sum_down = sum_packed[:, up_width : up_width + down_width]
    sum_small = sum_packed[:, up_width + grad_w_down.shape[1] :]
    sum_router = sum_small[:, :experts]
    sum_gain_attn = sum_small[:, experts]
    sum_gain_ffn = sum_small[:, experts + 1]
    sum_gain_latent = sum_small[: latent_gain.shape[0], experts + 2]

    shared_blocks = in_order([piece[None] for piece in shared_ring], device)

    def all_columns(blocks):
        blocks = blocks.reshape(ctx_size, shard_rows, fsdp_size, hidden_dev)
        return blocks.transpose(1, 2, 0, 3).reshape(shard_rows, -1).astype(single)

    sum_sh_gate = all_columns(shared_blocks[:, :, :hidden_part])
    sum_sh_up = all_columns(shared_blocks[:, :, hidden_part : 2 * hidden_part])
    sum_sh_down = shared_blocks[:, :, 2 * hidden_part :].reshape(shared_down.shape).astype(single)
    return (
        layer_output[None],
        grad_input[None],
        sum_query,
        sum_down,
        sum_up,
        sum_output,
        sum_router,
        sum_sh_gate,
        sum_sh_up,
        sum_sh_down,
        sum_gain_attn,
        sum_gain_latent,
        sum_gain_ffn,
        grad_piece_gate[None],
        grad_piece_up[None],
        grad_piece_down[None],
    )


def solution(mesh):
    in_specs = (
        P("fsdp", "ctx", None),
        P("fsdp", "ctx", None),
        P("fsdp", "ctx", None),
        P("fsdp", None),
        P(),
        P("fsdp", None),
        P("fsdp", None),
        P("fsdp", None),
        P("fsdp", None),
        P("fsdp", None),
        P("fsdp", None),
        P("fsdp", None),
        P("fsdp", None),
        P("fsdp"),
        P("fsdp"),
        P("fsdp"),
        P(("ctx", "fsdp"), None, None),
        P(("ctx", "fsdp"), None, None),
        P(("ctx", "fsdp"), None, None),
    )
    out_specs = (
        P("fsdp", "ctx", None),
        P("fsdp", "ctx", None),
        P("fsdp", None),
        P("fsdp", None),
        P("fsdp", None),
        P("fsdp", None),
        P("fsdp", None),
        P("fsdp", None),
        P("fsdp", None),
        P("fsdp", None),
        P("fsdp"),
        P("fsdp"),
        P("fsdp"),
        P(("ctx", "fsdp"), None, None),
        P(("ctx", "fsdp"), None, None),
        P(("ctx", "fsdp"), None, None),
    )
    return jax.shard_map(local, mesh=mesh, in_specs=in_specs, out_specs=out_specs, check_vma=False)
```

```python
import functools

import jax
import jax.numpy as jnp
from jax import lax
from jax.experimental import pallas as pl
from jax.experimental.layout import Layout, with_layout_constraint
from jax.experimental.pallas import tpu as pltpu
from jax.sharding import PartitionSpec as P

HEADS = 16
NOPE = 128
ROPE = 64
VDIM = 128
KV_RANK = 512
TOP = 6
PROMPT = 512
PROMPTS = 2
CONT_LEN = 128
CONTS = 2


epsilon = 1e-06
masked_score = -1e30
bfloat = jnp.bfloat16
single = jnp.float32


EXTRA = 128
by_rows = Layout(major_to_minor=(0, 1))


def matmul(left, right):
    return jnp.dot(left, right, preferred_element_type=single)


def rms_forward(values, gain):
    inverse = lax.rsqrt(jnp.mean(values * values, axis=-1, keepdims=True) + epsilon)
    normal_part = values * inverse
    return (normal_part * gain, normal_part, inverse)


def rms_backward(grad_out, normal_part, inverse, gain):
    grad_normal = grad_out * gain
    grad_gain = jnp.sum(grad_out * normal_part, axis=0)
    grad_in = inverse * (
        grad_normal - normal_part * jnp.mean(grad_normal * normal_part, axis=-1, keepdims=True)
    )
    return (grad_in, grad_gain)


def rotary_tables(positions):
    exponent = jnp.arange(ROPE // 2, dtype=jnp.float32) * (2.0 / ROPE)
    frequency = jnp.exp(-jnp.log(10000.0) * exponent)
    angles = positions[:, None] * frequency[None, :]
    return (jnp.cos(angles), jnp.sin(angles))


def rotate(values, cos_table, sin_table):
    half_width = values.shape[-1] // 2
    first_half = values[..., :half_width]
    second = values[..., half_width:]
    return jnp.concatenate(
        [first_half * cos_table - second * sin_table, second * cos_table + first_half * sin_table],
        axis=-1,
    )


def lookup(table_values, wanted):
    matches = wanted[:, None] == jnp.arange(table_values.shape[0], dtype=jnp.int32)[None, :]
    return jnp.sum(jnp.where(matches, table_values[None, :], 0), axis=1)


def row_layout(device, local_row, block_order, link_table, block_len, cont_dev):
    prompt_rows = PROMPTS * 2 * block_len
    in_prompt = local_row < prompt_rows
    prompt_id = local_row // (2 * block_len)
    half_slot = local_row // block_len % 2
    prompt_pos = lookup(block_order, 2 * device + half_slot) * block_len + local_row % block_len
    cont_index = device * cont_dev + jnp.maximum(local_row - prompt_rows, 0)
    cont_id = jnp.minimum(cont_index // CONT_LEN, CONTS - 1)
    cont_pos = cont_index % CONT_LEN
    sequence = jnp.where(in_prompt, prompt_id, PROMPTS + cont_id)
    position = jnp.where(in_prompt, prompt_pos, cont_pos)
    linked = jnp.where(in_prompt, -1, lookup(link_table, cont_id))
    rotary = jnp.where(in_prompt, prompt_pos, PROMPT + cont_pos)
    return (sequence, position, linked, rotary)


def silu_grads(grad_act, gate_pre, up_pre):
    sigmoid_gate = jax.nn.sigmoid(gate_pre)
    grad_gate = (grad_act * up_pre * sigmoid_gate * (1.0 + gate_pre * (1.0 - sigmoid_gate))).astype(
        bfloat
    )
    grad_up = (grad_act * gate_pre * sigmoid_gate).astype(bfloat)
    return (grad_gate, grad_up)


NT = (((1,), (1,)), ((), ()))
TN = (((0,), (0,)), ((), ()))


def product(left, right, dims):
    return lax.dot_general(left, right, dims, preferred_element_type=single)


def half_swap(values):
    width = values.shape[1]
    lane = lax.broadcasted_iota(jnp.int32, values.shape, 1)
    ahead = pltpu.roll(values, width - ROPE // 2, 1)
    behind = pltpu.roll(values, ROPE // 2, 1)
    return jnp.where(lane % ROPE < ROPE // 2, ahead, behind)


def head_query(nope, rotated, which):
    lane = lax.broadcasted_iota(jnp.int32, rotated.shape, 1)
    kept = jnp.where((lane >= ROPE) == (which == 1), rotated, 0.0)
    return jnp.concatenate(
        [nope[:, which * NOPE : (which + 1) * NOPE].astype(bfloat), kept.astype(bfloat)], axis=1
    )


def attend_kernel(
    rows, scale, link, nope, rope, cos, sin, keys, values, key_rope, prompt_mask, cont_mask, out, lse
):
    pair = pl.program_id(0)
    prompt_rows, cont_rows = rows
    first = prompt_rows * PROMPTS
    linked = pl.multiple_of(link[0] * PROMPT, PROMPT)
    rotated = rope[...] * cos[...] + half_swap(rope[...]) * sin[...]
    nopes = nope[...]

    @pl.when(pair == 0)
    def _():
        lse[...] = jnp.zeros_like(lse)

    def key_part(start, count, which):
        return jnp.concatenate(
            [keys[pl.ds(start, count), which * NOPE : (which + 1) * NOPE], key_rope[pl.ds(start, count), :]],
            axis=1,
        )

    def value_part(start, count, which):
        return values[pl.ds(start, count), which * VDIM : (which + 1) * VDIM]

    for which in range(2):
        query = head_query(nopes, rotated, which)
        outs = []
        logs = []
        for prompt in range(PROMPTS):
            part = query[prompt * prompt_rows : (prompt + 1) * prompt_rows]
            scores = product(part, key_part(prompt * PROMPT, PROMPT, which), NT) * scale
            scores = scores + prompt_mask[...]
            top = jnp.max(scores, axis=1, keepdims=True)
            exps = jnp.exp(scores - top)
            total = jnp.sum(exps, axis=1, keepdims=True)
            probs = (exps / total).astype(bfloat)
            outs.append(matmul(probs, value_part(prompt * PROMPT, PROMPT, which)))
            logs.append(top + jnp.log(total))
        part = query[first:]
        cont_keys = CONTS * CONT_LEN
        scores = product(part, key_part(linked, PROMPT, which), NT) * scale
        near = product(part, key_part(PROMPTS * PROMPT, cont_keys, which), NT) * scale
        near = near + cont_mask[...]
        top = jnp.maximum(
            jnp.max(scores, axis=1, keepdims=True), jnp.max(near, axis=1, keepdims=True)
        )
        exps = jnp.exp(scores - top)
        near_exps = jnp.exp(near - top)
        total = jnp.sum(exps, axis=1, keepdims=True) + jnp.sum(near_exps, axis=1, keepdims=True)
        outs.append(
            matmul((exps / total).astype(bfloat), value_part(linked, PROMPT, which))
            + matmul(
                (near_exps / total).astype(bfloat), value_part(PROMPTS * PROMPT, cont_keys, which)
            )
        )
        logs.append(top + jnp.log(total))
        out[:, which * VDIM : (which + 1) * VDIM] = jnp.concatenate(outs, axis=0).astype(bfloat)
        lane = lax.broadcasted_iota(jnp.int32, lse.shape, 1)
        lse[...] = jnp.where(lane == 2 * pair + which, jnp.concatenate(logs, axis=0), lse[...])


def attend_back_kernel(
    rows,
    scale,
    link,
    nope,
    rope,
    cos,
    sin,
    keys,
    values,
    key_rope,
    prompt_mask,
    cont_mask,
    lse,
    grad,
    grad_nope,
    grad_rope,
    grad_keys,
    grad_values,
    grad_key_rope,
    key_sum,
    value_sum,
    rope_sum,
):
    pair = pl.program_id(0)
    prompt_rows, cont_rows = rows
    first = prompt_rows * PROMPTS
    linked = pl.multiple_of(link[0] * PROMPT, PROMPT)
    cont_start = PROMPTS * PROMPT
    cont_keys = CONTS * CONT_LEN
    rotated = rope[...] * cos[...] + half_swap(rope[...]) * sin[...]
    nopes = nope[...]

    @pl.when(pair == 0)
    def _():
        rope_sum[...] = jnp.zeros_like(rope_sum)

    rope_grads = []
    for which in range(2):
        query = head_query(nopes, rotated, which)
        log_row = lse[which : which + 1, :]
        query_grads = []

        def one(lo, hi, start, count, mask):
            part = query[lo:hi]
            key_cat = jnp.concatenate(
                [
                    keys[pl.ds(start, count), which * NOPE : (which + 1) * NOPE],
                    key_rope[pl.ds(start, count), :],
                ],
                axis=1,
            )
            value = values[pl.ds(start, count), which * VDIM : (which + 1) * VDIM]
            grad_part = grad[lo:hi, which * VDIM : (which + 1) * VDIM]
            scores = product(key_cat, part, NT) * scale
            if mask is not None:
                scores = scores + mask
            probs = jnp.exp(scores - log_row[:, lo:hi])
            grad_probs = product(value, grad_part, NT)
            return part, key_cat, grad_part, probs, grad_probs

        def finish(parts, delta):
            part, key_cat, grad_part, probs, grad_probs = parts
            grad_scores = (probs * (grad_probs - delta)).astype(bfloat)
            query_grad = product(grad_scores, key_cat, TN)
            key_grad = matmul(grad_scores, part) * scale
            value_grad = matmul(probs.astype(bfloat), grad_part)
            return query_grad, key_grad, value_grad

        def delta_of(parts):
            return jnp.sum(parts[3] * parts[4], axis=0, keepdims=True)

        for prompt in range(PROMPTS):
            lo, hi = prompt * prompt_rows, (prompt + 1) * prompt_rows
            start = prompt * PROMPT
            parts = one(lo, hi, start, PROMPT, prompt_mask[...])
            query_grad, key_grad, value_grad = finish(parts, delta_of(parts))
            query_grads.append(query_grad)
            key_sum[start : start + PROMPT, :] = key_grad[:, :NOPE]
            value_sum[start : start + PROMPT, :] = value_grad
            rope_sum[start : start + PROMPT, :] += key_grad[:, NOPE:]
        far = one(first, first + cont_rows, linked, PROMPT, None)
        near = one(first, first + cont_rows, cont_start, cont_keys, cont_mask[...])
        delta = delta_of(far) + delta_of(near)
        far_query, far_key, far_value = finish(far, delta)
        near_query, near_key, near_value = finish(near, delta)
        query_grads.append(far_query + near_query)
        span = pl.ds(linked, PROMPT)
        key_sum[span, :] += far_key[:, :NOPE]
        value_sum[span, :] += far_value
        rope_sum[span, :] += far_key[:, NOPE:]
        key_sum[cont_start:, :] = near_key[:, :NOPE]
        value_sum[cont_start:, :] = near_value
        rope_sum[cont_start:, :] += near_key[:, NOPE:]
        query_grad = jnp.concatenate(query_grads, axis=0) * scale
        grad_nope[:, which * NOPE : (which + 1) * NOPE] = query_grad[:, :NOPE].astype(bfloat)
        rope_grads.append(query_grad[:, NOPE:])
        grad_keys[:, which * NOPE : (which + 1) * NOPE] = key_sum[...].astype(bfloat)
        grad_values[:, which * VDIM : (which + 1) * VDIM] = value_sum[...].astype(bfloat)
    lane = lax.broadcasted_iota(jnp.int32, rope_grads[0].shape, 1)
    both = jnp.where(lane < ROPE, rope_grads[0], rope_grads[1])
    grad_rope[...] = (both * cos[...] - half_swap(both) * sin[...]).astype(bfloat)
    grad_key_rope[...] = rope_sum[...]


def whole(shape):
    return pl.BlockSpec(shape, lambda pair: (0,) * len(shape))


def pair_specs(tokens, key_rows, prompt_mask, cont_mask):
    nope_blocks = HEADS * NOPE // (2 * ROPE)
    return [
        pl.BlockSpec(memory_space=pltpu.SMEM),
        pl.BlockSpec((tokens, 2 * NOPE), lambda pair: (0, pair)),
        pl.BlockSpec((tokens, 2 * ROPE), lambda pair: (0, nope_blocks + pair)),
        whole((tokens, 2 * ROPE)),
        whole((tokens, 2 * ROPE)),
        pl.BlockSpec((key_rows, 2 * NOPE), lambda pair: (0, pair)),
        pl.BlockSpec((key_rows, 2 * VDIM), lambda pair: (0, HEADS // 2 + pair)),
        whole((key_rows, 2 * ROPE)),
        whole(prompt_mask),
        whole(cont_mask),
    ]


def attend(rows, scale, link, query_pre, cos, sin, kv, key_rope, prompt_mask, cont_mask):
    tokens = query_pre.shape[0]
    key_rows = kv.shape[0]
    work = 2 * (rows[0] * PROMPT * PROMPTS + rows[1] * (PROMPT + CONTS * CONT_LEN)) * HEADS
    return pl.pallas_call(
        functools.partial(attend_kernel, rows, scale),
        grid=(HEADS // 2,),
        in_specs=pair_specs(tokens, key_rows, prompt_mask.shape, cont_mask.shape),
        out_specs=[
            pl.BlockSpec((tokens, 2 * VDIM), lambda pair: (0, pair)),
            whole((tokens, 128)),
        ],
        out_shape=[
            jax.ShapeDtypeStruct((tokens, HEADS * VDIM), bfloat),
            jax.ShapeDtypeStruct((tokens, 128), single),
        ],
        compiler_params=pltpu.CompilerParams(vmem_limit_bytes=40 * 2**20),
        cost_estimate=pl.CostEstimate(
            flops=work * 384, bytes_accessed=2 * kv.size + 6 * query_pre.size, transcendentals=work // 2
        ),
    )(link, query_pre, query_pre, cos, sin, kv, kv, key_rope, prompt_mask, cont_mask)


def attend_back(
    rows, scale, link, query_pre, cos, sin, kv, key_rope, prompt_mask, cont_mask, lse, grad
):
    tokens = query_pre.shape[0]
    key_rows = kv.shape[0]
    work = 2 * (rows[0] * PROMPT * PROMPTS + rows[1] * (PROMPT + CONTS * CONT_LEN)) * HEADS
    return pl.pallas_call(
        functools.partial(attend_back_kernel, rows, scale),
        grid=(HEADS // 2,),
        in_specs=pair_specs(tokens, key_rows, prompt_mask.shape, cont_mask.shape)
        + [
            pl.BlockSpec((None, 2, tokens), lambda pair: (pair, 0, 0)),
            pl.BlockSpec((tokens, 2 * VDIM), lambda pair: (0, pair)),
        ],
        out_specs=[
            pl.BlockSpec((tokens, 2 * NOPE), lambda pair: (0, pair)),
            pl.BlockSpec((tokens, 2 * ROPE), lambda pair: (0, pair)),
            pl.BlockSpec((key_rows, 2 * NOPE), lambda pair: (0, pair)),
            pl.BlockSpec((key_rows, 2 * VDIM), lambda pair: (0, pair)),
            whole((key_rows, 2 * ROPE)),
        ],
        out_shape=[
            jax.ShapeDtypeStruct((tokens, HEADS * NOPE), bfloat),
            jax.ShapeDtypeStruct((tokens, HEADS * ROPE), bfloat),
            jax.ShapeDtypeStruct((key_rows, HEADS * NOPE), bfloat),
            jax.ShapeDtypeStruct((key_rows, HEADS * VDIM), bfloat),
            jax.ShapeDtypeStruct((key_rows, 2 * ROPE), single),
        ],
        scratch_shapes=[
            pltpu.VMEM((key_rows, NOPE), single),
            pltpu.VMEM((key_rows, VDIM), single),
            pltpu.VMEM((key_rows, 2 * ROPE), single),
        ],
        compiler_params=pltpu.CompilerParams(vmem_limit_bytes=48 * 2**20),
        cost_estimate=pl.CostEstimate(
            flops=work * 1152, bytes_accessed=4 * kv.size + 10 * query_pre.size, transcendentals=work // 2
        ),
    )(link, query_pre, query_pre, cos, sin, kv, kv, key_rope, prompt_mask, cont_mask, lse, grad)


def expert_kernel(
    first_row,
    experts,
    expert,
    mine,
    theirs,
    grad_mine,
    grad_theirs,
    gate,
    up,
    down,
    *refs,
):
    back_mine, back_theirs, out_mine, out_theirs = refs[-21:-17]
    all_rows, all_grads, all_act, all_gate, all_up = refs[-17:-12]
    rows, grads, gate_w, up_w, down_w, act, grad_gate, grad_up, back, out = refs[-12:-2]
    in_sems, out_sems = refs[-2:]
    count = mine.shape[0]
    hidden, width = gate.shape
    lane = lax.broadcasted_iota(jnp.int32, (count, EXTRA), 1)
    here = lane == expert[0]
    loads = [
        pltpu.make_async_copy(source, target, in_sems.at[i])
        for i, (source, target) in enumerate(
            [
                (theirs, rows.at[1]),
                (gate, gate_w),
                (up, up_w),
                (grad_theirs, grads.at[1]),
                (down, down_w),
                (mine, rows.at[0]),
                (grad_mine, grads.at[0]),
            ]
        )
    ]
    for load in loads:
        load.start()

    def store(half, which):
        span = pl.ds(first_row + half * count, count)
        pairs = [
            (rows.at[half, :, pl.ds(0, width)], all_rows.at[span, :]),
            (grads.at[half], all_grads.at[span, :]),
            (act.at[half], all_act.at[span, :]),
            (grad_gate.at[half], all_gate.at[span, :]),
            (grad_up.at[half], all_up.at[span, :]),
            (back.at[half], (back_mine, back_theirs)[half]),
            (out.at[half], (out_mine, out_theirs)[half]),
        ]
        source, target = pairs[which]
        return pltpu.make_async_copy(source, target, out_sems.at[half, which])

    def one_half(turn, carry):
        half = 1 - turn

        def await_loads(first, second):
            for when, which in enumerate((first, second)):
                if which:

                    @pl.when(turn == when)
                    def _(which=which):
                        for i in which:
                            loads[i].wait()

        def start_stores(which):
            for when in range(2):

                @pl.when(turn == when)
                def _(when=when):
                    for i in which:
                        store(1 - when, i).start()

        await_loads((0, 1), (5,))
        start_stores((0,))
        extra = rows[half, :, width:].astype(single)
        slot_weight = jnp.sum(
            jnp.where(here | (lane == expert[0] + experts), extra, 0.0), axis=1, keepdims=True
        )
        total = jnp.zeros((count, 1), single)
        for lo in range(0, hidden, 256):
            hi = min(lo + 256, hidden)
            gate_pre = product(rows[half, :, :width], gate_w[lo:hi, :], NT)
            if lo == 0:
                await_loads((2,), ())
            up_pre = product(rows[half, :, :width], up_w[lo:hi, :], NT)
            if lo == 0:
                await_loads((3, 4), (6,))
                start_stores((1,))
            grad_act = product(grads[half], down_w[lo:hi, :], NT)
            sigmoid = 1.0 / (1.0 + jnp.exp(-gate_pre))
            silu = gate_pre * sigmoid
            value = silu * up_pre
            total = total + jnp.sum(
                value.astype(bfloat).astype(single) * grad_act, axis=1, keepdims=True
            )
            grad_act = grad_act * slot_weight
            act[half, :, lo:hi] = (value * slot_weight).astype(bfloat)
            grad_gate[half, :, lo:hi] = (
                grad_act * up_pre * sigmoid * (1.0 + gate_pre * (1.0 - sigmoid))
            ).astype(bfloat)
            grad_up[half, :, lo:hi] = (grad_act * silu).astype(bfloat)
        start_stores((2, 3, 4))
        back[half, :, width:] = jnp.where(here, total, 0.0).astype(bfloat)
        step = min(512, width)
        for lo in range(0, width, step):
            hi = lo + step
            part = matmul(grad_gate[half], gate_w[:, lo:hi])
            part = part + matmul(grad_up[half], up_w[:, lo:hi])
            back[half, :, lo:hi] = part.astype(bfloat)
        start_stores((5,))
        for lo in range(0, width, step):
            hi = lo + step
            out[half, :, lo:hi] = matmul(act[half], down_w[:, lo:hi]).astype(bfloat)
        start_stores((6,))
        return carry

    lax.fori_loop(0, 2, one_half, 0)
    for half in range(2):
        for which in range(7):
            store(half, which).wait()


def expert_call(
    step, steps, experts, expert, mine, theirs, grad_mine, grad_theirs, gate, up, down, kept
):
    count, wide = mine.shape
    hidden, width = gate.shape
    anywhere = pl.BlockSpec(memory_space=pl.ANY)
    back_shape = jax.ShapeDtypeStruct((count, wide), bfloat)
    out_shape = jax.ShapeDtypeStruct((count, width), bfloat)
    kept_shapes = [
        jax.ShapeDtypeStruct((steps * 2 * count, columns), bfloat)
        for columns in (width, width, hidden, hidden, hidden)
    ]
    outs = pl.pallas_call(
        functools.partial(expert_kernel, step * 2 * count, experts),
        in_specs=[pl.BlockSpec(memory_space=pltpu.SMEM)] + [anywhere] * (7 + len(kept)),
        out_specs=[anywhere] * 9,
        out_shape=[back_shape] * 2 + [out_shape] * 2 + kept_shapes,
        input_output_aliases={8 + i: 4 + i for i in range(len(kept))},
        scratch_shapes=[
            pltpu.VMEM((2, count, wide), bfloat),
            pltpu.VMEM((2, count, width), bfloat),
        ]
        + [pltpu.VMEM((hidden, width), bfloat)] * 3
        + [pltpu.VMEM((2, count, hidden), bfloat)] * 3
        + [pltpu.VMEM((2, count, wide), bfloat), pltpu.VMEM((2, count, width), bfloat)]
        + [pltpu.SemaphoreType.DMA((7,)), pltpu.SemaphoreType.DMA((2, 7))],
        compiler_params=pltpu.CompilerParams(vmem_limit_bytes=56 * 2**20),
        cost_estimate=pl.CostEstimate(
            flops=2 * 6 * 2 * count * width * hidden,
            bytes_accessed=2 * (12 * count * width + 3 * hidden * width + 6 * count * hidden),
            transcendentals=2 * count * hidden,
        ),
    )(expert, mine, theirs, grad_mine, grad_theirs, gate, up, down, *kept)
    return outs[:4], list(outs[4:])


def ring_next(value):
    size = lax.axis_size("ctx")
    return lax.ppermute(value, "ctx", [(i, (i + 1) % size) for i in range(size)])


def to_chips(value):
    size = lax.axis_size("fsdp")
    return lax.all_to_all(
        value,
        "fsdp",
        split_axis=0,
        concat_axis=0,
        tiled=True,
        axis_index_groups=[list(range(core, size, 2)) for core in range(2)],
    )


def to_core(value):
    size = lax.axis_size("fsdp")
    return lax.ppermute(value, "fsdp", [(i, i ^ 1) for i in range(size)])


def gather_rows(value):
    return lax.all_gather(value, "fsdp", axis=0, tiled=True)


def scatter_rows(value):
    return lax.psum_scatter(value.astype(bfloat), "fsdp", scatter_dimension=0, tiled=True)


def along_ctx(value, shift):
    size = lax.axis_size("ctx")
    return lax.ppermute(value, "ctx", [(i, (i + shift) % size) for i in range(size)])


def column_shares(value, device):
    size = lax.axis_size("ctx")
    count = value.shape[1] // size

    def share(owner):
        return lax.dynamic_slice_in_dim(value, owner % size * count, count, axis=1)

    return [share(device)] + [along_ctx(share(device + k), k) for k in range(1, size)]


def all_columns_of(part, device):
    pieces = [part] + [along_ctx(part, shift) for shift in range(1, lax.axis_size("ctx"))]
    return in_order([piece.astype(single) for piece in pieces], device, 1)


def ctx_spread(part, device):
    pieces = [part] + [along_ctx(part, shift) for shift in range(1, lax.axis_size("ctx"))]
    return in_order([piece.astype(single) for piece in pieces], device)


def sum_ctx(value):
    device = lax.axis_index("ctx")
    return ctx_spread(ctx_total(value, device).astype(bfloat), device)


def in_order(pieces, device, axis=0):
    size = len(pieces)
    count = pieces[0].shape[axis]
    shape = list(pieces[0].shape)
    shape[axis] = size * count
    result = jnp.zeros(shape, pieces[0].dtype)
    for shift, piece in enumerate(pieces):
        owner = (device - shift + size) % size
        result = lax.dynamic_update_slice_in_dim(result, piece, owner * count, axis=axis)
    return result


def together(*values):
    return lax.optimization_barrier(values)


def ctx_total(group, device):
    size = lax.axis_size("ctx")
    count = group.shape[0] // size

    def share(owner):
        return lax.dynamic_slice_in_dim(group, owner % size * count, count, axis=0)

    total = share(device).astype(single)
    for shift in range(1, size):
        total = total + along_ctx(share(device + shift), shift).astype(single)
    return total


def rank_table(route_block, experts, capacity):
    tokens = route_block.shape[0]
    expert_ids = jnp.arange(experts, dtype=jnp.int32)
    named = jnp.any(route_block[:, :, None] == expert_ids[None, None, :], axis=1)
    order = jnp.arange(tokens, dtype=jnp.int32)
    earlier = (order[:, None] > order[None, :]).astype(bfloat)
    rank = matmul(earlier, named.astype(bfloat)).astype(jnp.int32)
    return jnp.where(named & (rank < capacity), rank, -1)


def dispatch(rows):
    mine = to_chips(rows)
    return mine, to_core(mine)


def add_halves(mine, theirs):
    return (mine.astype(single) + to_core(theirs).astype(single)).astype(bfloat)


def local(
    layer_input,
    grad_output,
    routes,
    continuation_prompt,
    block_order,
    query_weight,
    latent_down,
    latent_up,
    output_weight,
    router_weight,
    shared_gate,
    shared_up,
    shared_down,
    attn_gain,
    latent_gain,
    ffn_gain,
    expert_gate,
    expert_up,
    expert_down,
):
    ctx_size = lax.axis_size("ctx")
    fsdp_size = lax.axis_size("fsdp")
    chips = fsdp_size // 2
    device = lax.axis_index("ctx")
    tokens = layer_input.shape[1]
    model_width = layer_input.shape[2]
    experts = router_weight.shape[1]
    group_tok = tokens * ctx_size
    block_len = PROMPT // (2 * ctx_size)
    cont_dev = CONTS * CONT_LEN // ctx_size
    capacity = (5 * tokens * TOP + 4 * experts - 1) // (4 * experts)
    slots = (capacity + 7) // 8 * 8
    score_scale = (NOPE + ROPE) ** (-0.5)
    shard_rows = latent_down.shape[0]
    down_width = latent_down.shape[1]
    hidden_dev = shared_down.shape[0] // ctx_size

    def hidden_columns(weight):
        parts = weight.reshape(shard_rows, fsdp_size, ctx_size, hidden_dev)
        return lax.dynamic_index_in_dim(parts, device, axis=2, keepdims=False).reshape(
            shard_rows, fsdp_size * hidden_dev
        )

    hidden_part = fsdp_size * hidden_dev
    part_down = lax.dynamic_slice_in_dim(shared_down, device * hidden_dev, hidden_dev, axis=0)
    part_shared = jnp.concatenate([hidden_columns(shared_gate), hidden_columns(shared_up)], axis=1)

    own_rows = jnp.arange(tokens, dtype=jnp.int32)
    link_table = continuation_prompt[0]
    own_seq, own_pos, own_link, own_rotary = row_layout(
        device, own_rows, block_order, link_table, block_len, cont_dev
    )
    prompt_rows = 2 * block_len
    first_cont = PROMPTS * prompt_rows
    link = lookup(link_table, (device * cont_dev // CONT_LEN)[None])
    key_pos = (block_order[:, None] * block_len + jnp.arange(block_len, dtype=jnp.int32)).reshape(-1)
    prompt_mask = jnp.where(key_pos[None, :] <= own_pos[:prompt_rows, None], 0.0, masked_score)
    cont_rows = device * cont_dev + jnp.arange(cont_dev, dtype=jnp.int32)
    cont_ids = jnp.arange(CONTS * CONT_LEN, dtype=jnp.int32)
    cont_mask = jnp.where(
        (cont_ids[None, :] // CONT_LEN == cont_rows[:, None] // CONT_LEN)
        & (cont_ids[None, :] <= cont_rows[:, None]),
        0.0,
        masked_score,
    )
    cos_table, sin_table = rotary_tables(own_rotary.astype(single))
    pair_cos = jnp.concatenate([cos_table] * 4, axis=1)
    pair_sin = jnp.concatenate([-sin_table, sin_table] * 2, axis=1)

    def by_sequence(group):
        blocks = group.reshape(ctx_size, tokens, -1)
        parts = [
            blocks[:, p * prompt_rows : (p + 1) * prompt_rows].reshape(PROMPT, -1)
            for p in range(PROMPTS)
        ]
        return jnp.concatenate(parts + [blocks[:, first_cont:].reshape(CONTS * CONT_LEN, -1)])

    def by_block(group):
        parts = [
            group[p * PROMPT : (p + 1) * PROMPT].reshape(ctx_size, prompt_rows, -1)
            for p in range(PROMPTS)
        ]
        last = group[PROMPTS * PROMPT :].reshape(ctx_size, cont_dev, -1)
        return jnp.concatenate(parts + [last], axis=1).reshape(group_tok, -1)

    plane_experts = device * chips + jnp.arange(chips, dtype=jnp.int32)
    chosen_here = plane_experts[:, None] == jnp.arange(experts, dtype=jnp.int32)[None, :]
    def here(table):
        return jnp.sum(jnp.where(chosen_here[:, None, :], table[None], 0), axis=2)

    slot_ids = jnp.arange(slots, dtype=jnp.int32)

    def pick_rows(step, rows):
        return jnp.einsum(
            "jrt,td->jrd", slot_pick[step], rows, preferred_element_type=single
        ).astype(bfloat)

    def put_rows(step, results):
        return jnp.einsum("jrt,jrd->td", slot_pick[step], results, preferred_element_type=single)

    def add_slots(route_block):
        ranks = rank_table(route_block, experts, capacity)
        match = here(ranks)[:, None, :] == slot_ids[None, :, None]
        slot_pick.append(match.astype(bfloat))
        return ranks

    slot_pick = []
    own_ranks = add_slots(routes[0])
    packed = gather_rows(
        jnp.concatenate(
            [
                latent_down,
                router_weight,
                attn_gain[:, None],
                ffn_gain[:, None],
                jnp.pad(latent_gain, (0, shard_rows - latent_gain.shape[0]))[:, None],
            ],
            axis=1,
        )
    )
    route_ring = [along_ctx(routes[0], s) for s in range(1, ctx_size)]
    grad_ring = [grad_output[0]]
    grad_next = ring_next(grad_ring[0])
    grad_mine = [to_chips(pick_rows(0, grad_ring[0]))]
    grad_theirs = []
    packed, query_shard, route_ring, grad_next, grad_mine[0] = together(
        packed, query_weight, route_ring, grad_next, grad_mine[0]
    )

    for route_block in route_ring:
        add_slots(route_block)
    full_down = packed[:, :down_width]
    full_router = packed[:, down_width : down_width + experts]
    gain_attn = packed[:, down_width + experts].astype(single)
    gain_ffn = packed[:, down_width + experts + 1].astype(single)
    gain_latent = (
        packed[:, down_width + experts + 2]
        .reshape(fsdp_size, shard_rows)[:, : latent_gain.shape[0]]
        .reshape(-1)
        .astype(single)
    )
    inputs_full = layer_input[0].astype(single)
    normed, attn_normal, attn_inverse = rms_forward(inputs_full, gain_attn)
    normed_low = normed.astype(bfloat)
    latent_pre = matmul(normed_low, full_down)
    latent, latent_normal, latent_inverse = rms_forward(latent_pre[:, :KV_RANK], gain_latent)
    latent_low = latent.astype(bfloat)
    key_rope_own = rotate(latent_pre[:, KV_RANK:], cos_table, sin_table).astype(bfloat)
    key_own = jnp.concatenate([latent_low, key_rope_own], axis=1)

    def more_grad_rows():
        step = len(grad_mine)
        grad_ring.append(grad_next)
        following = ring_next(grad_next) if step + 1 < ctx_size else grad_next
        theirs = to_core(grad_mine[-1])
        return following, theirs, to_chips(pick_rows(step, grad_ring[step]))

    full_query = gather_rows(query_shard)
    key_pieces = [key_own] + [along_ctx(key_own, s) for s in range(1, ctx_size)]
    grad_next, theirs, mine = more_grad_rows()
    full_query, up_shard, key_pieces, grad_next, theirs, mine = together(
        full_query, latent_up, key_pieces, grad_next, theirs, mine
    )
    grad_theirs.append(theirs)
    grad_mine.append(mine)

    full_up = gather_rows(up_shard)
    query_pre = matmul(normed_low, full_query)
    grad_next, theirs, mine = more_grad_rows()
    full_up, output_shard, query_pre, grad_next, theirs, mine = together(
        full_up, output_weight, query_pre, grad_next, theirs, mine
    )
    grad_theirs.append(theirs)
    grad_mine.append(mine)

    full_output = gather_rows(output_shard)
    key_group = by_sequence(in_order(key_pieces, device))
    latent_group = key_group[:, :KV_RANK]
    rope_pair = jnp.concatenate([key_group[:, KV_RANK:]] * 2, axis=1)
    kv_group = matmul(latent_group, full_up).astype(bfloat)
    rows_here = (prompt_rows, cont_dev)
    attended_low, log_total = attend(
        rows_here,
        score_scale,
        link,
        query_pre,
        pair_cos,
        pair_sin,
        kv_group,
        rope_pair,
        prompt_mask,
        cont_mask,
    )
    while len(grad_mine) < ctx_size:
        grad_next, theirs, mine = more_grad_rows()
        grad_theirs.append(theirs)
        grad_mine.append(mine)
    grad_group = jnp.concatenate(grad_ring)
    (
        full_output,
        shared_shard,
        down_shard,
        attended_low,
        grad_mine,
        grad_theirs,
        grad_group,
    ) = together(
        full_output,
        part_shared,
        part_down,
        attended_low,
        grad_mine,
        grad_theirs,
        grad_group,
    )
    grad_theirs.append(to_core(grad_mine[-1]))

    part_shared = gather_rows(shared_shard)
    part_down = gather_rows(down_shard)
    hidden = inputs_full + matmul(attended_low, full_output)
    ffn_in, ffn_normal, ffn_inverse = rms_forward(hidden, gain_ffn)
    ffn_low = ffn_in.astype(bfloat)
    logits = matmul(ffn_low, full_router)
    router_exps = jnp.exp(logits - jnp.max(logits, axis=1, keepdims=True))
    router = router_exps / jnp.sum(router_exps, axis=1, keepdims=True)
    route_match = jnp.any(
        routes[0][:, :, None] == jnp.arange(experts, dtype=jnp.int32)[None, None, :], axis=1
    )
    chosen_total = jnp.sum(jnp.where(route_match, router, 0.0), axis=1, keepdims=True)
    gates = jnp.where(route_match, router, 0.0) / chosen_total
    pair_weight = jnp.where(own_ranks >= 0, gates, 0.0)

    weight_high = pair_weight.astype(bfloat)
    weight_low = (pair_weight - weight_high.astype(single)).astype(bfloat)
    ffn_wide = jnp.concatenate(
        [
            ffn_low,
            weight_high,
            weight_low,
            jnp.zeros((tokens, EXTRA - 2 * experts), bfloat),
        ],
        axis=1,
    )
    own_expert = (device * chips + lax.axis_index("fsdp") // 2)[None].astype(jnp.int32)
    kept = []
    out_sends = []

    def flat(rows):
        return rows.reshape(-1, rows.shape[-1])

    def expert_step(step, mine, theirs):
        results, kept[:] = expert_call(
            step,
            ctx_size,
            experts,
            own_expert,
            flat(mine),
            flat(theirs),
            flat(grad_mine[step]),
            flat(grad_theirs[step]),
            expert_gate[0].T,
            expert_up[0].T,
            expert_down[0],
            kept,
        )
        return [rows.reshape(chips, slots, -1) for rows in results]

    def shared_step(step):
        rows = (shared_rows + ffn_ring[len(shared_rows) :])[step][:, :model_width]
        gate_pre = matmul(rows, part_gate)
        up_pre = matmul(rows, part_up)
        act = (jax.nn.silu(gate_pre) * up_pre).astype(bfloat)
        grad_act = jnp.einsum(
            "td,fd->tf",
            shared_grad_rows[step * tokens : (step + 1) * tokens],
            part_down,
            preferred_element_type=single,
        )
        grad_gate, grad_up = silu_grads(grad_act, gate_pre, up_pre)
        back = jnp.einsum("tf,df->td", grad_gate, part_gate, preferred_element_type=single)
        back = back + jnp.einsum("tf,df->td", grad_up, part_up, preferred_element_type=single)
        return rows, act, grad_gate, grad_up, back

    def shared_grads(group):
        act, grad_gate, grad_up = [
            jnp.concatenate([shared[step][i] for step in range(ctx_size)]) for i in range(1, 4)
        ]
        pieces = [
            jnp.einsum("ta,tb->ab", left, right, preferred_element_type=single).astype(bfloat)
            for left, right in ((group, grad_gate), (group, grad_up), (act, shared_grad_rows))
        ]
        return jnp.concatenate(pieces[:2] + [pieces[2].reshape(model_width, hidden_part)], axis=1)

    last = ctx_size - 1
    ffn_ring = [ffn_wide]
    attended_ring = [attended_low]
    shared, mines, theirs, backs, added, returned, out_added, out_steps = ({} for _ in range(8))
    moving = None

    def block_part(step):
        part = put_rows(step, returned[step])
        return part + jnp.pad(shared[step][4], ((0, 0), (0, EXTRA)))

    def hop(step):
        part = block_part(step)
        if moving is not None:
            part = part + moving.astype(single)
        return ring_next(part.astype(bfloat))

    for tick in range(ctx_size + 5):
        sent = {}
        if tick <= last:
            sent["mine"] = to_chips(pick_rows(tick, ffn_ring[tick]))
        if tick < last:
            sent["ring"] = ring_next(ffn_ring[tick])
        if 0 <= tick - 1 <= last:
            sent["theirs"] = to_core(mines[tick - 1])
        if 0 <= tick - 2 <= last:
            sent["back"] = expert_step(tick - 2, mines[tick - 2], theirs[tick - 2])
        if 0 <= tick - 3 <= last:
            sent["added"] = add_halves(*backs[tick - 3])
        if 0 <= tick - 4 <= last:
            sent["returned"] = to_chips(added[tick - 4])
        if 1 <= tick - 4 <= last:
            shared[tick - 4] = shared_step(tick - 4)
            sent["shared"] = shared[tick - 4]
        if 1 <= tick - 5 <= last:
            sent["moving"] = hop(tick - 5)
        if tick == 0:
            sent["grads"] = grad_theirs[-1]
        if tick == 1:
            sent["weights"] = (part_shared, part_down)
        if tick == 4:
            sent["shared_in"] = (ffn_ring, grad_group, part_gate, part_up, part_down)
        if tick == ctx_size + 3:
            sent["shared_all"] = shared
            sent["group"] = jnp.concatenate(
                [block[:, :model_width] for block in shared_rows + ffn_ring[len(shared_rows) :]]
            )
            sent["out"] = add_halves(*out_sends[1])
        if tick == ctx_size + 4:
            sent["shared_grads"] = shared_grads(ffn_group)
            sent["out_step"] = to_chips(out_added[1])
        if last <= tick < 2 * last:
            sent["attended"] = ring_next(attended_ring[-1])
        if tick == ctx_size + 2:
            shared[0] = shared_step(0)
            sent["first"] = shared[0]
        if tick == ctx_size + 4:
            sent["out"] = add_halves(*out_sends[2])
        names = sorted(sent)
        sent = dict(zip(names, together(*(sent[name] for name in names))))
        if "mine" in sent:
            mines[tick] = sent["mine"]
        if "ring" in sent:
            ffn_ring.append(sent["ring"])
        if "theirs" in sent:
            theirs[tick - 1] = sent["theirs"]
        if "back" in sent:
            backs[tick - 2] = sent["back"][:2]
            out_sends.append(sent["back"][2:])
        if "added" in sent:
            added[tick - 3] = sent["added"]
        if "returned" in sent:
            returned[tick - 4] = sent["returned"]
        if "shared_in" in sent:
            shared_rows, shared_grad_rows, part_gate, part_up, part_down = sent["shared_in"]
        if "shared" in sent:
            shared[tick - 4] = sent["shared"]
        if "first" in sent:
            shared[0] = sent["first"]
        if "shared_all" in sent:
            shared = sent["shared_all"]
        if "attended" in sent:
            attended_ring.append(sent["attended"])
        if "out" in sent:
            out_added[tick - ctx_size - 2] = sent["out"]
        if "group" in sent:
            ffn_group = sent["group"]
        if "out_step" in sent:
            out_steps[1] = sent["out_step"]
        moving = sent.get("moving", moving)
        if tick == 0:
            grad_theirs[-1] = sent["grads"]
        if tick == 1:
            part_gate = sent["weights"][0][:, :hidden_part]
            part_up = sent["weights"][0][:, hidden_part:]
            part_down = sent["weights"][1]

    while len(attended_ring) < ctx_size:
        attended_ring.append(ring_next(attended_ring[-1]))
    shared_part = scatter_rows(sent["shared_grads"])
    first_part = block_part(0)

    def next_out(step):
        ahead = (step + 1) % ctx_size
        return to_chips(out_added[step]), add_halves(*out_sends[ahead]) if step else out_added[step]

    grad_wide = moving.astype(single) + first_part
    grad_ffn = grad_wide[:, :model_width]
    grad_gate_pair = jnp.where(
        own_ranks >= 0, grad_wide[:, model_width : model_width + experts], 0.0
    )

    grad_low = grad_output[0]
    grad_top = grad_low.astype(single)
    grad_chosen = (
        grad_gate_pair - jnp.sum(grad_gate_pair * gates, axis=1, keepdims=True)
    ) / chosen_total
    grad_router = jnp.where(route_match, grad_chosen, 0.0)
    grad_logits = (
        router * (grad_router - jnp.sum(router * grad_router, axis=1, keepdims=True))
    ).astype(bfloat)
    grad_w_router = jnp.einsum("td,te->de", ffn_low, grad_logits, preferred_element_type=single)
    grad_ffn = grad_ffn + jnp.einsum(
        "te,de->td", grad_logits, full_router, preferred_element_type=single
    )
    grad_hidden_norm, grad_gain_ffn = rms_backward(grad_ffn, ffn_normal, ffn_inverse, gain_ffn)
    grad_hidden = grad_top + grad_hidden_norm
    grad_attn_low = grad_hidden.astype(bfloat)

    def out_hop(step, moving):
        part = put_rows(step, out_steps[step]) + matmul(shared[step][1], part_down)
        if moving is not None:
            part = part + moving.astype(single)
        return ring_next(part.astype(bfloat))

    grad_attended = jnp.einsum(
        "td,vd->tv", grad_attn_low, full_output, preferred_element_type=single
    ).astype(bfloat)
    out_next = next_out(2)
    out_moving = out_hop(1, None)
    att_shares = column_shares(grad_attn_low, device)
    grad_attended, out_next, out_moving = together(grad_attended, out_next, out_moving)
    out_steps[2], out_added[3] = out_next

    def weight_grad(left, right):
        return jnp.einsum("ra,rb->ab", left, right, preferred_element_type=single)

    grad_w_output = weight_grad(jnp.concatenate(attended_ring), jnp.concatenate(att_shares))

    out_next = next_out(3)
    out_moving = out_hop(2, out_moving)

    log_rows = log_total[:, :HEADS].T.reshape(HEADS // 2, 2, tokens)
    grad_nope, grad_rope, grad_key_part, grad_value_part, rope_pair_grad = attend_back(
        rows_here,
        score_scale,
        link,
        query_pre,
        pair_cos,
        pair_sin,
        kv_group,
        rope_pair,
        prompt_mask.T,
        cont_mask.T,
        log_rows,
        grad_attended,
    )
    (
        grad_nope,
        grad_rope,
        grad_key_part,
        grad_value_part,
        rope_pair_grad,
        out_next,
        out_moving,
        shared_part,
        grad_w_output,
    ) = together(
        grad_nope,
        grad_rope,
        grad_key_part,
        grad_value_part,
        rope_pair_grad,
        out_next,
        out_moving,
        shared_part,
        grad_w_output,
    )
    out_steps[3], out_added[4 % ctx_size] = out_next
    out_next = next_out(0) if ctx_size == 4 else next_out(4)
    out_moving = out_hop(3, out_moving)
    output_part = scatter_rows(grad_w_output)
    grad_key_rope = rope_pair_grad[:, :ROPE] + rope_pair_grad[:, ROPE:]
    keys_width = HEADS * NOPE
    grad_latent_group = jnp.einsum(
        "tk,ck->tc", grad_key_part, full_up[:, :keys_width], preferred_element_type=single
    ) + jnp.einsum(
        "tk,ck->tc", grad_value_part, full_up[:, keys_width:], preferred_element_type=single
    )
    grad_query_pre = jnp.concatenate([grad_nope, grad_rope], axis=1)
    grad_w_query = weight_grad(normed_low, grad_query_pre)
    grad_keys_own = ctx_total(
        by_block(jnp.concatenate([grad_latent_group, grad_key_rope], axis=1).astype(bfloat)), device
    )
    grad_keys_own, output_part, grad_w_query, out_next, out_moving = together(
        grad_keys_own, output_part, grad_w_query, out_next, out_moving
    )
    if ctx_size == 4:
        out_steps[0] = out_next[0]
    else:
        out_steps[4], out_added[5] = out_next
        for step in range(4, ctx_size):
            if step > 4:
                out_steps[step], out_added[(step + 1) % ctx_size] = next_out(step)
            out_moving = out_hop(step, out_moving)
        out_steps[0] = to_chips(out_added[0])
    query_part = scatter_rows(grad_w_query)
    shared_ring = [shared_part, ring_next(shared_part)]
    sum_output = all_columns_of(output_part, device)
    grad_w_up = jnp.concatenate(
        [
            weight_grad(latent_group, part).astype(bfloat).reshape(model_width, -1)
            for part in (grad_key_part, grad_value_part)
        ],
        axis=1,
    )
    grad_latent = grad_keys_own[:, :KV_RANK]
    grad_rope_own = grad_keys_own[:, KV_RANK:]
    grad_latent_in, grad_gain_latent = rms_backward(
        grad_latent, latent_normal, latent_inverse, gain_latent
    )
    grad_rope_in = rotate(grad_rope_own, cos_table, -sin_table)
    grad_latent_pre = jnp.concatenate([grad_latent_in, grad_rope_in], axis=1).astype(bfloat)
    grad_w_down = jnp.einsum(
        "td,tk->dk",
        normed_low,
        jnp.pad(grad_latent_pre, ((0, 0), (0, -down_width % 128))),
        preferred_element_type=single,
    )
    grad_normed = jnp.einsum(
        "tq,dq->td", grad_query_pre, full_query, preferred_element_type=single
    ) + jnp.einsum("tk,dk->td", grad_latent_pre, full_down, preferred_element_type=single)
    grad_x_norm, grad_gain_attn = rms_backward(grad_normed, attn_normal, attn_inverse, gain_attn)
    grad_input = (grad_hidden + grad_x_norm).astype(bfloat)

    padded_latent = jnp.pad(
        grad_gain_latent.reshape(fsdp_size, -1),
        ((0, 0), (0, shard_rows - latent_gain.shape[0])),
    ).reshape(-1)
    up_width = grad_w_up.shape[1]
    small = jnp.concatenate(
        [
            grad_w_router,
            grad_gain_attn[:, None],
            grad_gain_ffn[:, None],
            padded_latent[:, None],
        ],
        axis=1,
    ).astype(bfloat)
    packed_grads = jnp.concatenate(
        [
            grad_w_up,
            grad_w_down.astype(bfloat),
            jnp.pad(small, ((0, 0), (0, -small.shape[1] % 128))),
        ],
        axis=1,
    )
    packed_grads, shared_ring, kept = together(packed_grads, shared_ring, kept)
    all_rows, all_grads, all_act, all_gate, all_up = kept
    grad_piece_down = weight_grad(all_act, all_grads)
    while len(shared_ring) < ctx_size:
        shared_ring.append(ring_next(shared_ring[-1]))
    query_part, packed_grads, shared_ring, sum_output, grad_piece_down, kept = together(
        query_part, packed_grads, shared_ring, sum_output, grad_piece_down, kept
    )
    packed_part = scatter_rows(with_layout_constraint(packed_grads, by_rows))
    all_rows, all_grads, all_act, all_gate, all_up = kept
    grad_piece_gate = weight_grad(all_rows, all_gate)
    query_total = ctx_total(query_part, device).astype(bfloat)
    query_total, grad_piece_gate, kept = together(query_total, grad_piece_gate, kept)
    all_rows, all_grads, all_act, all_gate, all_up = kept
    grad_piece_up = weight_grad(all_rows, all_up)
    sum_query = ctx_spread(query_total, device)
    first_out = put_rows(0, out_steps[0]) + matmul(shared[0][1], part_down)
    layer_output = (hidden + out_moving.astype(single) + first_out).astype(bfloat)
    packed_part, sum_query, grad_piece_up = together(packed_part, sum_query, grad_piece_up)
    sum_packed = with_layout_constraint(
        sum_ctx(with_layout_constraint(packed_part, by_rows)), by_rows
    )
    sum_up = jnp.concatenate(
        [
            part.reshape(latent_up.shape[0], -1)
            for part in (sum_packed[:, : up_width // 2], sum_packed[:, up_width // 2 : up_width])
        ],
        axis=1,
    )
    sum_down = sum_packed[:, up_width : up_width + down_width]
    sum_small = sum_packed[:, up_width + grad_w_down.shape[1] :]
    sum_router = sum_small[:, :experts]
    sum_gain_attn = sum_small[:, experts]
    sum_gain_ffn = sum_small[:, experts + 1]
    sum_gain_latent = sum_small[: latent_gain.shape[0], experts + 2]

    shared_blocks = in_order([piece[None] for piece in shared_ring], device)

    def all_columns(blocks):
        blocks = blocks.reshape(ctx_size, shard_rows, fsdp_size, hidden_dev)
        return blocks.transpose(1, 2, 0, 3).reshape(shard_rows, -1).astype(single)

    sum_sh_gate = all_columns(shared_blocks[:, :, :hidden_part])
    sum_sh_up = all_columns(shared_blocks[:, :, hidden_part : 2 * hidden_part])
    sum_sh_down = shared_blocks[:, :, 2 * hidden_part :].reshape(shared_down.shape).astype(single)
    return (
        layer_output[None],
        grad_input[None],
        sum_query,
        sum_down,
        sum_up,
        sum_output,
        sum_router,
        sum_sh_gate,
        sum_sh_up,
        sum_sh_down,
        sum_gain_attn,
        sum_gain_latent,
        sum_gain_ffn,
        grad_piece_gate[None],
        grad_piece_up[None],
        grad_piece_down[None],
    )


def solution(mesh):
    in_specs = (
        P("fsdp", "ctx", None),
        P("fsdp", "ctx", None),
        P("fsdp", "ctx", None),
        P("fsdp", None),
        P(),
        P("fsdp", None),
        P("fsdp", None),
        P("fsdp", None),
        P("fsdp", None),
        P("fsdp", None),
        P("fsdp", None),
        P("fsdp", None),
        P("fsdp", None),
        P("fsdp"),
        P("fsdp"),
        P("fsdp"),
        P(("ctx", "fsdp"), None, None),
        P(("ctx", "fsdp"), None, None),
        P(("ctx", "fsdp"), None, None),
    )
    out_specs = (
        P("fsdp", "ctx", None),
        P("fsdp", "ctx", None),
        P("fsdp", None),
        P("fsdp", None),
        P("fsdp", None),
        P("fsdp", None),
        P("fsdp", None),
        P("fsdp", None),
        P("fsdp", None),
        P("fsdp", None),
        P("fsdp"),
        P("fsdp"),
        P("fsdp"),
        P(("ctx", "fsdp"), None, None),
        P(("ctx", "fsdp"), None, None),
        P(("ctx", "fsdp"), None, None),
    )
    return jax.shard_map(local, mesh=mesh, in_specs=in_specs, out_specs=out_specs, check_vma=False)
```

```python
import functools

import jax
import jax.numpy as jnp
from jax import lax
from jax.experimental import pallas as pl
from jax.experimental.layout import Layout, with_layout_constraint
from jax.experimental.pallas import tpu as pltpu
from jax.sharding import PartitionSpec as P

HEADS = 16
NOPE = 128
ROPE = 64
VDIM = 128
KV_RANK = 512
TOP = 6
PROMPT = 512
PROMPTS = 2
CONT_LEN = 128
CONTS = 2


epsilon = 1e-06
masked_score = -1e30
bfloat = jnp.bfloat16
single = jnp.float32


EXTRA = 128
by_rows = Layout(major_to_minor=(0, 1))


def matmul(left, right):
    return jnp.dot(left, right, preferred_element_type=single)


def rms_forward(values, gain):
    inverse = lax.rsqrt(jnp.mean(values * values, axis=-1, keepdims=True) + epsilon)
    normal_part = values * inverse
    return (normal_part * gain, normal_part, inverse)


def rms_backward(grad_out, normal_part, inverse, gain):
    grad_normal = grad_out * gain
    grad_gain = jnp.sum(grad_out * normal_part, axis=0)
    grad_in = inverse * (
        grad_normal - normal_part * jnp.mean(grad_normal * normal_part, axis=-1, keepdims=True)
    )
    return (grad_in, grad_gain)


def rotary_tables(positions):
    exponent = jnp.arange(ROPE // 2, dtype=jnp.float32) * (2.0 / ROPE)
    frequency = jnp.exp(-jnp.log(10000.0) * exponent)
    angles = positions[:, None] * frequency[None, :]
    return (jnp.cos(angles), jnp.sin(angles))


def rotate(values, cos_table, sin_table):
    half_width = values.shape[-1] // 2
    first_half = values[..., :half_width]
    second = values[..., half_width:]
    return jnp.concatenate(
        [first_half * cos_table - second * sin_table, second * cos_table + first_half * sin_table],
        axis=-1,
    )


def lookup(table_values, wanted):
    matches = wanted[:, None] == jnp.arange(table_values.shape[0], dtype=jnp.int32)[None, :]
    return jnp.sum(jnp.where(matches, table_values[None, :], 0), axis=1)


def row_layout(device, local_row, block_order, link_table, block_len, cont_dev):
    prompt_rows = PROMPTS * 2 * block_len
    in_prompt = local_row < prompt_rows
    prompt_id = local_row // (2 * block_len)
    half_slot = local_row // block_len % 2
    prompt_pos = lookup(block_order, 2 * device + half_slot) * block_len + local_row % block_len
    cont_index = device * cont_dev + jnp.maximum(local_row - prompt_rows, 0)
    cont_id = jnp.minimum(cont_index // CONT_LEN, CONTS - 1)
    cont_pos = cont_index % CONT_LEN
    sequence = jnp.where(in_prompt, prompt_id, PROMPTS + cont_id)
    position = jnp.where(in_prompt, prompt_pos, cont_pos)
    linked = jnp.where(in_prompt, -1, lookup(link_table, cont_id))
    rotary = jnp.where(in_prompt, prompt_pos, PROMPT + cont_pos)
    return (sequence, position, linked, rotary)


def silu_grads(grad_act, gate_pre, up_pre):
    sigmoid_gate = jax.nn.sigmoid(gate_pre)
    grad_gate = (grad_act * up_pre * sigmoid_gate * (1.0 + gate_pre * (1.0 - sigmoid_gate))).astype(
        bfloat
    )
    grad_up = (grad_act * gate_pre * sigmoid_gate).astype(bfloat)
    return (grad_gate, grad_up)


NT = (((1,), (1,)), ((), ()))
TN = (((0,), (0,)), ((), ()))


def product(left, right, dims):
    return lax.dot_general(left, right, dims, preferred_element_type=single)


def half_swap(values):
    width = values.shape[1]
    lane = lax.broadcasted_iota(jnp.int32, values.shape, 1)
    ahead = pltpu.roll(values, width - ROPE // 2, 1)
    behind = pltpu.roll(values, ROPE // 2, 1)
    return jnp.where(lane % ROPE < ROPE // 2, ahead, behind)


def head_query(nope, rotated, which):
    lane = lax.broadcasted_iota(jnp.int32, rotated.shape, 1)
    kept = jnp.where((lane >= ROPE) == (which == 1), rotated, 0.0)
    return jnp.concatenate(
        [nope[:, which * NOPE : (which + 1) * NOPE].astype(bfloat), kept.astype(bfloat)], axis=1
    )


def attend_kernel(
    rows, scale, link, nope, rope, cos, sin, keys, values, key_rope, prompt_mask, cont_mask, out, lse
):
    pair = pl.program_id(0)
    prompt_rows, cont_rows = rows
    first = prompt_rows * PROMPTS
    linked = pl.multiple_of(link[0] * PROMPT, PROMPT)
    rotated = rope[...] * cos[...] + half_swap(rope[...]) * sin[...]
    nopes = nope[...]

    @pl.when(pair == 0)
    def _():
        lse[...] = jnp.zeros_like(lse)

    def key_part(start, count, which):
        return jnp.concatenate(
            [keys[pl.ds(start, count), which * NOPE : (which + 1) * NOPE], key_rope[pl.ds(start, count), :]],
            axis=1,
        )

    def value_part(start, count, which):
        return values[pl.ds(start, count), which * VDIM : (which + 1) * VDIM]

    for which in range(2):
        query = head_query(nopes, rotated, which)
        outs = []
        logs = []
        for prompt in range(PROMPTS):
            part = query[prompt * prompt_rows : (prompt + 1) * prompt_rows]
            scores = product(part, key_part(prompt * PROMPT, PROMPT, which), NT) * scale
            scores = scores + prompt_mask[...]
            top = jnp.max(scores, axis=1, keepdims=True)
            exps = jnp.exp(scores - top)
            total = jnp.sum(exps, axis=1, keepdims=True)
            probs = (exps / total).astype(bfloat)
            outs.append(matmul(probs, value_part(prompt * PROMPT, PROMPT, which)))
            logs.append(top + jnp.log(total))
        part = query[first:]
        cont_keys = CONTS * CONT_LEN
        scores = product(part, key_part(linked, PROMPT, which), NT) * scale
        near = product(part, key_part(PROMPTS * PROMPT, cont_keys, which), NT) * scale
        near = near + cont_mask[...]
        top = jnp.maximum(
            jnp.max(scores, axis=1, keepdims=True), jnp.max(near, axis=1, keepdims=True)
        )
        exps = jnp.exp(scores - top)
        near_exps = jnp.exp(near - top)
        total = jnp.sum(exps, axis=1, keepdims=True) + jnp.sum(near_exps, axis=1, keepdims=True)
        outs.append(
            matmul((exps / total).astype(bfloat), value_part(linked, PROMPT, which))
            + matmul(
                (near_exps / total).astype(bfloat), value_part(PROMPTS * PROMPT, cont_keys, which)
            )
        )
        logs.append(top + jnp.log(total))
        out[:, which * VDIM : (which + 1) * VDIM] = jnp.concatenate(outs, axis=0).astype(bfloat)
        lane = lax.broadcasted_iota(jnp.int32, lse.shape, 1)
        lse[...] = jnp.where(lane == 2 * pair + which, jnp.concatenate(logs, axis=0), lse[...])


def attend_back_kernel(
    rows,
    scale,
    link,
    nope,
    rope,
    cos,
    sin,
    keys,
    values,
    key_rope,
    prompt_mask,
    cont_mask,
    lse,
    grad,
    grad_nope,
    grad_rope,
    grad_keys,
    grad_values,
    grad_key_rope,
    key_sum,
    value_sum,
    rope_sum,
):
    pair = pl.program_id(0)
    prompt_rows, cont_rows = rows
    first = prompt_rows * PROMPTS
    linked = pl.multiple_of(link[0] * PROMPT, PROMPT)
    cont_start = PROMPTS * PROMPT
    cont_keys = CONTS * CONT_LEN
    rotated = rope[...] * cos[...] + half_swap(rope[...]) * sin[...]
    nopes = nope[...]

    @pl.when(pair == 0)
    def _():
        rope_sum[...] = jnp.zeros_like(rope_sum)

    rope_grads = []
    for which in range(2):
        query = head_query(nopes, rotated, which)
        log_row = lse[which : which + 1, :]
        query_grads = []

        def one(lo, hi, start, count, mask):
            part = query[lo:hi]
            key_cat = jnp.concatenate(
                [
                    keys[pl.ds(start, count), which * NOPE : (which + 1) * NOPE],
                    key_rope[pl.ds(start, count), :],
                ],
                axis=1,
            )
            value = values[pl.ds(start, count), which * VDIM : (which + 1) * VDIM]
            grad_part = grad[lo:hi, which * VDIM : (which + 1) * VDIM]
            scores = product(key_cat, part, NT) * scale
            if mask is not None:
                scores = scores + mask
            probs = jnp.exp(scores - log_row[:, lo:hi])
            grad_probs = product(value, grad_part, NT)
            return part, key_cat, grad_part, probs, grad_probs

        def finish(parts, delta):
            part, key_cat, grad_part, probs, grad_probs = parts
            grad_scores = (probs * (grad_probs - delta)).astype(bfloat)
            query_grad = product(grad_scores, key_cat, TN)
            key_grad = matmul(grad_scores, part) * scale
            value_grad = matmul(probs.astype(bfloat), grad_part)
            return query_grad, key_grad, value_grad

        def delta_of(parts):
            return jnp.sum(parts[3] * parts[4], axis=0, keepdims=True)

        for prompt in range(PROMPTS):
            lo, hi = prompt * prompt_rows, (prompt + 1) * prompt_rows
            start = prompt * PROMPT
            parts = one(lo, hi, start, PROMPT, prompt_mask[...])
            query_grad, key_grad, value_grad = finish(parts, delta_of(parts))
            query_grads.append(query_grad)
            key_sum[start : start + PROMPT, :] = key_grad[:, :NOPE]
            value_sum[start : start + PROMPT, :] = value_grad
            rope_sum[start : start + PROMPT, :] += key_grad[:, NOPE:]
        far = one(first, first + cont_rows, linked, PROMPT, None)
        near = one(first, first + cont_rows, cont_start, cont_keys, cont_mask[...])
        delta = delta_of(far) + delta_of(near)
        far_query, far_key, far_value = finish(far, delta)
        near_query, near_key, near_value = finish(near, delta)
        query_grads.append(far_query + near_query)
        span = pl.ds(linked, PROMPT)
        key_sum[span, :] += far_key[:, :NOPE]
        value_sum[span, :] += far_value
        rope_sum[span, :] += far_key[:, NOPE:]
        key_sum[cont_start:, :] = near_key[:, :NOPE]
        value_sum[cont_start:, :] = near_value
        rope_sum[cont_start:, :] += near_key[:, NOPE:]
        query_grad = jnp.concatenate(query_grads, axis=0) * scale
        grad_nope[:, which * NOPE : (which + 1) * NOPE] = query_grad[:, :NOPE].astype(bfloat)
        rope_grads.append(query_grad[:, NOPE:])
        grad_keys[:, which * NOPE : (which + 1) * NOPE] = key_sum[...].astype(bfloat)
        grad_values[:, which * VDIM : (which + 1) * VDIM] = value_sum[...].astype(bfloat)
    lane = lax.broadcasted_iota(jnp.int32, rope_grads[0].shape, 1)
    both = jnp.where(lane < ROPE, rope_grads[0], rope_grads[1])
    grad_rope[...] = (both * cos[...] - half_swap(both) * sin[...]).astype(bfloat)
    grad_key_rope[...] = rope_sum[...]


def whole(shape):
    return pl.BlockSpec(shape, lambda pair: (0,) * len(shape))


def pair_specs(tokens, key_rows, prompt_mask, cont_mask):
    nope_blocks = HEADS * NOPE // (2 * ROPE)
    return [
        pl.BlockSpec(memory_space=pltpu.SMEM),
        pl.BlockSpec((tokens, 2 * NOPE), lambda pair: (0, pair)),
        pl.BlockSpec((tokens, 2 * ROPE), lambda pair: (0, nope_blocks + pair)),
        whole((tokens, 2 * ROPE)),
        whole((tokens, 2 * ROPE)),
        pl.BlockSpec((key_rows, 2 * NOPE), lambda pair: (0, pair)),
        pl.BlockSpec((key_rows, 2 * VDIM), lambda pair: (0, HEADS // 2 + pair)),
        whole((key_rows, 2 * ROPE)),
        whole(prompt_mask),
        whole(cont_mask),
    ]


def attend(rows, scale, link, query_pre, cos, sin, kv, key_rope, prompt_mask, cont_mask):
    tokens = query_pre.shape[0]
    key_rows = kv.shape[0]
    work = 2 * (rows[0] * PROMPT * PROMPTS + rows[1] * (PROMPT + CONTS * CONT_LEN)) * HEADS
    return pl.pallas_call(
        functools.partial(attend_kernel, rows, scale),
        grid=(HEADS // 2,),
        in_specs=pair_specs(tokens, key_rows, prompt_mask.shape, cont_mask.shape),
        out_specs=[
            pl.BlockSpec((tokens, 2 * VDIM), lambda pair: (0, pair)),
            whole((tokens, 128)),
        ],
        out_shape=[
            jax.ShapeDtypeStruct((tokens, HEADS * VDIM), bfloat),
            jax.ShapeDtypeStruct((tokens, 128), single),
        ],
        compiler_params=pltpu.CompilerParams(vmem_limit_bytes=40 * 2**20),
        cost_estimate=pl.CostEstimate(
            flops=work * 384, bytes_accessed=2 * kv.size + 6 * query_pre.size, transcendentals=work // 2
        ),
    )(link, query_pre, query_pre, cos, sin, kv, kv, key_rope, prompt_mask, cont_mask)


def attend_back(
    rows, scale, link, query_pre, cos, sin, kv, key_rope, prompt_mask, cont_mask, lse, grad
):
    tokens = query_pre.shape[0]
    key_rows = kv.shape[0]
    work = 2 * (rows[0] * PROMPT * PROMPTS + rows[1] * (PROMPT + CONTS * CONT_LEN)) * HEADS
    return pl.pallas_call(
        functools.partial(attend_back_kernel, rows, scale),
        grid=(HEADS // 2,),
        in_specs=pair_specs(tokens, key_rows, prompt_mask.shape, cont_mask.shape)
        + [
            pl.BlockSpec((None, 2, tokens), lambda pair: (pair, 0, 0)),
            pl.BlockSpec((tokens, 2 * VDIM), lambda pair: (0, pair)),
        ],
        out_specs=[
            pl.BlockSpec((tokens, 2 * NOPE), lambda pair: (0, pair)),
            pl.BlockSpec((tokens, 2 * ROPE), lambda pair: (0, pair)),
            pl.BlockSpec((key_rows, 2 * NOPE), lambda pair: (0, pair)),
            pl.BlockSpec((key_rows, 2 * VDIM), lambda pair: (0, pair)),
            whole((key_rows, 2 * ROPE)),
        ],
        out_shape=[
            jax.ShapeDtypeStruct((tokens, HEADS * NOPE), bfloat),
            jax.ShapeDtypeStruct((tokens, HEADS * ROPE), bfloat),
            jax.ShapeDtypeStruct((key_rows, HEADS * NOPE), bfloat),
            jax.ShapeDtypeStruct((key_rows, HEADS * VDIM), bfloat),
            jax.ShapeDtypeStruct((key_rows, 2 * ROPE), single),
        ],
        scratch_shapes=[
            pltpu.VMEM((key_rows, NOPE), single),
            pltpu.VMEM((key_rows, VDIM), single),
            pltpu.VMEM((key_rows, 2 * ROPE), single),
        ],
        compiler_params=pltpu.CompilerParams(vmem_limit_bytes=48 * 2**20),
        cost_estimate=pl.CostEstimate(
            flops=work * 1152, bytes_accessed=4 * kv.size + 10 * query_pre.size, transcendentals=work // 2
        ),
    )(link, query_pre, query_pre, cos, sin, kv, kv, key_rope, prompt_mask, cont_mask, lse, grad)


def expert_kernel(
    first_row,
    experts,
    expert,
    mine,
    theirs,
    grad_mine,
    grad_theirs,
    gate,
    up,
    down,
    *refs,
):
    back_mine, back_theirs, out_mine, out_theirs = refs[-21:-17]
    all_rows, all_grads, all_act, all_gate, all_up = refs[-17:-12]
    rows, grads, gate_w, up_w, down_w, act, grad_gate, grad_up, back, out = refs[-12:-2]
    in_sems, out_sems = refs[-2:]
    count = mine.shape[0]
    hidden, width = gate.shape
    lane = lax.broadcasted_iota(jnp.int32, (count, EXTRA), 1)
    here = lane == expert[0]
    loads = [
        pltpu.make_async_copy(source, target, in_sems.at[i])
        for i, (source, target) in enumerate(
            [
                (theirs, rows.at[1]),
                (gate, gate_w),
                (up, up_w),
                (grad_theirs, grads.at[1]),
                (down, down_w),
                (mine, rows.at[0]),
                (grad_mine, grads.at[0]),
            ]
        )
    ]
    for load in loads:
        load.start()

    def store(half, which):
        span = pl.ds(first_row + half * count, count)
        pairs = [
            (rows.at[half, :, pl.ds(0, width)], all_rows.at[span, :]),
            (grads.at[half], all_grads.at[span, :]),
            (act.at[half], all_act.at[span, :]),
            (grad_gate.at[half], all_gate.at[span, :]),
            (grad_up.at[half], all_up.at[span, :]),
            (back.at[half], (back_mine, back_theirs)[half]),
            (out.at[half], (out_mine, out_theirs)[half]),
        ]
        source, target = pairs[which]
        return pltpu.make_async_copy(source, target, out_sems.at[half, which])

    def one_half(turn, carry):
        half = 1 - turn

        def await_loads(first, second):
            for when, which in enumerate((first, second)):
                if which:

                    @pl.when(turn == when)
                    def _(which=which):
                        for i in which:
                            loads[i].wait()

        def start_stores(which):
            for when in range(2):

                @pl.when(turn == when)
                def _(when=when):
                    for i in which:
                        store(1 - when, i).start()

        await_loads((0, 1), (5,))
        start_stores((0,))
        extra = rows[half, :, width:].astype(single)
        slot_weight = jnp.sum(
            jnp.where(here | (lane == expert[0] + experts), extra, 0.0), axis=1, keepdims=True
        )
        total = jnp.zeros((count, 1), single)
        for lo in range(0, hidden, 256):
            hi = min(lo + 256, hidden)
            gate_pre = product(rows[half, :, :width], gate_w[lo:hi, :], NT)
            if lo == 0:
                await_loads((2,), ())
            up_pre = product(rows[half, :, :width], up_w[lo:hi, :], NT)
            if lo == 0:
                await_loads((3, 4), (6,))
                start_stores((1,))
            grad_act = product(grads[half], down_w[lo:hi, :], NT)
            sigmoid = 1.0 / (1.0 + jnp.exp(-gate_pre))
            silu = gate_pre * sigmoid
            value = silu * up_pre
            total = total + jnp.sum(
                value.astype(bfloat).astype(single) * grad_act, axis=1, keepdims=True
            )
            grad_act = grad_act * slot_weight
            act[half, :, lo:hi] = (value * slot_weight).astype(bfloat)
            grad_gate[half, :, lo:hi] = (
                grad_act * up_pre * sigmoid * (1.0 + gate_pre * (1.0 - sigmoid))
            ).astype(bfloat)
            grad_up[half, :, lo:hi] = (grad_act * silu).astype(bfloat)
        start_stores((2, 3, 4))
        back[half, :, width:] = jnp.where(here, total, 0.0).astype(bfloat)
        step = min(512, width)
        for lo in range(0, width, step):
            hi = lo + step
            part = matmul(grad_gate[half], gate_w[:, lo:hi])
            part = part + matmul(grad_up[half], up_w[:, lo:hi])
            back[half, :, lo:hi] = part.astype(bfloat)
        start_stores((5,))
        for lo in range(0, width, step):
            hi = lo + step
            out[half, :, lo:hi] = matmul(act[half], down_w[:, lo:hi]).astype(bfloat)
        start_stores((6,))
        return carry

    lax.fori_loop(0, 2, one_half, 0)
    for half in range(2):
        for which in range(7):
            store(half, which).wait()


def expert_call(
    step, steps, experts, expert, mine, theirs, grad_mine, grad_theirs, gate, up, down, kept
):
    count, wide = mine.shape
    hidden, width = gate.shape
    anywhere = pl.BlockSpec(memory_space=pl.ANY)
    back_shape = jax.ShapeDtypeStruct((count, wide), bfloat)
    out_shape = jax.ShapeDtypeStruct((count, width), bfloat)
    kept_shapes = [
        jax.ShapeDtypeStruct((steps * 2 * count, columns), bfloat)
        for columns in (width, width, hidden, hidden, hidden)
    ]
    outs = pl.pallas_call(
        functools.partial(expert_kernel, step * 2 * count, experts),
        in_specs=[pl.BlockSpec(memory_space=pltpu.SMEM)] + [anywhere] * (7 + len(kept)),
        out_specs=[anywhere] * 9,
        out_shape=[back_shape] * 2 + [out_shape] * 2 + kept_shapes,
        input_output_aliases={8 + i: 4 + i for i in range(len(kept))},
        scratch_shapes=[
            pltpu.VMEM((2, count, wide), bfloat),
            pltpu.VMEM((2, count, width), bfloat),
        ]
        + [pltpu.VMEM((hidden, width), bfloat)] * 3
        + [pltpu.VMEM((2, count, hidden), bfloat)] * 3
        + [pltpu.VMEM((2, count, wide), bfloat), pltpu.VMEM((2, count, width), bfloat)]
        + [pltpu.SemaphoreType.DMA((7,)), pltpu.SemaphoreType.DMA((2, 7))],
        compiler_params=pltpu.CompilerParams(vmem_limit_bytes=56 * 2**20),
        cost_estimate=pl.CostEstimate(
            flops=2 * 6 * 2 * count * width * hidden,
            bytes_accessed=2 * (12 * count * width + 3 * hidden * width + 6 * count * hidden),
            transcendentals=2 * count * hidden,
        ),
    )(expert, mine, theirs, grad_mine, grad_theirs, gate, up, down, *kept)
    return outs[:4], list(outs[4:])


def ring_next(value):
    size = lax.axis_size("ctx")
    return lax.ppermute(value, "ctx", [(i, (i + 1) % size) for i in range(size)])


def to_chips(value):
    size = lax.axis_size("fsdp")
    return lax.all_to_all(
        value,
        "fsdp",
        split_axis=0,
        concat_axis=0,
        tiled=True,
        axis_index_groups=[list(range(core, size, 2)) for core in range(2)],
    )


def to_core(value):
    size = lax.axis_size("fsdp")
    return lax.ppermute(value, "fsdp", [(i, i ^ 1) for i in range(size)])


def gather_rows(value):
    return lax.all_gather(value, "fsdp", axis=0, tiled=True)


def scatter_rows(value):
    return lax.psum_scatter(value.astype(bfloat), "fsdp", scatter_dimension=0, tiled=True)


def along_ctx(value, shift):
    size = lax.axis_size("ctx")
    return lax.ppermute(value, "ctx", [(i, (i + shift) % size) for i in range(size)])


def column_shares(value, device):
    size = lax.axis_size("ctx")
    count = value.shape[1] // size

    def share(owner):
        return lax.dynamic_slice_in_dim(value, owner % size * count, count, axis=1)

    return [share(device)] + [along_ctx(share(device + k), k) for k in range(1, size)]


def all_columns_of(part, device):
    pieces = [part] + [along_ctx(part, shift) for shift in range(1, lax.axis_size("ctx"))]
    return in_order([piece.astype(single) for piece in pieces], device, 1)


def ctx_spread(part, device):
    pieces = [part] + [along_ctx(part, shift) for shift in range(1, lax.axis_size("ctx"))]
    return in_order([piece.astype(single) for piece in pieces], device)


def sum_ctx(value):
    device = lax.axis_index("ctx")
    return ctx_spread(ctx_total(value, device).astype(bfloat), device)


def in_order(pieces, device, axis=0):
    size = len(pieces)
    count = pieces[0].shape[axis]
    shape = list(pieces[0].shape)
    shape[axis] = size * count
    result = jnp.zeros(shape, pieces[0].dtype)
    for shift, piece in enumerate(pieces):
        owner = (device - shift + size) % size
        result = lax.dynamic_update_slice_in_dim(result, piece, owner * count, axis=axis)
    return result


def together(*values):
    return lax.optimization_barrier(values)


def ctx_total(group, device):
    size = lax.axis_size("ctx")
    count = group.shape[0] // size

    def share(owner):
        return lax.dynamic_slice_in_dim(group, owner % size * count, count, axis=0)

    total = share(device).astype(single)
    for shift in range(1, size):
        total = total + along_ctx(share(device + shift), shift).astype(single)
    return total


def rank_table(route_block, experts, capacity):
    tokens = route_block.shape[0]
    expert_ids = jnp.arange(experts, dtype=jnp.int32)
    named = jnp.any(route_block[:, :, None] == expert_ids[None, None, :], axis=1)
    order = jnp.arange(tokens, dtype=jnp.int32)
    earlier = (order[:, None] > order[None, :]).astype(bfloat)
    rank = matmul(earlier, named.astype(bfloat)).astype(jnp.int32)
    return jnp.where(named & (rank < capacity), rank, -1)


def dispatch(rows):
    mine = to_chips(rows)
    return mine, to_core(mine)


def add_halves(mine, theirs):
    return (mine.astype(single) + to_core(theirs).astype(single)).astype(bfloat)


def local(
    layer_input,
    grad_output,
    routes,
    continuation_prompt,
    block_order,
    query_weight,
    latent_down,
    latent_up,
    output_weight,
    router_weight,
    shared_gate,
    shared_up,
    shared_down,
    attn_gain,
    latent_gain,
    ffn_gain,
    expert_gate,
    expert_up,
    expert_down,
):
    ctx_size = lax.axis_size("ctx")
    fsdp_size = lax.axis_size("fsdp")
    chips = fsdp_size // 2
    device = lax.axis_index("ctx")
    tokens = layer_input.shape[1]
    model_width = layer_input.shape[2]
    experts = router_weight.shape[1]
    group_tok = tokens * ctx_size
    block_len = PROMPT // (2 * ctx_size)
    cont_dev = CONTS * CONT_LEN // ctx_size
    capacity = (5 * tokens * TOP + 4 * experts - 1) // (4 * experts)
    slots = (capacity + 7) // 8 * 8
    score_scale = (NOPE + ROPE) ** (-0.5)
    shard_rows = latent_down.shape[0]
    down_width = latent_down.shape[1]
    hidden_dev = shared_down.shape[0] // ctx_size

    def hidden_columns(weight):
        parts = weight.reshape(shard_rows, fsdp_size, ctx_size, hidden_dev)
        return lax.dynamic_index_in_dim(parts, device, axis=2, keepdims=False).reshape(
            shard_rows, fsdp_size * hidden_dev
        )

    hidden_part = fsdp_size * hidden_dev
    part_down = lax.dynamic_slice_in_dim(shared_down, device * hidden_dev, hidden_dev, axis=0)
    part_shared = jnp.concatenate([hidden_columns(shared_gate), hidden_columns(shared_up)], axis=1)

    own_rows = jnp.arange(tokens, dtype=jnp.int32)
    link_table = continuation_prompt[0]
    own_seq, own_pos, own_link, own_rotary = row_layout(
        device, own_rows, block_order, link_table, block_len, cont_dev
    )
    prompt_rows = 2 * block_len
    first_cont = PROMPTS * prompt_rows
    link = lookup(link_table, (device * cont_dev // CONT_LEN)[None])
    key_pos = (block_order[:, None] * block_len + jnp.arange(block_len, dtype=jnp.int32)).reshape(-1)
    prompt_mask = jnp.where(key_pos[None, :] <= own_pos[:prompt_rows, None], 0.0, masked_score)
    cont_rows = device * cont_dev + jnp.arange(cont_dev, dtype=jnp.int32)
    cont_ids = jnp.arange(CONTS * CONT_LEN, dtype=jnp.int32)
    cont_mask = jnp.where(
        (cont_ids[None, :] // CONT_LEN == cont_rows[:, None] // CONT_LEN)
        & (cont_ids[None, :] <= cont_rows[:, None]),
        0.0,
        masked_score,
    )
    cos_table, sin_table = rotary_tables(own_rotary.astype(single))
    pair_cos = jnp.concatenate([cos_table] * 4, axis=1)
    pair_sin = jnp.concatenate([-sin_table, sin_table] * 2, axis=1)

    def by_sequence(group):
        blocks = group.reshape(ctx_size, tokens, -1)
        parts = [
            blocks[:, p * prompt_rows : (p + 1) * prompt_rows].reshape(PROMPT, -1)
            for p in range(PROMPTS)
        ]
        return jnp.concatenate(parts + [blocks[:, first_cont:].reshape(CONTS * CONT_LEN, -1)])

    def by_block(group):
        parts = [
            group[p * PROMPT : (p + 1) * PROMPT].reshape(ctx_size, prompt_rows, -1)
            for p in range(PROMPTS)
        ]
        last = group[PROMPTS * PROMPT :].reshape(ctx_size, cont_dev, -1)
        return jnp.concatenate(parts + [last], axis=1).reshape(group_tok, -1)

    plane_experts = device * chips + jnp.arange(chips, dtype=jnp.int32)
    chosen_here = plane_experts[:, None] == jnp.arange(experts, dtype=jnp.int32)[None, :]
    def here(table):
        return jnp.sum(jnp.where(chosen_here[:, None, :], table[None], 0), axis=2)

    slot_ids = jnp.arange(slots, dtype=jnp.int32)

    def pick_rows(step, rows):
        return jnp.einsum(
            "jrt,td->jrd", slot_pick[step], rows, preferred_element_type=single
        ).astype(bfloat)

    def put_rows(step, results):
        return jnp.einsum("jrt,jrd->td", slot_pick[step], results, preferred_element_type=single)

    def add_slots(route_block):
        ranks = rank_table(route_block, experts, capacity)
        match = here(ranks)[:, None, :] == slot_ids[None, :, None]
        slot_pick.append(match.astype(bfloat))
        return ranks

    slot_pick = []
    own_ranks = add_slots(routes[0])
    packed = gather_rows(
        jnp.concatenate(
            [
                latent_down,
                router_weight,
                attn_gain[:, None],
                ffn_gain[:, None],
                jnp.pad(latent_gain, (0, shard_rows - latent_gain.shape[0]))[:, None],
            ],
            axis=1,
        )
    )
    route_ring = [along_ctx(routes[0], s) for s in range(1, ctx_size)]
    grad_ring = [grad_output[0]]
    grad_next = ring_next(grad_ring[0])
    grad_mine = [to_chips(pick_rows(0, grad_ring[0]))]
    grad_theirs = []
    packed, query_shard, route_ring, grad_next, grad_mine[0] = together(
        packed, query_weight, route_ring, grad_next, grad_mine[0]
    )

    for route_block in route_ring:
        add_slots(route_block)
    full_down = packed[:, :down_width]
    full_router = packed[:, down_width : down_width + experts]
    gain_attn = packed[:, down_width + experts].astype(single)
    gain_ffn = packed[:, down_width + experts + 1].astype(single)
    gain_latent = (
        packed[:, down_width + experts + 2]
        .reshape(fsdp_size, shard_rows)[:, : latent_gain.shape[0]]
        .reshape(-1)
        .astype(single)
    )
    inputs_full = layer_input[0].astype(single)
    normed, attn_normal, attn_inverse = rms_forward(inputs_full, gain_attn)
    normed_low = normed.astype(bfloat)
    latent_pre = matmul(normed_low, full_down)
    latent, latent_normal, latent_inverse = rms_forward(latent_pre[:, :KV_RANK], gain_latent)
    latent_low = latent.astype(bfloat)
    key_rope_own = rotate(latent_pre[:, KV_RANK:], cos_table, sin_table).astype(bfloat)
    key_own = jnp.concatenate([latent_low, key_rope_own], axis=1)

    def more_grad_rows():
        step = len(grad_mine)
        grad_ring.append(grad_next)
        following = ring_next(grad_next) if step + 1 < ctx_size else grad_next
        theirs = to_core(grad_mine[-1])
        return following, theirs, to_chips(pick_rows(step, grad_ring[step]))

    full_query = gather_rows(query_shard)
    key_pieces = [key_own] + [along_ctx(key_own, s) for s in range(1, ctx_size)]
    grad_next, theirs, mine = more_grad_rows()
    full_query, up_shard, key_pieces, grad_next, theirs, mine = together(
        full_query, latent_up, key_pieces, grad_next, theirs, mine
    )
    grad_theirs.append(theirs)
    grad_mine.append(mine)

    full_up = gather_rows(up_shard)
    query_pre = matmul(normed_low, full_query)
    grad_next, theirs, mine = more_grad_rows()
    full_up, output_shard, query_pre, grad_next, theirs, mine = together(
        full_up, output_weight, query_pre, grad_next, theirs, mine
    )
    grad_theirs.append(theirs)
    grad_mine.append(mine)

    full_output = gather_rows(output_shard)
    key_group = by_sequence(in_order(key_pieces, device))
    latent_group = key_group[:, :KV_RANK]
    rope_pair = jnp.concatenate([key_group[:, KV_RANK:]] * 2, axis=1)
    kv_group = matmul(latent_group, full_up).astype(bfloat)
    rows_here = (prompt_rows, cont_dev)
    attended_low, log_total = attend(
        rows_here,
        score_scale,
        link,
        query_pre,
        pair_cos,
        pair_sin,
        kv_group,
        rope_pair,
        prompt_mask,
        cont_mask,
    )
    while len(grad_mine) < ctx_size:
        grad_next, theirs, mine = more_grad_rows()
        grad_theirs.append(theirs)
        grad_mine.append(mine)
    grad_group = jnp.concatenate(grad_ring)
    (
        full_output,
        shared_shard,
        down_shard,
        attended_low,
        grad_mine,
        grad_theirs,
        grad_group,
    ) = together(
        full_output,
        part_shared,
        part_down,
        attended_low,
        grad_mine,
        grad_theirs,
        grad_group,
    )
    grad_theirs.append(to_core(grad_mine[-1]))

    part_shared = gather_rows(shared_shard)
    part_down = gather_rows(down_shard)
    hidden = inputs_full + matmul(attended_low, full_output)
    ffn_in, ffn_normal, ffn_inverse = rms_forward(hidden, gain_ffn)
    ffn_low = ffn_in.astype(bfloat)
    logits = matmul(ffn_low, full_router)
    router_exps = jnp.exp(logits - jnp.max(logits, axis=1, keepdims=True))
    router = router_exps / jnp.sum(router_exps, axis=1, keepdims=True)
    route_match = jnp.any(
        routes[0][:, :, None] == jnp.arange(experts, dtype=jnp.int32)[None, None, :], axis=1
    )
    chosen_total = jnp.sum(jnp.where(route_match, router, 0.0), axis=1, keepdims=True)
    gates = jnp.where(route_match, router, 0.0) / chosen_total
    pair_weight = jnp.where(own_ranks >= 0, gates, 0.0)

    weight_high = pair_weight.astype(bfloat)
    weight_low = (pair_weight - weight_high.astype(single)).astype(bfloat)
    ffn_wide = jnp.concatenate(
        [
            ffn_low,
            weight_high,
            weight_low,
            jnp.zeros((tokens, EXTRA - 2 * experts), bfloat),
        ],
        axis=1,
    )
    own_expert = (device * chips + lax.axis_index("fsdp") // 2)[None].astype(jnp.int32)
    kept = []
    out_sends = []

    def flat(rows):
        return rows.reshape(-1, rows.shape[-1])

    def expert_step(step, mine, theirs):
        results, kept[:] = expert_call(
            step,
            ctx_size,
            experts,
            own_expert,
            flat(mine),
            flat(theirs),
            flat(grad_mine[step]),
            flat(grad_theirs[step]),
            expert_gate[0].T,
            expert_up[0].T,
            expert_down[0],
            kept,
        )
        return [rows.reshape(chips, slots, -1) for rows in results]

    def shared_step(rows, grad_act):
        gate_pre = matmul(rows, part_gate)
        up_pre = matmul(rows, part_up)
        act = (jax.nn.silu(gate_pre) * up_pre).astype(bfloat)
        grad_gate, grad_up = silu_grads(grad_act, gate_pre, up_pre)
        back = jnp.einsum("tf,df->td", grad_gate, part_gate, preferred_element_type=single)
        back = back + jnp.einsum("tf,df->td", grad_up, part_up, preferred_element_type=single)
        return act, grad_gate, grad_up, back

    def shared_grads():
        group = jnp.concatenate(groups)
        act, grad_gate, grad_up = [
            jnp.concatenate([part[i] for part in shared]) for i in range(3)
        ]
        pieces = [
            jnp.einsum("ta,tb->ab", left, right, preferred_element_type=single).astype(bfloat)
            for left, right in ((group, grad_gate), (group, grad_up), (act, grad_group))
        ]
        return jnp.concatenate(pieces[:2] + [pieces[2].reshape(model_width, hidden_part)], axis=1)

    last = ctx_size - 1
    ffn_ring = [ffn_wide]
    attended_ring = [attended_low]
    mines, theirs, backs, added, returned, out_added, out_steps = ({} for _ in range(7))
    shared, groups = [], []
    together_blocks = 4
    moving = None

    def of_block(which, step):
        first = step % together_blocks * tokens
        return shared[step // together_blocks][which][first : first + tokens]

    def block_part(step):
        part = put_rows(step, returned[step])
        return part + jnp.pad(of_block(3, step), ((0, 0), (0, EXTRA)))

    def hop(step):
        part = block_part(step)
        if moving is not None:
            part = part + moving.astype(single)
        return ring_next(part.astype(bfloat))

    for tick in range(ctx_size + 5):
        sent = {}
        if tick <= last:
            sent["mine"] = to_chips(pick_rows(tick, ffn_ring[tick]))
        if tick < last:
            sent["ring"] = ring_next(ffn_ring[tick])
        if 0 <= tick - 1 <= last:
            sent["theirs"] = to_core(mines[tick - 1])
        if 0 <= tick - 2 <= last:
            sent["back"] = expert_step(tick - 2, mines[tick - 2], theirs[tick - 2])
        if 0 <= tick - 3 <= last:
            sent["added"] = add_halves(*backs[tick - 3])
        if 0 <= tick - 4 <= last:
            sent["returned"] = to_chips(added[tick - 4])
        first = tick - 4
        if 0 <= first <= last and first % together_blocks == 0:
            sent["group"] = jnp.concatenate(
                [
                    block[:, :model_width]
                    for block in ffn_ring[first : first + together_blocks]
                ]
            )
        first = tick - 5
        if 0 <= first <= last and first % together_blocks == 0:
            rows = groups[-1].shape[0]
            shared.append(
                shared_step(groups[-1], grad_act[first * tokens : first * tokens + rows])
            )
            sent["shared"] = shared[-1]
        if 1 <= tick - 5 <= last:
            sent["moving"] = hop(tick - 5)
        if tick == 0:
            sent["grads"] = grad_theirs[-1]
        if tick == 1:
            sent["weights"] = (part_shared, part_down)
            sent["grad_act"] = jnp.einsum(
                "td,fd->tf", grad_group, part_down, preferred_element_type=single
            )
        if tick == ctx_size + 3:
            sent["shared_all"] = (shared, groups, grad_group)
            sent["out"] = add_halves(*out_sends[1])
        if tick == ctx_size + 4:
            sent["shared_grads"] = shared_grads()
            sent["out_step"] = to_chips(out_added[1])
        if last <= tick < 2 * last:
            sent["attended"] = ring_next(attended_ring[-1])
        if tick == ctx_size + 4:
            sent["out"] = add_halves(*out_sends[2])
        names = sorted(sent)
        sent = dict(zip(names, together(*(sent[name] for name in names))))
        if "mine" in sent:
            mines[tick] = sent["mine"]
        if "ring" in sent:
            ffn_ring.append(sent["ring"])
        if "theirs" in sent:
            theirs[tick - 1] = sent["theirs"]
        if "back" in sent:
            backs[tick - 2] = sent["back"][:2]
            out_sends.append(sent["back"][2:])
        if "added" in sent:
            added[tick - 3] = sent["added"]
        if "returned" in sent:
            returned[tick - 4] = sent["returned"]
        if "group" in sent:
            groups.append(sent["group"])
        if "shared" in sent:
            shared[-1] = sent["shared"]
        if "shared_all" in sent:
            shared, groups, grad_group = sent["shared_all"]
        if "attended" in sent:
            attended_ring.append(sent["attended"])
        if "out" in sent:
            out_added[tick - ctx_size - 2] = sent["out"]
        if "out_step" in sent:
            out_steps[1] = sent["out_step"]
        moving = sent.get("moving", moving)
        if tick == 0:
            grad_theirs[-1] = sent["grads"]
        if tick == 1:
            part_gate = sent["weights"][0][:, :hidden_part]
            part_up = sent["weights"][0][:, hidden_part:]
            part_down = sent["weights"][1]
            grad_act = sent["grad_act"]

    while len(attended_ring) < ctx_size:
        attended_ring.append(ring_next(attended_ring[-1]))
    shared_part = scatter_rows(sent["shared_grads"])
    first_part = block_part(0)

    def next_out(step):
        ahead = (step + 1) % ctx_size
        return to_chips(out_added[step]), add_halves(*out_sends[ahead]) if step else out_added[step]

    grad_wide = moving.astype(single) + first_part
    grad_ffn = grad_wide[:, :model_width]
    grad_gate_pair = jnp.where(
        own_ranks >= 0, grad_wide[:, model_width : model_width + experts], 0.0
    )

    grad_low = grad_output[0]
    grad_top = grad_low.astype(single)
    grad_chosen = (
        grad_gate_pair - jnp.sum(grad_gate_pair * gates, axis=1, keepdims=True)
    ) / chosen_total
    grad_router = jnp.where(route_match, grad_chosen, 0.0)
    grad_logits = (
        router * (grad_router - jnp.sum(router * grad_router, axis=1, keepdims=True))
    ).astype(bfloat)
    grad_w_router = jnp.einsum("td,te->de", ffn_low, grad_logits, preferred_element_type=single)
    grad_ffn = grad_ffn + jnp.einsum(
        "te,de->td", grad_logits, full_router, preferred_element_type=single
    )
    grad_hidden_norm, grad_gain_ffn = rms_backward(grad_ffn, ffn_normal, ffn_inverse, gain_ffn)
    grad_hidden = grad_top + grad_hidden_norm
    grad_attn_low = grad_hidden.astype(bfloat)

    def out_hop(step, moving):
        part = put_rows(step, out_steps[step]) + matmul(of_block(0, step), part_down)
        if moving is not None:
            part = part + moving.astype(single)
        return ring_next(part.astype(bfloat))

    grad_attended = jnp.einsum(
        "td,vd->tv", grad_attn_low, full_output, preferred_element_type=single
    ).astype(bfloat)
    out_steps[2] = to_chips(out_added[2])
    out_moving = out_hop(1, None)
    att_shares = column_shares(grad_attn_low, device)
    grad_attended, out_sends = together(grad_attended, out_sends)

    def weight_grad(left, right):
        return jnp.einsum("ra,rb->ab", left, right, preferred_element_type=single)

    grad_w_output = weight_grad(jnp.concatenate(attended_ring), jnp.concatenate(att_shares))

    out_added[3] = add_halves(*out_sends[3])

    log_rows = log_total[:, :HEADS].T.reshape(HEADS // 2, 2, tokens)
    grad_nope, grad_rope, grad_key_part, grad_value_part, rope_pair_grad = attend_back(
        rows_here,
        score_scale,
        link,
        query_pre,
        pair_cos,
        pair_sin,
        kv_group,
        rope_pair,
        prompt_mask.T,
        cont_mask.T,
        log_rows,
        grad_attended,
    )
    (
        grad_nope,
        grad_rope,
        grad_key_part,
        grad_value_part,
        rope_pair_grad,
        out_steps[2],
        out_added[3],
        out_moving,
        shared_part,
        grad_w_output,
    ) = together(
        grad_nope,
        grad_rope,
        grad_key_part,
        grad_value_part,
        rope_pair_grad,
        out_steps[2],
        out_added[3],
        out_moving,
        shared_part,
        grad_w_output,
    )
    out_next = next_out(3)
    out_moving = out_hop(2, out_moving)
    output_part = scatter_rows(grad_w_output)
    grad_key_rope = rope_pair_grad[:, :ROPE] + rope_pair_grad[:, ROPE:]
    keys_width = HEADS * NOPE
    grad_latent_group = jnp.einsum(
        "tk,ck->tc", grad_key_part, full_up[:, :keys_width], preferred_element_type=single
    ) + jnp.einsum(
        "tk,ck->tc", grad_value_part, full_up[:, keys_width:], preferred_element_type=single
    )
    grad_query_pre = jnp.concatenate([grad_nope, grad_rope], axis=1)
    grad_w_query = weight_grad(normed_low, grad_query_pre)
    grad_keys_own = ctx_total(
        by_block(jnp.concatenate([grad_latent_group, grad_key_rope], axis=1).astype(bfloat)), device
    )
    grad_keys_own, output_part, grad_w_query, out_next, out_moving = together(
        grad_keys_own, output_part, grad_w_query, out_next, out_moving
    )
    out_steps[3], out_added[4 % ctx_size] = out_next
    for step in range(3, ctx_size):
        if step > 3:
            out_steps[step], out_added[(step + 1) % ctx_size] = next_out(step)
        out_moving = out_hop(step, out_moving)
    out_steps[0] = to_chips(out_added[0])
    query_part = scatter_rows(grad_w_query)
    shared_ring = [shared_part, ring_next(shared_part)]
    shared_ring.append(ring_next(shared_ring[-1]))
    sum_output = all_columns_of(output_part, device)
    grad_w_up = jnp.concatenate(
        [
            weight_grad(latent_group, part).astype(bfloat).reshape(model_width, -1)
            for part in (grad_key_part, grad_value_part)
        ],
        axis=1,
    )
    grad_latent = grad_keys_own[:, :KV_RANK]
    grad_rope_own = grad_keys_own[:, KV_RANK:]
    grad_latent_in, grad_gain_latent = rms_backward(
        grad_latent, latent_normal, latent_inverse, gain_latent
    )
    grad_rope_in = rotate(grad_rope_own, cos_table, -sin_table)
    grad_latent_pre = jnp.concatenate([grad_latent_in, grad_rope_in], axis=1).astype(bfloat)
    grad_w_down = jnp.einsum(
        "td,tk->dk",
        normed_low,
        jnp.pad(grad_latent_pre, ((0, 0), (0, -down_width % 128))),
        preferred_element_type=single,
    )
    grad_normed = jnp.einsum(
        "tq,dq->td", grad_query_pre, full_query, preferred_element_type=single
    ) + jnp.einsum("tk,dk->td", grad_latent_pre, full_down, preferred_element_type=single)
    grad_x_norm, grad_gain_attn = rms_backward(grad_normed, attn_normal, attn_inverse, gain_attn)
    grad_input = (grad_hidden + grad_x_norm).astype(bfloat)

    padded_latent = jnp.pad(
        grad_gain_latent.reshape(fsdp_size, -1),
        ((0, 0), (0, shard_rows - latent_gain.shape[0])),
    ).reshape(-1)
    up_width = grad_w_up.shape[1]
    small = jnp.concatenate(
        [
            grad_w_router,
            grad_gain_attn[:, None],
            grad_gain_ffn[:, None],
            padded_latent[:, None],
        ],
        axis=1,
    ).astype(bfloat)
    packed_grads = jnp.concatenate(
        [
            grad_w_up,
            grad_w_down.astype(bfloat),
            jnp.pad(small, ((0, 0), (0, -small.shape[1] % 128))),
        ],
        axis=1,
    )
    (
        query_part,
        packed_grads,
        shared_ring,
        kept,
        out_moving,
        out_steps[0],
        sum_output,
    ) = together(
        query_part, packed_grads, shared_ring, kept, out_moving, out_steps[0], sum_output
    )
    packed_part = scatter_rows(with_layout_constraint(packed_grads, by_rows))
    all_rows, all_grads, all_act, all_gate, all_up = kept
    grad_piece_down = weight_grad(all_act, all_grads)
    grad_piece_gate = weight_grad(all_rows, all_gate)
    sum_query = sum_ctx(query_part)
    packed_part, sum_query, grad_piece_down, grad_piece_gate, kept = together(
        packed_part, sum_query, grad_piece_down, grad_piece_gate, kept
    )
    all_rows, all_grads, all_act, all_gate, all_up = kept
    grad_piece_up = weight_grad(all_rows, all_up)
    while len(shared_ring) < ctx_size:
        shared_ring.append(ring_next(shared_ring[-1]))
    first_out = put_rows(0, out_steps[0]) + matmul(of_block(0, 0), part_down)
    layer_output = (hidden + out_moving.astype(single) + first_out).astype(bfloat)
    sum_packed = with_layout_constraint(
        sum_ctx(with_layout_constraint(packed_part, by_rows)), by_rows
    )
    sum_up = jnp.concatenate(
        [
            part.reshape(latent_up.shape[0], -1)
            for part in (sum_packed[:, : up_width // 2], sum_packed[:, up_width // 2 : up_width])
        ],
        axis=1,
    )
    sum_down = sum_packed[:, up_width : up_width + down_width]
    sum_small = sum_packed[:, up_width + grad_w_down.shape[1] :]
    sum_router = sum_small[:, :experts]
    sum_gain_attn = sum_small[:, experts]
    sum_gain_ffn = sum_small[:, experts + 1]
    sum_gain_latent = sum_small[: latent_gain.shape[0], experts + 2]

    shared_blocks = in_order([piece[None] for piece in shared_ring], device)

    def all_columns(blocks):
        blocks = blocks.reshape(ctx_size, shard_rows, fsdp_size, hidden_dev)
        return blocks.transpose(1, 2, 0, 3).reshape(shard_rows, -1).astype(single)

    sum_sh_gate = all_columns(shared_blocks[:, :, :hidden_part])
    sum_sh_up = all_columns(shared_blocks[:, :, hidden_part : 2 * hidden_part])
    sum_sh_down = shared_blocks[:, :, 2 * hidden_part :].reshape(shared_down.shape).astype(single)
    return (
        layer_output[None],
        grad_input[None],
        sum_query,
        sum_down,
        sum_up,
        sum_output,
        sum_router,
        sum_sh_gate,
        sum_sh_up,
        sum_sh_down,
        sum_gain_attn,
        sum_gain_latent,
        sum_gain_ffn,
        grad_piece_gate[None],
        grad_piece_up[None],
        grad_piece_down[None],
    )


def solution(mesh):
    in_specs = (
        P("fsdp", "ctx", None),
        P("fsdp", "ctx", None),
        P("fsdp", "ctx", None),
        P("fsdp", None),
        P(),
        P("fsdp", None),
        P("fsdp", None),
        P("fsdp", None),
        P("fsdp", None),
        P("fsdp", None),
        P("fsdp", None),
        P("fsdp", None),
        P("fsdp", None),
        P("fsdp"),
        P("fsdp"),
        P("fsdp"),
        P(("ctx", "fsdp"), None, None),
        P(("ctx", "fsdp"), None, None),
        P(("ctx", "fsdp"), None, None),
    )
    out_specs = (
        P("fsdp", "ctx", None),
        P("fsdp", "ctx", None),
        P("fsdp", None),
        P("fsdp", None),
        P("fsdp", None),
        P("fsdp", None),
        P("fsdp", None),
        P("fsdp", None),
        P("fsdp", None),
        P("fsdp", None),
        P("fsdp"),
        P("fsdp"),
        P("fsdp"),
        P(("ctx", "fsdp"), None, None),
        P(("ctx", "fsdp"), None, None),
        P(("ctx", "fsdp"), None, None),
    )
    return jax.shard_map(local, mesh=mesh, in_specs=in_specs, out_specs=out_specs, check_vma=False)
```

```python
import functools

import jax
import jax.numpy as jnp
from jax import lax
from jax.experimental import pallas as pl
from jax.experimental.layout import Layout, with_layout_constraint
from jax.experimental.pallas import tpu as pltpu
from jax.sharding import PartitionSpec as P

HEADS = 16
NOPE = 128
ROPE = 64
VDIM = 128
KV_RANK = 512
TOP = 6
PROMPT = 512
PROMPTS = 2
CONT_LEN = 128
CONTS = 2


epsilon = 1e-06
masked_score = -1e30
bfloat = jnp.bfloat16
single = jnp.float32


EXTRA = 128
by_rows = Layout(major_to_minor=(0, 1))


def matmul(left, right):
    return jnp.dot(left, right, preferred_element_type=single)


def rms_forward(values, gain):
    inverse = lax.rsqrt(jnp.mean(values * values, axis=-1, keepdims=True) + epsilon)
    normal_part = values * inverse
    return (normal_part * gain, normal_part, inverse)


def rms_backward(grad_out, normal_part, inverse, gain):
    grad_normal = grad_out * gain
    grad_gain = jnp.sum(grad_out * normal_part, axis=0)
    grad_in = inverse * (
        grad_normal - normal_part * jnp.mean(grad_normal * normal_part, axis=-1, keepdims=True)
    )
    return (grad_in, grad_gain)


def rotary_tables(positions):
    exponent = jnp.arange(ROPE // 2, dtype=jnp.float32) * (2.0 / ROPE)
    frequency = jnp.exp(-jnp.log(10000.0) * exponent)
    angles = positions[:, None] * frequency[None, :]
    return (jnp.cos(angles), jnp.sin(angles))


def rotate(values, cos_table, sin_table):
    half_width = values.shape[-1] // 2
    first_half = values[..., :half_width]
    second = values[..., half_width:]
    return jnp.concatenate(
        [first_half * cos_table - second * sin_table, second * cos_table + first_half * sin_table],
        axis=-1,
    )


def lookup(table_values, wanted):
    matches = wanted[:, None] == jnp.arange(table_values.shape[0], dtype=jnp.int32)[None, :]
    return jnp.sum(jnp.where(matches, table_values[None, :], 0), axis=1)


def row_layout(device, local_row, block_order, link_table, block_len, cont_dev):
    prompt_rows = PROMPTS * 2 * block_len
    in_prompt = local_row < prompt_rows
    prompt_id = local_row // (2 * block_len)
    half_slot = local_row // block_len % 2
    prompt_pos = lookup(block_order, 2 * device + half_slot) * block_len + local_row % block_len
    cont_index = device * cont_dev + jnp.maximum(local_row - prompt_rows, 0)
    cont_id = jnp.minimum(cont_index // CONT_LEN, CONTS - 1)
    cont_pos = cont_index % CONT_LEN
    sequence = jnp.where(in_prompt, prompt_id, PROMPTS + cont_id)
    position = jnp.where(in_prompt, prompt_pos, cont_pos)
    linked = jnp.where(in_prompt, -1, lookup(link_table, cont_id))
    rotary = jnp.where(in_prompt, prompt_pos, PROMPT + cont_pos)
    return (sequence, position, linked, rotary)


def silu_grads(grad_act, gate_pre, up_pre):
    sigmoid_gate = jax.nn.sigmoid(gate_pre)
    grad_gate = (grad_act * up_pre * sigmoid_gate * (1.0 + gate_pre * (1.0 - sigmoid_gate))).astype(
        bfloat
    )
    grad_up = (grad_act * gate_pre * sigmoid_gate).astype(bfloat)
    return (grad_gate, grad_up)


NT = (((1,), (1,)), ((), ()))
TN = (((0,), (0,)), ((), ()))


def product(left, right, dims):
    return lax.dot_general(left, right, dims, preferred_element_type=single)


def half_swap(values):
    width = values.shape[1]
    lane = lax.broadcasted_iota(jnp.int32, values.shape, 1)
    ahead = pltpu.roll(values, width - ROPE // 2, 1)
    behind = pltpu.roll(values, ROPE // 2, 1)
    return jnp.where(lane % ROPE < ROPE // 2, ahead, behind)


def head_query(nope, rotated, which):
    lane = lax.broadcasted_iota(jnp.int32, rotated.shape, 1)
    kept = jnp.where((lane >= ROPE) == (which == 1), rotated, 0.0)
    return jnp.concatenate(
        [nope[:, which * NOPE : (which + 1) * NOPE].astype(bfloat), kept.astype(bfloat)], axis=1
    )


def attend_kernel(
    rows, scale, link, nope, rope, cos, sin, keys, values, key_rope, prompt_mask, cont_mask, out, lse
):
    pair = pl.program_id(0)
    prompt_rows, cont_rows = rows
    first = prompt_rows * PROMPTS
    linked = pl.multiple_of(link[0] * PROMPT, PROMPT)
    rotated = rope[...] * cos[...] + half_swap(rope[...]) * sin[...]
    nopes = nope[...]

    @pl.when(pair == 0)
    def _():
        lse[...] = jnp.zeros_like(lse)

    def key_part(start, count, which):
        return jnp.concatenate(
            [keys[pl.ds(start, count), which * NOPE : (which + 1) * NOPE], key_rope[pl.ds(start, count), :]],
            axis=1,
        )

    def value_part(start, count, which):
        return values[pl.ds(start, count), which * VDIM : (which + 1) * VDIM]

    for which in range(2):
        query = head_query(nopes, rotated, which)
        outs = []
        logs = []
        for prompt in range(PROMPTS):
            part = query[prompt * prompt_rows : (prompt + 1) * prompt_rows]
            scores = product(part, key_part(prompt * PROMPT, PROMPT, which), NT) * scale
            scores = scores + prompt_mask[...]
            top = jnp.max(scores, axis=1, keepdims=True)
            exps = jnp.exp(scores - top)
            total = jnp.sum(exps, axis=1, keepdims=True)
            probs = (exps / total).astype(bfloat)
            outs.append(matmul(probs, value_part(prompt * PROMPT, PROMPT, which)))
            logs.append(top + jnp.log(total))
        part = query[first:]
        cont_keys = CONTS * CONT_LEN
        scores = product(part, key_part(linked, PROMPT, which), NT) * scale
        near = product(part, key_part(PROMPTS * PROMPT, cont_keys, which), NT) * scale
        near = near + cont_mask[...]
        top = jnp.maximum(
            jnp.max(scores, axis=1, keepdims=True), jnp.max(near, axis=1, keepdims=True)
        )
        exps = jnp.exp(scores - top)
        near_exps = jnp.exp(near - top)
        total = jnp.sum(exps, axis=1, keepdims=True) + jnp.sum(near_exps, axis=1, keepdims=True)
        outs.append(
            matmul((exps / total).astype(bfloat), value_part(linked, PROMPT, which))
            + matmul(
                (near_exps / total).astype(bfloat), value_part(PROMPTS * PROMPT, cont_keys, which)
            )
        )
        logs.append(top + jnp.log(total))
        out[:, which * VDIM : (which + 1) * VDIM] = jnp.concatenate(outs, axis=0).astype(bfloat)
        lane = lax.broadcasted_iota(jnp.int32, lse.shape, 1)
        lse[...] = jnp.where(lane == 2 * pair + which, jnp.concatenate(logs, axis=0), lse[...])


def attend_back_kernel(
    rows,
    scale,
    link,
    nope,
    rope,
    cos,
    sin,
    keys,
    values,
    key_rope,
    prompt_mask,
    cont_mask,
    lse,
    grad,
    grad_nope,
    grad_rope,
    grad_keys,
    grad_values,
    grad_key_rope,
    key_sum,
    value_sum,
    rope_sum,
):
    pair = pl.program_id(0)
    prompt_rows, cont_rows = rows
    first = prompt_rows * PROMPTS
    linked = pl.multiple_of(link[0] * PROMPT, PROMPT)
    cont_start = PROMPTS * PROMPT
    cont_keys = CONTS * CONT_LEN
    rotated = rope[...] * cos[...] + half_swap(rope[...]) * sin[...]
    nopes = nope[...]

    @pl.when(pair == 0)
    def _():
        rope_sum[...] = jnp.zeros_like(rope_sum)

    rope_grads = []
    for which in range(2):
        query = head_query(nopes, rotated, which)
        log_row = lse[which : which + 1, :]
        query_grads = []

        def one(lo, hi, start, count, mask):
            part = query[lo:hi]
            key_cat = jnp.concatenate(
                [
                    keys[pl.ds(start, count), which * NOPE : (which + 1) * NOPE],
                    key_rope[pl.ds(start, count), :],
                ],
                axis=1,
            )
            value = values[pl.ds(start, count), which * VDIM : (which + 1) * VDIM]
            grad_part = grad[lo:hi, which * VDIM : (which + 1) * VDIM]
            scores = product(key_cat, part, NT) * scale
            if mask is not None:
                scores = scores + mask
            probs = jnp.exp(scores - log_row[:, lo:hi])
            grad_probs = product(value, grad_part, NT)
            return part, key_cat, grad_part, probs, grad_probs

        def finish(parts, delta):
            part, key_cat, grad_part, probs, grad_probs = parts
            grad_scores = (probs * (grad_probs - delta)).astype(bfloat)
            query_grad = product(grad_scores, key_cat, TN)
            key_grad = matmul(grad_scores, part) * scale
            value_grad = matmul(probs.astype(bfloat), grad_part)
            return query_grad, key_grad, value_grad

        def delta_of(parts):
            return jnp.sum(parts[3] * parts[4], axis=0, keepdims=True)

        for prompt in range(PROMPTS):
            lo, hi = prompt * prompt_rows, (prompt + 1) * prompt_rows
            start = prompt * PROMPT
            parts = one(lo, hi, start, PROMPT, prompt_mask[...])
            query_grad, key_grad, value_grad = finish(parts, delta_of(parts))
            query_grads.append(query_grad)
            key_sum[start : start + PROMPT, :] = key_grad[:, :NOPE]
            value_sum[start : start + PROMPT, :] = value_grad
            rope_sum[start : start + PROMPT, :] += key_grad[:, NOPE:]
        far = one(first, first + cont_rows, linked, PROMPT, None)
        near = one(first, first + cont_rows, cont_start, cont_keys, cont_mask[...])
        delta = delta_of(far) + delta_of(near)
        far_query, far_key, far_value = finish(far, delta)
        near_query, near_key, near_value = finish(near, delta)
        query_grads.append(far_query + near_query)
        span = pl.ds(linked, PROMPT)
        key_sum[span, :] += far_key[:, :NOPE]
        value_sum[span, :] += far_value
        rope_sum[span, :] += far_key[:, NOPE:]
        key_sum[cont_start:, :] = near_key[:, :NOPE]
        value_sum[cont_start:, :] = near_value
        rope_sum[cont_start:, :] += near_key[:, NOPE:]
        query_grad = jnp.concatenate(query_grads, axis=0) * scale
        grad_nope[:, which * NOPE : (which + 1) * NOPE] = query_grad[:, :NOPE].astype(bfloat)
        rope_grads.append(query_grad[:, NOPE:])
        grad_keys[:, which * NOPE : (which + 1) * NOPE] = key_sum[...].astype(bfloat)
        grad_values[:, which * VDIM : (which + 1) * VDIM] = value_sum[...].astype(bfloat)
    lane = lax.broadcasted_iota(jnp.int32, rope_grads[0].shape, 1)
    both = jnp.where(lane < ROPE, rope_grads[0], rope_grads[1])
    grad_rope[...] = (both * cos[...] - half_swap(both) * sin[...]).astype(bfloat)
    grad_key_rope[...] = rope_sum[...]


def whole(shape):
    return pl.BlockSpec(shape, lambda pair: (0,) * len(shape))


def pair_specs(tokens, key_rows, prompt_mask, cont_mask):
    nope_blocks = HEADS * NOPE // (2 * ROPE)
    return [
        pl.BlockSpec(memory_space=pltpu.SMEM),
        pl.BlockSpec((tokens, 2 * NOPE), lambda pair: (0, pair)),
        pl.BlockSpec((tokens, 2 * ROPE), lambda pair: (0, nope_blocks + pair)),
        whole((tokens, 2 * ROPE)),
        whole((tokens, 2 * ROPE)),
        pl.BlockSpec((key_rows, 2 * NOPE), lambda pair: (0, pair)),
        pl.BlockSpec((key_rows, 2 * VDIM), lambda pair: (0, HEADS // 2 + pair)),
        whole((key_rows, 2 * ROPE)),
        whole(prompt_mask),
        whole(cont_mask),
    ]


def attend(rows, scale, link, query_pre, cos, sin, kv, key_rope, prompt_mask, cont_mask):
    tokens = query_pre.shape[0]
    key_rows = kv.shape[0]
    work = 2 * (rows[0] * PROMPT * PROMPTS + rows[1] * (PROMPT + CONTS * CONT_LEN)) * HEADS
    return pl.pallas_call(
        functools.partial(attend_kernel, rows, scale),
        grid=(HEADS // 2,),
        in_specs=pair_specs(tokens, key_rows, prompt_mask.shape, cont_mask.shape),
        out_specs=[
            pl.BlockSpec((tokens, 2 * VDIM), lambda pair: (0, pair)),
            whole((tokens, 128)),
        ],
        out_shape=[
            jax.ShapeDtypeStruct((tokens, HEADS * VDIM), bfloat),
            jax.ShapeDtypeStruct((tokens, 128), single),
        ],
        compiler_params=pltpu.CompilerParams(vmem_limit_bytes=40 * 2**20),
        cost_estimate=pl.CostEstimate(
            flops=work * 384, bytes_accessed=2 * kv.size + 6 * query_pre.size, transcendentals=work // 2
        ),
    )(link, query_pre, query_pre, cos, sin, kv, kv, key_rope, prompt_mask, cont_mask)


def attend_back(
    rows, scale, link, query_pre, cos, sin, kv, key_rope, prompt_mask, cont_mask, lse, grad
):
    tokens = query_pre.shape[0]
    key_rows = kv.shape[0]
    work = 2 * (rows[0] * PROMPT * PROMPTS + rows[1] * (PROMPT + CONTS * CONT_LEN)) * HEADS
    return pl.pallas_call(
        functools.partial(attend_back_kernel, rows, scale),
        grid=(HEADS // 2,),
        in_specs=pair_specs(tokens, key_rows, prompt_mask.shape, cont_mask.shape)
        + [
            pl.BlockSpec((None, 2, tokens), lambda pair: (pair, 0, 0)),
            pl.BlockSpec((tokens, 2 * VDIM), lambda pair: (0, pair)),
        ],
        out_specs=[
            pl.BlockSpec((tokens, 2 * NOPE), lambda pair: (0, pair)),
            pl.BlockSpec((tokens, 2 * ROPE), lambda pair: (0, pair)),
            pl.BlockSpec((key_rows, 2 * NOPE), lambda pair: (0, pair)),
            pl.BlockSpec((key_rows, 2 * VDIM), lambda pair: (0, pair)),
            whole((key_rows, 2 * ROPE)),
        ],
        out_shape=[
            jax.ShapeDtypeStruct((tokens, HEADS * NOPE), bfloat),
            jax.ShapeDtypeStruct((tokens, HEADS * ROPE), bfloat),
            jax.ShapeDtypeStruct((key_rows, HEADS * NOPE), bfloat),
            jax.ShapeDtypeStruct((key_rows, HEADS * VDIM), bfloat),
            jax.ShapeDtypeStruct((key_rows, 2 * ROPE), single),
        ],
        scratch_shapes=[
            pltpu.VMEM((key_rows, NOPE), single),
            pltpu.VMEM((key_rows, VDIM), single),
            pltpu.VMEM((key_rows, 2 * ROPE), single),
        ],
        compiler_params=pltpu.CompilerParams(vmem_limit_bytes=48 * 2**20),
        cost_estimate=pl.CostEstimate(
            flops=work * 1152, bytes_accessed=4 * kv.size + 10 * query_pre.size, transcendentals=work // 2
        ),
    )(link, query_pre, query_pre, cos, sin, kv, kv, key_rope, prompt_mask, cont_mask, lse, grad)


def expert_kernel(
    first_row,
    experts,
    expert,
    mine,
    theirs,
    grad_mine,
    grad_theirs,
    gate,
    up,
    down,
    *refs,
):
    back_mine, back_theirs, out_mine, out_theirs = refs[-21:-17]
    all_rows, all_grads, all_act, all_gate, all_up = refs[-17:-12]
    rows, grads, gate_w, up_w, down_w, act, grad_gate, grad_up, back, out = refs[-12:-2]
    in_sems, out_sems = refs[-2:]
    count = mine.shape[0]
    hidden, width = gate.shape
    lane = lax.broadcasted_iota(jnp.int32, (count, EXTRA), 1)
    here = lane == expert[0]
    loads = [
        pltpu.make_async_copy(source, target, in_sems.at[i])
        for i, (source, target) in enumerate(
            [
                (theirs, rows.at[1]),
                (gate, gate_w),
                (up, up_w),
                (grad_theirs, grads.at[1]),
                (down, down_w),
                (mine, rows.at[0]),
                (grad_mine, grads.at[0]),
            ]
        )
    ]
    for load in loads:
        load.start()

    def store(half, which):
        span = pl.ds(first_row + half * count, count)
        pairs = [
            (rows.at[half, :, pl.ds(0, width)], all_rows.at[span, :]),
            (grads.at[half], all_grads.at[span, :]),
            (act.at[half], all_act.at[span, :]),
            (grad_gate.at[half], all_gate.at[span, :]),
            (grad_up.at[half], all_up.at[span, :]),
            (back.at[half], (back_mine, back_theirs)[half]),
            (out.at[half], (out_mine, out_theirs)[half]),
        ]
        source, target = pairs[which]
        return pltpu.make_async_copy(source, target, out_sems.at[half, which])

    def one_half(turn, carry):
        half = 1 - turn

        def await_loads(first, second):
            for when, which in enumerate((first, second)):
                if which:

                    @pl.when(turn == when)
                    def _(which=which):
                        for i in which:
                            loads[i].wait()

        def start_stores(which):
            for when in range(2):

                @pl.when(turn == when)
                def _(when=when):
                    for i in which:
                        store(1 - when, i).start()

        await_loads((0, 1), (5,))
        start_stores((0,))
        extra = rows[half, :, width:].astype(single)
        slot_weight = jnp.sum(
            jnp.where(here | (lane == expert[0] + experts), extra, 0.0), axis=1, keepdims=True
        )
        total = jnp.zeros((count, 1), single)
        for lo in range(0, hidden, 256):
            hi = min(lo + 256, hidden)
            gate_pre = product(rows[half, :, :width], gate_w[lo:hi, :], NT)
            if lo == 0:
                await_loads((2,), ())
            up_pre = product(rows[half, :, :width], up_w[lo:hi, :], NT)
            if lo == 0:
                await_loads((3, 4), (6,))
                start_stores((1,))
            grad_act = product(grads[half], down_w[lo:hi, :], NT)
            sigmoid = 1.0 / (1.0 + jnp.exp(-gate_pre))
            silu = gate_pre * sigmoid
            value = silu * up_pre
            total = total + jnp.sum(
                value.astype(bfloat).astype(single) * grad_act, axis=1, keepdims=True
            )
            grad_act = grad_act * slot_weight
            act[half, :, lo:hi] = (value * slot_weight).astype(bfloat)
            grad_gate[half, :, lo:hi] = (
                grad_act * up_pre * sigmoid * (1.0 + gate_pre * (1.0 - sigmoid))
            ).astype(bfloat)
            grad_up[half, :, lo:hi] = (grad_act * silu).astype(bfloat)
        start_stores((2, 3, 4))
        back[half, :, width:] = jnp.where(here, total, 0.0).astype(bfloat)
        step = min(512, width)
        for lo in range(0, width, step):
            hi = lo + step
            part = matmul(grad_gate[half], gate_w[:, lo:hi])
            part = part + matmul(grad_up[half], up_w[:, lo:hi])
            back[half, :, lo:hi] = part.astype(bfloat)
        start_stores((5,))
        for lo in range(0, width, step):
            hi = lo + step
            out[half, :, lo:hi] = matmul(act[half], down_w[:, lo:hi]).astype(bfloat)
        start_stores((6,))
        return carry

    lax.fori_loop(0, 2, one_half, 0)
    for half in range(2):
        for which in range(7):
            store(half, which).wait()


def expert_call(
    step, steps, experts, expert, mine, theirs, grad_mine, grad_theirs, gate, up, down, kept
):
    count, wide = mine.shape
    hidden, width = gate.shape
    anywhere = pl.BlockSpec(memory_space=pl.ANY)
    back_shape = jax.ShapeDtypeStruct((count, wide), bfloat)
    out_shape = jax.ShapeDtypeStruct((count, width), bfloat)
    kept_shapes = [
        jax.ShapeDtypeStruct((steps * 2 * count, columns), bfloat)
        for columns in (width, width, hidden, hidden, hidden)
    ]
    outs = pl.pallas_call(
        functools.partial(expert_kernel, step * 2 * count, experts),
        in_specs=[pl.BlockSpec(memory_space=pltpu.SMEM)] + [anywhere] * (7 + len(kept)),
        out_specs=[anywhere] * 9,
        out_shape=[back_shape] * 2 + [out_shape] * 2 + kept_shapes,
        input_output_aliases={8 + i: 4 + i for i in range(len(kept))},
        scratch_shapes=[
            pltpu.VMEM((2, count, wide), bfloat),
            pltpu.VMEM((2, count, width), bfloat),
        ]
        + [pltpu.VMEM((hidden, width), bfloat)] * 3
        + [pltpu.VMEM((2, count, hidden), bfloat)] * 3
        + [pltpu.VMEM((2, count, wide), bfloat), pltpu.VMEM((2, count, width), bfloat)]
        + [pltpu.SemaphoreType.DMA((7,)), pltpu.SemaphoreType.DMA((2, 7))],
        compiler_params=pltpu.CompilerParams(vmem_limit_bytes=56 * 2**20),
        cost_estimate=pl.CostEstimate(
            flops=2 * 6 * 2 * count * width * hidden,
            bytes_accessed=2 * (12 * count * width + 3 * hidden * width + 6 * count * hidden),
            transcendentals=2 * count * hidden,
        ),
    )(expert, mine, theirs, grad_mine, grad_theirs, gate, up, down, *kept)
    return outs[:4], list(outs[4:])


def ring_next(value):
    size = lax.axis_size("ctx")
    return lax.ppermute(value, "ctx", [(i, (i + 1) % size) for i in range(size)])


def to_chips(value):
    size = lax.axis_size("fsdp")
    return lax.all_to_all(
        value,
        "fsdp",
        split_axis=0,
        concat_axis=0,
        tiled=True,
        axis_index_groups=[list(range(core, size, 2)) for core in range(2)],
    )


def to_core(value):
    size = lax.axis_size("fsdp")
    return lax.ppermute(value, "fsdp", [(i, i ^ 1) for i in range(size)])


def gather_rows(value):
    return lax.all_gather(value, "fsdp", axis=0, tiled=True)


def scatter_rows(value):
    return lax.psum_scatter(value.astype(bfloat), "fsdp", scatter_dimension=0, tiled=True)


def along_ctx(value, shift):
    size = lax.axis_size("ctx")
    return lax.ppermute(value, "ctx", [(i, (i + shift) % size) for i in range(size)])


def column_shares(value, device):
    size = lax.axis_size("ctx")
    count = value.shape[1] // size

    def share(owner):
        return lax.dynamic_slice_in_dim(value, owner % size * count, count, axis=1)

    return [share(device)] + [along_ctx(share(device + k), k) for k in range(1, size)]


def all_columns_of(part, device):
    pieces = [part] + [along_ctx(part, shift) for shift in range(1, lax.axis_size("ctx"))]
    return in_order([piece.astype(single) for piece in pieces], device, 1)


def ctx_spread(part, device):
    pieces = [part] + [along_ctx(part, shift) for shift in range(1, lax.axis_size("ctx"))]
    return in_order([piece.astype(single) for piece in pieces], device)


def sum_ctx(value):
    device = lax.axis_index("ctx")
    return ctx_spread(ctx_total(value, device).astype(bfloat), device)


def in_order(pieces, device, axis=0):
    size = len(pieces)
    count = pieces[0].shape[axis]
    shape = list(pieces[0].shape)
    shape[axis] = size * count
    result = jnp.zeros(shape, pieces[0].dtype)
    for shift, piece in enumerate(pieces):
        owner = (device - shift + size) % size
        result = lax.dynamic_update_slice_in_dim(result, piece, owner * count, axis=axis)
    return result


def together(*values):
    return lax.optimization_barrier(values)


def ctx_total(group, device):
    size = lax.axis_size("ctx")
    count = group.shape[0] // size

    def share(owner):
        return lax.dynamic_slice_in_dim(group, owner % size * count, count, axis=0)

    total = share(device).astype(single)
    for shift in range(1, size):
        total = total + along_ctx(share(device + shift), shift).astype(single)
    return total


def rank_table(route_block, experts, capacity):
    tokens = route_block.shape[0]
    expert_ids = jnp.arange(experts, dtype=jnp.int32)
    named = jnp.any(route_block[:, :, None] == expert_ids[None, None, :], axis=1)
    order = jnp.arange(tokens, dtype=jnp.int32)
    earlier = (order[:, None] > order[None, :]).astype(bfloat)
    rank = matmul(earlier, named.astype(bfloat)).astype(jnp.int32)
    return jnp.where(named & (rank < capacity), rank, -1)


def dispatch(rows):
    mine = to_chips(rows)
    return mine, to_core(mine)


def add_halves(mine, theirs):
    return (mine.astype(single) + to_core(theirs).astype(single)).astype(bfloat)


def local(
    layer_input,
    grad_output,
    routes,
    continuation_prompt,
    block_order,
    query_weight,
    latent_down,
    latent_up,
    output_weight,
    router_weight,
    shared_gate,
    shared_up,
    shared_down,
    attn_gain,
    latent_gain,
    ffn_gain,
    expert_gate,
    expert_up,
    expert_down,
):
    ctx_size = lax.axis_size("ctx")
    fsdp_size = lax.axis_size("fsdp")
    chips = fsdp_size // 2
    device = lax.axis_index("ctx")
    tokens = layer_input.shape[1]
    model_width = layer_input.shape[2]
    experts = router_weight.shape[1]
    group_tok = tokens * ctx_size
    block_len = PROMPT // (2 * ctx_size)
    cont_dev = CONTS * CONT_LEN // ctx_size
    capacity = (5 * tokens * TOP + 4 * experts - 1) // (4 * experts)
    slots = (capacity + 7) // 8 * 8
    score_scale = (NOPE + ROPE) ** (-0.5)
    shard_rows = latent_down.shape[0]
    down_width = latent_down.shape[1]
    hidden_dev = shared_down.shape[0] // ctx_size

    def hidden_columns(weight):
        parts = weight.reshape(shard_rows, fsdp_size, ctx_size, hidden_dev)
        return lax.dynamic_index_in_dim(parts, device, axis=2, keepdims=False).reshape(
            shard_rows, fsdp_size * hidden_dev
        )

    hidden_part = fsdp_size * hidden_dev
    part_down = lax.dynamic_slice_in_dim(shared_down, device * hidden_dev, hidden_dev, axis=0)
    part_shared = jnp.concatenate([hidden_columns(shared_gate), hidden_columns(shared_up)], axis=1)

    own_rows = jnp.arange(tokens, dtype=jnp.int32)
    link_table = continuation_prompt[0]
    own_seq, own_pos, own_link, own_rotary = row_layout(
        device, own_rows, block_order, link_table, block_len, cont_dev
    )
    prompt_rows = 2 * block_len
    first_cont = PROMPTS * prompt_rows
    link = lookup(link_table, (device * cont_dev // CONT_LEN)[None])
    key_pos = (block_order[:, None] * block_len + jnp.arange(block_len, dtype=jnp.int32)).reshape(-1)
    prompt_mask = jnp.where(key_pos[None, :] <= own_pos[:prompt_rows, None], 0.0, masked_score)
    cont_rows = device * cont_dev + jnp.arange(cont_dev, dtype=jnp.int32)
    cont_ids = jnp.arange(CONTS * CONT_LEN, dtype=jnp.int32)
    cont_mask = jnp.where(
        (cont_ids[None, :] // CONT_LEN == cont_rows[:, None] // CONT_LEN)
        & (cont_ids[None, :] <= cont_rows[:, None]),
        0.0,
        masked_score,
    )
    cos_table, sin_table = rotary_tables(own_rotary.astype(single))
    pair_cos = jnp.concatenate([cos_table] * 4, axis=1)
    pair_sin = jnp.concatenate([-sin_table, sin_table] * 2, axis=1)

    def by_sequence(group):
        blocks = group.reshape(ctx_size, tokens, -1)
        parts = [
            blocks[:, p * prompt_rows : (p + 1) * prompt_rows].reshape(PROMPT, -1)
            for p in range(PROMPTS)
        ]
        return jnp.concatenate(parts + [blocks[:, first_cont:].reshape(CONTS * CONT_LEN, -1)])

    def by_block(group):
        parts = [
            group[p * PROMPT : (p + 1) * PROMPT].reshape(ctx_size, prompt_rows, -1)
            for p in range(PROMPTS)
        ]
        last = group[PROMPTS * PROMPT :].reshape(ctx_size, cont_dev, -1)
        return jnp.concatenate(parts + [last], axis=1).reshape(group_tok, -1)

    plane_experts = device * chips + jnp.arange(chips, dtype=jnp.int32)
    chosen_here = plane_experts[:, None] == jnp.arange(experts, dtype=jnp.int32)[None, :]
    def here(table):
        return jnp.sum(jnp.where(chosen_here[:, None, :], table[None], 0), axis=2)

    slot_ids = jnp.arange(slots, dtype=jnp.int32)

    def pick_rows(step, rows):
        return jnp.einsum(
            "jrt,td->jrd", slot_pick[step], rows, preferred_element_type=single
        ).astype(bfloat)

    def put_rows(step, results):
        return jnp.einsum("jrt,jrd->td", slot_pick[step], results, preferred_element_type=single)

    def add_slots(route_block):
        ranks = rank_table(route_block, experts, capacity)
        match = here(ranks)[:, None, :] == slot_ids[None, :, None]
        slot_pick.append(match.astype(bfloat))
        return ranks

    slot_pick = []
    own_ranks = add_slots(routes[0])
    packed = gather_rows(
        jnp.concatenate(
            [
                latent_down,
                router_weight,
                attn_gain[:, None],
                ffn_gain[:, None],
                jnp.pad(latent_gain, (0, shard_rows - latent_gain.shape[0]))[:, None],
            ],
            axis=1,
        )
    )
    route_ring = [along_ctx(routes[0], s) for s in range(1, ctx_size)]
    grad_ring = [grad_output[0]]
    grad_next = ring_next(grad_ring[0])
    grad_mine = [to_chips(pick_rows(0, grad_ring[0]))]
    grad_theirs = []
    packed, query_shard, route_ring, grad_next, grad_mine[0] = together(
        packed, query_weight, route_ring, grad_next, grad_mine[0]
    )

    for route_block in route_ring:
        add_slots(route_block)
    full_down = packed[:, :down_width]
    full_router = packed[:, down_width : down_width + experts]
    gain_attn = packed[:, down_width + experts].astype(single)
    gain_ffn = packed[:, down_width + experts + 1].astype(single)
    gain_latent = (
        packed[:, down_width + experts + 2]
        .reshape(fsdp_size, shard_rows)[:, : latent_gain.shape[0]]
        .reshape(-1)
        .astype(single)
    )
    inputs_full = layer_input[0].astype(single)
    normed, attn_normal, attn_inverse = rms_forward(inputs_full, gain_attn)
    normed_low = normed.astype(bfloat)
    latent_pre = matmul(normed_low, full_down)
    latent, latent_normal, latent_inverse = rms_forward(latent_pre[:, :KV_RANK], gain_latent)
    latent_low = latent.astype(bfloat)
    key_rope_own = rotate(latent_pre[:, KV_RANK:], cos_table, sin_table).astype(bfloat)
    key_own = jnp.concatenate([latent_low, key_rope_own], axis=1)

    def more_grad_rows():
        step = len(grad_mine)
        grad_ring.append(grad_next)
        following = ring_next(grad_next) if step + 1 < ctx_size else grad_next
        theirs = to_core(grad_mine[-1])
        return following, theirs, to_chips(pick_rows(step, grad_ring[step]))

    full_query = gather_rows(query_shard)
    key_pieces = [key_own] + [along_ctx(key_own, s) for s in range(1, ctx_size)]
    grad_next, theirs, mine = more_grad_rows()
    full_query, up_shard, key_pieces, grad_next, theirs, mine = together(
        full_query, latent_up, key_pieces, grad_next, theirs, mine
    )
    grad_theirs.append(theirs)
    grad_mine.append(mine)

    full_up = gather_rows(up_shard)
    query_pre = matmul(normed_low, full_query)
    grad_next, theirs, mine = more_grad_rows()
    full_up, output_shard, query_pre, grad_next, theirs, mine = together(
        full_up, output_weight, query_pre, grad_next, theirs, mine
    )
    grad_theirs.append(theirs)
    grad_mine.append(mine)

    full_output = gather_rows(output_shard)
    key_group = by_sequence(in_order(key_pieces, device))
    latent_group = key_group[:, :KV_RANK]
    rope_pair = jnp.concatenate([key_group[:, KV_RANK:]] * 2, axis=1)
    kv_group = matmul(latent_group, full_up).astype(bfloat)
    rows_here = (prompt_rows, cont_dev)
    attended_low, log_total = attend(
        rows_here,
        score_scale,
        link,
        query_pre,
        pair_cos,
        pair_sin,
        kv_group,
        rope_pair,
        prompt_mask,
        cont_mask,
    )
    while len(grad_mine) < ctx_size:
        grad_next, theirs, mine = more_grad_rows()
        grad_theirs.append(theirs)
        grad_mine.append(mine)
    grad_group = jnp.concatenate(grad_ring)
    (
        full_output,
        shared_shard,
        down_shard,
        attended_low,
        grad_mine,
        grad_theirs,
        grad_group,
    ) = together(
        full_output,
        part_shared,
        part_down,
        attended_low,
        grad_mine,
        grad_theirs,
        grad_group,
    )
    grad_theirs.append(to_core(grad_mine[-1]))

    part_down = gather_rows(down_shard)
    hidden = inputs_full + matmul(attended_low, full_output)
    ffn_in, ffn_normal, ffn_inverse = rms_forward(hidden, gain_ffn)
    ffn_low = ffn_in.astype(bfloat)
    logits = matmul(ffn_low, full_router)
    router_exps = jnp.exp(logits - jnp.max(logits, axis=1, keepdims=True))
    router = router_exps / jnp.sum(router_exps, axis=1, keepdims=True)
    route_match = jnp.any(
        routes[0][:, :, None] == jnp.arange(experts, dtype=jnp.int32)[None, None, :], axis=1
    )
    chosen_total = jnp.sum(jnp.where(route_match, router, 0.0), axis=1, keepdims=True)
    gates = jnp.where(route_match, router, 0.0) / chosen_total
    pair_weight = jnp.where(own_ranks >= 0, gates, 0.0)

    weight_high = pair_weight.astype(bfloat)
    weight_low = (pair_weight - weight_high.astype(single)).astype(bfloat)
    ffn_wide = jnp.concatenate(
        [
            ffn_low,
            weight_high,
            weight_low,
            jnp.zeros((tokens, EXTRA - 2 * experts), bfloat),
        ],
        axis=1,
    )
    own_expert = (device * chips + lax.axis_index("fsdp") // 2)[None].astype(jnp.int32)
    kept = []
    out_sends = []

    def flat(rows):
        return rows.reshape(-1, rows.shape[-1])

    def expert_step(step, mine, theirs):
        results, kept[:] = expert_call(
            step,
            ctx_size,
            experts,
            own_expert,
            flat(mine),
            flat(theirs),
            flat(grad_mine[step]),
            flat(grad_theirs[step]),
            expert_gate[0].T,
            expert_up[0].T,
            expert_down[0],
            kept,
        )
        return [rows.reshape(chips, slots, -1) for rows in results]

    def shared_step(rows, grad_act):
        gate_pre = matmul(rows, part_gate)
        up_pre = matmul(rows, part_up)
        act = (jax.nn.silu(gate_pre) * up_pre).astype(bfloat)
        grad_gate, grad_up = silu_grads(grad_act, gate_pre, up_pre)
        back = jnp.einsum("tf,df->td", grad_gate, part_gate, preferred_element_type=single)
        back = back + jnp.einsum("tf,df->td", grad_up, part_up, preferred_element_type=single)
        return act, grad_gate, grad_up, back

    def shared_grads():
        group = jnp.concatenate(groups)
        act, grad_gate, grad_up = [
            jnp.concatenate([part[i] for part in shared]) for i in range(3)
        ]
        pieces = [
            jnp.einsum("ta,tb->ab", left, right, preferred_element_type=single).astype(bfloat)
            for left, right in ((group, grad_gate), (group, grad_up), (act, grad_group))
        ]
        return pieces

    last = ctx_size - 1
    ffn_ring = [ffn_wide]
    attended_ring = [attended_low]
    mines, theirs, backs, added, returned, out_added, out_steps = ({} for _ in range(7))
    shared, groups = [], []
    together_blocks = 4
    moving = None

    def of_block(which, step):
        first = step % together_blocks * tokens
        return shared[step // together_blocks][which][first : first + tokens]

    def block_part(step):
        part = put_rows(step, returned[step])
        return part + jnp.pad(of_block(3, step), ((0, 0), (0, EXTRA)))

    def hop(step):
        part = block_part(step)
        if moving is not None:
            part = part + moving.astype(single)
        return ring_next(part.astype(bfloat))

    for tick in range(ctx_size + 5):
        sent = {}
        if tick <= last:
            sent["mine"] = to_chips(pick_rows(tick, ffn_ring[tick]))
        if tick < last:
            sent["ring"] = ring_next(ffn_ring[tick])
        if 0 <= tick - 1 <= last:
            sent["theirs"] = to_core(mines[tick - 1])
        if 0 <= tick - 2 <= last:
            sent["back"] = expert_step(tick - 2, mines[tick - 2], theirs[tick - 2])
        if 0 <= tick - 3 <= last:
            sent["added"] = add_halves(*backs[tick - 3])
        if 0 <= tick - 4 <= last:
            sent["returned"] = to_chips(added[tick - 4])
        first = tick - 4
        if 0 <= first <= last and first % together_blocks == 0:
            sent["group"] = jnp.concatenate(
                [
                    block[:, :model_width]
                    for block in ffn_ring[first : first + together_blocks]
                ]
            )
        first = tick - 5
        if 0 <= first <= last and first % together_blocks == 0:
            rows = groups[-1].shape[0]
            shared.append(
                shared_step(groups[-1], grad_act[first * tokens : first * tokens + rows])
            )
            sent["shared"] = shared[-1]
        if 1 <= tick - 5 <= last:
            sent["moving"] = hop(tick - 5)
        if tick == 0:
            sent["grads"] = grad_theirs[-1]
        if tick == 0:
            sent["shard"] = shared_shard
        if tick == 3:
            sent["weights"] = part_shared
        if tick == 1:
            sent["down"] = part_down
            sent["grad_act"] = jnp.einsum(
                "td,fd->tf", grad_group, part_down, preferred_element_type=single
            )
        if tick == ctx_size + 2:
            sent["shared_all"] = (shared, groups, grad_group)
        if tick == ctx_size + 3:
            sent["shared_grads"] = shared_grads()
            sent["out"] = add_halves(*out_sends[1])
        if tick == ctx_size + 4:
            sent["shared_packed"] = jnp.concatenate(
                shared_pieces[:2] + [shared_pieces[2].reshape(model_width, hidden_part)], axis=1
            )
            sent["out_step"] = to_chips(out_added[1])
        if last <= tick < 2 * last:
            sent["attended"] = ring_next(attended_ring[-1])
        if tick == ctx_size + 4:
            sent["out"] = add_halves(*out_sends[2])
        names = sorted(sent)
        sent = dict(zip(names, together(*(sent[name] for name in names))))
        if "mine" in sent:
            mines[tick] = sent["mine"]
        if "ring" in sent:
            ffn_ring.append(sent["ring"])
        if "theirs" in sent:
            theirs[tick - 1] = sent["theirs"]
        if "back" in sent:
            backs[tick - 2] = sent["back"][:2]
            out_sends.append(sent["back"][2:])
        if "added" in sent:
            added[tick - 3] = sent["added"]
        if "returned" in sent:
            returned[tick - 4] = sent["returned"]
        if "group" in sent:
            groups.append(sent["group"])
        if "shared" in sent:
            shared[-1] = sent["shared"]
        if "shared_grads" in sent:
            shared_pieces = list(sent["shared_grads"])
        if "shared_all" in sent:
            shared, groups, grad_group = sent["shared_all"]
        if "attended" in sent:
            attended_ring.append(sent["attended"])
        if "out" in sent:
            out_added[tick - ctx_size - 2] = sent["out"]
        if "out_step" in sent:
            out_steps[1] = sent["out_step"]
        moving = sent.get("moving", moving)
        if tick == 0:
            grad_theirs[-1] = sent["grads"]
        if "shard" in sent:
            part_shared = gather_rows(sent["shard"])
        if "down" in sent:
            part_down = sent["down"]
            grad_act = sent["grad_act"]
        if "weights" in sent:
            part_gate = sent["weights"][:, :hidden_part]
            part_up = sent["weights"][:, hidden_part:]

    while len(attended_ring) < ctx_size:
        attended_ring.append(ring_next(attended_ring[-1]))
    shared_part = scatter_rows(sent["shared_packed"])
    first_part = block_part(0)

    def next_out(step):
        ahead = (step + 1) % ctx_size
        return to_chips(out_added[step]), add_halves(*out_sends[ahead]) if step else out_added[step]

    grad_wide = moving.astype(single) + first_part
    grad_ffn = grad_wide[:, :model_width]
    grad_gate_pair = jnp.where(
        own_ranks >= 0, grad_wide[:, model_width : model_width + experts], 0.0
    )

    grad_low = grad_output[0]
    grad_top = grad_low.astype(single)
    grad_chosen = (
        grad_gate_pair - jnp.sum(grad_gate_pair * gates, axis=1, keepdims=True)
    ) / chosen_total
    grad_router = jnp.where(route_match, grad_chosen, 0.0)
    grad_logits = (
        router * (grad_router - jnp.sum(router * grad_router, axis=1, keepdims=True))
    ).astype(bfloat)
    grad_w_router = jnp.einsum("td,te->de", ffn_low, grad_logits, preferred_element_type=single)
    grad_ffn = grad_ffn + jnp.einsum(
        "te,de->td", grad_logits, full_router, preferred_element_type=single
    )
    grad_hidden_norm, grad_gain_ffn = rms_backward(grad_ffn, ffn_normal, ffn_inverse, gain_ffn)
    grad_hidden = grad_top + grad_hidden_norm
    grad_attn_low = grad_hidden.astype(bfloat)

    def out_hop(step, moving):
        part = put_rows(step, out_steps[step]) + matmul(of_block(0, step), part_down)
        if moving is not None:
            part = part + moving.astype(single)
        return ring_next(part.astype(bfloat))

    grad_attended = jnp.einsum(
        "td,vd->tv", grad_attn_low, full_output, preferred_element_type=single
    ).astype(bfloat)
    out_steps[2] = to_chips(out_added[2])
    out_moving = out_hop(2, out_hop(1, None))
    att_shares = column_shares(grad_attn_low, device)
    grad_attended, out_sends = together(grad_attended, out_sends)

    def weight_grad(left, right):
        return jnp.einsum("ra,rb->ab", left, right, preferred_element_type=single)

    grad_w_output = weight_grad(jnp.concatenate(attended_ring), jnp.concatenate(att_shares))

    out_added[3] = add_halves(*out_sends[3])

    log_rows = log_total[:, :HEADS].T.reshape(HEADS // 2, 2, tokens)
    grad_nope, grad_rope, grad_key_part, grad_value_part, rope_pair_grad = attend_back(
        rows_here,
        score_scale,
        link,
        query_pre,
        pair_cos,
        pair_sin,
        kv_group,
        rope_pair,
        prompt_mask.T,
        cont_mask.T,
        log_rows,
        grad_attended,
    )
    (
        grad_nope,
        grad_rope,
        grad_key_part,
        grad_value_part,
        rope_pair_grad,
        out_steps[2],
        out_added[3],
        out_moving,
        shared_part,
        grad_w_output,
    ) = together(
        grad_nope,
        grad_rope,
        grad_key_part,
        grad_value_part,
        rope_pair_grad,
        out_steps[2],
        out_added[3],
        out_moving,
        shared_part,
        grad_w_output,
    )
    out_next = next_out(3)
    output_part = scatter_rows(grad_w_output)
    grad_key_rope = rope_pair_grad[:, :ROPE] + rope_pair_grad[:, ROPE:]
    keys_width = HEADS * NOPE
    grad_latent_group = jnp.einsum(
        "tk,ck->tc", grad_key_part, full_up[:, :keys_width], preferred_element_type=single
    ) + jnp.einsum(
        "tk,ck->tc", grad_value_part, full_up[:, keys_width:], preferred_element_type=single
    )
    grad_query_pre = jnp.concatenate([grad_nope, grad_rope], axis=1)
    grad_w_query = weight_grad(normed_low, grad_query_pre)
    grad_keys_own = ctx_total(
        by_block(jnp.concatenate([grad_latent_group, grad_key_rope], axis=1).astype(bfloat)), device
    )
    grad_keys_own, output_part, grad_w_query, out_next, out_moving = together(
        grad_keys_own, output_part, grad_w_query, out_next, out_moving
    )
    out_steps[3], out_added[4 % ctx_size] = out_next
    for step in range(3, ctx_size):
        if step > 3:
            out_steps[step], out_added[(step + 1) % ctx_size] = next_out(step)
        out_moving = out_hop(step, out_moving)
    out_steps[0] = to_chips(out_added[0])
    query_part = scatter_rows(grad_w_query)
    shared_ring = [shared_part, ring_next(shared_part)]
    shared_ring.append(ring_next(shared_ring[-1]))
    sum_output = all_columns_of(output_part, device)
    grad_w_up = jnp.concatenate(
        [
            weight_grad(latent_group, part).astype(bfloat).reshape(model_width, -1)
            for part in (grad_key_part, grad_value_part)
        ],
        axis=1,
    )
    grad_latent = grad_keys_own[:, :KV_RANK]
    grad_rope_own = grad_keys_own[:, KV_RANK:]
    grad_latent_in, grad_gain_latent = rms_backward(
        grad_latent, latent_normal, latent_inverse, gain_latent
    )
    grad_rope_in = rotate(grad_rope_own, cos_table, -sin_table)
    grad_latent_pre = jnp.concatenate([grad_latent_in, grad_rope_in], axis=1).astype(bfloat)
    grad_w_down = jnp.einsum(
        "td,tk->dk",
        normed_low,
        jnp.pad(grad_latent_pre, ((0, 0), (0, -down_width % 128))),
        preferred_element_type=single,
    )
    grad_normed = jnp.einsum(
        "tq,dq->td", grad_query_pre, full_query, preferred_element_type=single
    ) + jnp.einsum("tk,dk->td", grad_latent_pre, full_down, preferred_element_type=single)
    grad_x_norm, grad_gain_attn = rms_backward(grad_normed, attn_normal, attn_inverse, gain_attn)
    grad_input = (grad_hidden + grad_x_norm).astype(bfloat)

    padded_latent = jnp.pad(
        grad_gain_latent.reshape(fsdp_size, -1),
        ((0, 0), (0, shard_rows - latent_gain.shape[0])),
    ).reshape(-1)
    up_width = grad_w_up.shape[1]
    small = jnp.concatenate(
        [
            grad_w_router,
            grad_gain_attn[:, None],
            grad_gain_ffn[:, None],
            padded_latent[:, None],
        ],
        axis=1,
    ).astype(bfloat)
    packed_grads = jnp.concatenate(
        [
            grad_w_up,
            grad_w_down.astype(bfloat),
            jnp.pad(small, ((0, 0), (0, -small.shape[1] % 128))),
        ],
        axis=1,
    )
    (
        query_part,
        packed_grads,
        shared_ring,
        kept,
        out_moving,
        out_steps[0],
        sum_output,
    ) = together(
        query_part, packed_grads, shared_ring, kept, out_moving, out_steps[0], sum_output
    )
    packed_part = scatter_rows(with_layout_constraint(packed_grads, by_rows))
    all_rows, all_grads, all_act, all_gate, all_up = kept
    grad_piece_down = weight_grad(all_act, all_grads)
    grad_piece_gate = weight_grad(all_rows, all_gate)
    sum_query = sum_ctx(query_part)
    packed_part, sum_query, grad_piece_down, grad_piece_gate, kept = together(
        packed_part, sum_query, grad_piece_down, grad_piece_gate, kept
    )
    all_rows, all_grads, all_act, all_gate, all_up = kept
    grad_piece_up = weight_grad(all_rows, all_up)
    while len(shared_ring) < ctx_size:
        shared_ring.append(ring_next(shared_ring[-1]))
    first_out = put_rows(0, out_steps[0]) + matmul(of_block(0, 0), part_down)
    layer_output = (hidden + out_moving.astype(single) + first_out).astype(bfloat)
    sum_packed = with_layout_constraint(
        sum_ctx(with_layout_constraint(packed_part, by_rows)), by_rows
    )
    sum_up = jnp.concatenate(
        [
            part.reshape(latent_up.shape[0], -1)
            for part in (sum_packed[:, : up_width // 2], sum_packed[:, up_width // 2 : up_width])
        ],
        axis=1,
    )
    sum_down = sum_packed[:, up_width : up_width + down_width]
    sum_small = sum_packed[:, up_width + grad_w_down.shape[1] :]
    sum_router = sum_small[:, :experts]
    sum_gain_attn = sum_small[:, experts]
    sum_gain_ffn = sum_small[:, experts + 1]
    sum_gain_latent = sum_small[: latent_gain.shape[0], experts + 2]

    shared_blocks = in_order([piece[None] for piece in shared_ring], device)

    def all_columns(blocks):
        blocks = blocks.reshape(ctx_size, shard_rows, fsdp_size, hidden_dev)
        return blocks.transpose(1, 2, 0, 3).reshape(shard_rows, -1).astype(single)

    sum_sh_gate = all_columns(shared_blocks[:, :, :hidden_part])
    sum_sh_up = all_columns(shared_blocks[:, :, hidden_part : 2 * hidden_part])
    sum_sh_down = shared_blocks[:, :, 2 * hidden_part :].reshape(shared_down.shape).astype(single)
    return (
        layer_output[None],
        grad_input[None],
        sum_query,
        sum_down,
        sum_up,
        sum_output,
        sum_router,
        sum_sh_gate,
        sum_sh_up,
        sum_sh_down,
        sum_gain_attn,
        sum_gain_latent,
        sum_gain_ffn,
        grad_piece_gate[None],
        grad_piece_up[None],
        grad_piece_down[None],
    )


def solution(mesh):
    in_specs = (
        P("fsdp", "ctx", None),
        P("fsdp", "ctx", None),
        P("fsdp", "ctx", None),
        P("fsdp", None),
        P(),
        P("fsdp", None),
        P("fsdp", None),
        P("fsdp", None),
        P("fsdp", None),
        P("fsdp", None),
        P("fsdp", None),
        P("fsdp", None),
        P("fsdp", None),
        P("fsdp"),
        P("fsdp"),
        P("fsdp"),
        P(("ctx", "fsdp"), None, None),
        P(("ctx", "fsdp"), None, None),
        P(("ctx", "fsdp"), None, None),
    )
    out_specs = (
        P("fsdp", "ctx", None),
        P("fsdp", "ctx", None),
        P("fsdp", None),
        P("fsdp", None),
        P("fsdp", None),
        P("fsdp", None),
        P("fsdp", None),
        P("fsdp", None),
        P("fsdp", None),
        P("fsdp", None),
        P("fsdp"),
        P("fsdp"),
        P("fsdp"),
        P(("ctx", "fsdp"), None, None),
        P(("ctx", "fsdp"), None, None),
        P(("ctx", "fsdp"), None, None),
    )
    return jax.shard_map(local, mesh=mesh, in_specs=in_specs, out_specs=out_specs, check_vma=False)
```

```python
import functools

import jax
import jax.numpy as jnp
from jax import lax
from jax.experimental import pallas as pl
from jax.experimental.layout import Layout, with_layout_constraint
from jax.experimental.pallas import tpu as pltpu
from jax.sharding import PartitionSpec as P

HEADS = 16
NOPE = 128
ROPE = 64
VDIM = 128
KV_RANK = 512
TOP = 6
PROMPT = 512
PROMPTS = 2
CONT_LEN = 128
CONTS = 2


epsilon = 1e-06
masked_score = -1e30
bfloat = jnp.bfloat16
single = jnp.float32


EXTRA = 128
by_rows = Layout(major_to_minor=(0, 1))


def matmul(left, right):
    return jnp.dot(left, right, preferred_element_type=single)


def rms_forward(values, gain):
    inverse = lax.rsqrt(jnp.mean(values * values, axis=-1, keepdims=True) + epsilon)
    normal_part = values * inverse
    return (normal_part * gain, normal_part, inverse)


def rms_backward(grad_out, normal_part, inverse, gain):
    grad_normal = grad_out * gain
    grad_gain = jnp.sum(grad_out * normal_part, axis=0)
    grad_in = inverse * (
        grad_normal - normal_part * jnp.mean(grad_normal * normal_part, axis=-1, keepdims=True)
    )
    return (grad_in, grad_gain)


def rotary_tables(positions):
    exponent = jnp.arange(ROPE // 2, dtype=jnp.float32) * (2.0 / ROPE)
    frequency = jnp.exp(-jnp.log(10000.0) * exponent)
    angles = positions[:, None] * frequency[None, :]
    return (jnp.cos(angles), jnp.sin(angles))


def rotate(values, cos_table, sin_table):
    half_width = values.shape[-1] // 2
    first_half = values[..., :half_width]
    second = values[..., half_width:]
    return jnp.concatenate(
        [first_half * cos_table - second * sin_table, second * cos_table + first_half * sin_table],
        axis=-1,
    )


def lookup(table_values, wanted):
    matches = wanted[:, None] == jnp.arange(table_values.shape[0], dtype=jnp.int32)[None, :]
    return jnp.sum(jnp.where(matches, table_values[None, :], 0), axis=1)


def row_layout(device, local_row, block_order, link_table, block_len, cont_dev):
    prompt_rows = PROMPTS * 2 * block_len
    in_prompt = local_row < prompt_rows
    prompt_id = local_row // (2 * block_len)
    half_slot = local_row // block_len % 2
    prompt_pos = lookup(block_order, 2 * device + half_slot) * block_len + local_row % block_len
    cont_index = device * cont_dev + jnp.maximum(local_row - prompt_rows, 0)
    cont_id = jnp.minimum(cont_index // CONT_LEN, CONTS - 1)
    cont_pos = cont_index % CONT_LEN
    sequence = jnp.where(in_prompt, prompt_id, PROMPTS + cont_id)
    position = jnp.where(in_prompt, prompt_pos, cont_pos)
    linked = jnp.where(in_prompt, -1, lookup(link_table, cont_id))
    rotary = jnp.where(in_prompt, prompt_pos, PROMPT + cont_pos)
    return (sequence, position, linked, rotary)


def silu_grads(grad_act, gate_pre, up_pre):
    sigmoid_gate = jax.nn.sigmoid(gate_pre)
    grad_gate = (grad_act * up_pre * sigmoid_gate * (1.0 + gate_pre * (1.0 - sigmoid_gate))).astype(
        bfloat
    )
    grad_up = (grad_act * gate_pre * sigmoid_gate).astype(bfloat)
    return (grad_gate, grad_up)


NT = (((1,), (1,)), ((), ()))
TN = (((0,), (0,)), ((), ()))


def product(left, right, dims):
    return lax.dot_general(left, right, dims, preferred_element_type=single)


def half_swap(values):
    width = values.shape[1]
    lane = lax.broadcasted_iota(jnp.int32, values.shape, 1)
    ahead = pltpu.roll(values, width - ROPE // 2, 1)
    behind = pltpu.roll(values, ROPE // 2, 1)
    return jnp.where(lane % ROPE < ROPE // 2, ahead, behind)


def head_query(nope, rotated, which):
    lane = lax.broadcasted_iota(jnp.int32, rotated.shape, 1)
    kept = jnp.where((lane >= ROPE) == (which == 1), rotated, 0.0)
    return jnp.concatenate(
        [nope[:, which * NOPE : (which + 1) * NOPE].astype(bfloat), kept.astype(bfloat)], axis=1
    )


def attend_kernel(
    rows, scale, link, nope, rope, cos, sin, keys, values, key_rope, prompt_mask, cont_mask, out, lse
):
    pair = pl.program_id(0)
    prompt_rows, cont_rows = rows
    first = prompt_rows * PROMPTS
    linked = pl.multiple_of(link[0] * PROMPT, PROMPT)
    rotated = rope[...] * cos[...] + half_swap(rope[...]) * sin[...]
    nopes = nope[...]

    @pl.when(pair == 0)
    def _():
        lse[...] = jnp.zeros_like(lse)

    def key_part(start, count, which):
        return jnp.concatenate(
            [keys[pl.ds(start, count), which * NOPE : (which + 1) * NOPE], key_rope[pl.ds(start, count), :]],
            axis=1,
        )

    def value_part(start, count, which):
        return values[pl.ds(start, count), which * VDIM : (which + 1) * VDIM]

    for which in range(2):
        query = head_query(nopes, rotated, which)
        outs = []
        logs = []
        for prompt in range(PROMPTS):
            part = query[prompt * prompt_rows : (prompt + 1) * prompt_rows]
            scores = product(part, key_part(prompt * PROMPT, PROMPT, which), NT) * scale
            scores = scores + prompt_mask[...]
            top = jnp.max(scores, axis=1, keepdims=True)
            exps = jnp.exp(scores - top)
            total = jnp.sum(exps, axis=1, keepdims=True)
            probs = (exps / total).astype(bfloat)
            outs.append(matmul(probs, value_part(prompt * PROMPT, PROMPT, which)))
            logs.append(top + jnp.log(total))
        part = query[first:]
        cont_keys = CONTS * CONT_LEN
        scores = product(part, key_part(linked, PROMPT, which), NT) * scale
        near = product(part, key_part(PROMPTS * PROMPT, cont_keys, which), NT) * scale
        near = near + cont_mask[...]
        top = jnp.maximum(
            jnp.max(scores, axis=1, keepdims=True), jnp.max(near, axis=1, keepdims=True)
        )
        exps = jnp.exp(scores - top)
        near_exps = jnp.exp(near - top)
        total = jnp.sum(exps, axis=1, keepdims=True) + jnp.sum(near_exps, axis=1, keepdims=True)
        outs.append(
            matmul((exps / total).astype(bfloat), value_part(linked, PROMPT, which))
            + matmul(
                (near_exps / total).astype(bfloat), value_part(PROMPTS * PROMPT, cont_keys, which)
            )
        )
        logs.append(top + jnp.log(total))
        out[:, which * VDIM : (which + 1) * VDIM] = jnp.concatenate(outs, axis=0).astype(bfloat)
        lane = lax.broadcasted_iota(jnp.int32, lse.shape, 1)
        lse[...] = jnp.where(lane == 2 * pair + which, jnp.concatenate(logs, axis=0), lse[...])


def attend_back_kernel(
    rows,
    scale,
    link,
    nope,
    rope,
    cos,
    sin,
    keys,
    values,
    key_rope,
    prompt_mask,
    cont_mask,
    lse,
    grad,
    grad_nope,
    grad_rope,
    grad_keys,
    grad_values,
    grad_key_rope,
    key_sum,
    value_sum,
    rope_sum,
):
    pair = pl.program_id(0)
    prompt_rows, cont_rows = rows
    first = prompt_rows * PROMPTS
    linked = pl.multiple_of(link[0] * PROMPT, PROMPT)
    cont_start = PROMPTS * PROMPT
    cont_keys = CONTS * CONT_LEN
    rotated = rope[...] * cos[...] + half_swap(rope[...]) * sin[...]
    nopes = nope[...]

    @pl.when(pair == 0)
    def _():
        rope_sum[...] = jnp.zeros_like(rope_sum)

    rope_grads = []
    for which in range(2):
        query = head_query(nopes, rotated, which)
        log_row = lse[which : which + 1, :]
        query_grads = []

        def one(lo, hi, start, count, mask):
            part = query[lo:hi]
            key_cat = jnp.concatenate(
                [
                    keys[pl.ds(start, count), which * NOPE : (which + 1) * NOPE],
                    key_rope[pl.ds(start, count), :],
                ],
                axis=1,
            )
            value = values[pl.ds(start, count), which * VDIM : (which + 1) * VDIM]
            grad_part = grad[lo:hi, which * VDIM : (which + 1) * VDIM]
            scores = product(key_cat, part, NT) * scale
            if mask is not None:
                scores = scores + mask
            probs = jnp.exp(scores - log_row[:, lo:hi])
            grad_probs = product(value, grad_part, NT)
            return part, key_cat, grad_part, probs, grad_probs

        def finish(parts, delta):
            part, key_cat, grad_part, probs, grad_probs = parts
            grad_scores = (probs * (grad_probs - delta)).astype(bfloat)
            query_grad = product(grad_scores, key_cat, TN)
            key_grad = matmul(grad_scores, part) * scale
            value_grad = matmul(probs.astype(bfloat), grad_part)
            return query_grad, key_grad, value_grad

        def delta_of(parts):
            return jnp.sum(parts[3] * parts[4], axis=0, keepdims=True)

        for prompt in range(PROMPTS):
            lo, hi = prompt * prompt_rows, (prompt + 1) * prompt_rows
            start = prompt * PROMPT
            parts = one(lo, hi, start, PROMPT, prompt_mask[...])
            query_grad, key_grad, value_grad = finish(parts, delta_of(parts))
            query_grads.append(query_grad)
            key_sum[start : start + PROMPT, :] = key_grad[:, :NOPE]
            value_sum[start : start + PROMPT, :] = value_grad
            rope_sum[start : start + PROMPT, :] += key_grad[:, NOPE:]
        far = one(first, first + cont_rows, linked, PROMPT, None)
        near = one(first, first + cont_rows, cont_start, cont_keys, cont_mask[...])
        delta = delta_of(far) + delta_of(near)
        far_query, far_key, far_value = finish(far, delta)
        near_query, near_key, near_value = finish(near, delta)
        query_grads.append(far_query + near_query)
        span = pl.ds(linked, PROMPT)
        key_sum[span, :] += far_key[:, :NOPE]
        value_sum[span, :] += far_value
        rope_sum[span, :] += far_key[:, NOPE:]
        key_sum[cont_start:, :] = near_key[:, :NOPE]
        value_sum[cont_start:, :] = near_value
        rope_sum[cont_start:, :] += near_key[:, NOPE:]
        query_grad = jnp.concatenate(query_grads, axis=0) * scale
        grad_nope[:, which * NOPE : (which + 1) * NOPE] = query_grad[:, :NOPE].astype(bfloat)
        rope_grads.append(query_grad[:, NOPE:])
        grad_keys[:, which * NOPE : (which + 1) * NOPE] = key_sum[...].astype(bfloat)
        grad_values[:, which * VDIM : (which + 1) * VDIM] = value_sum[...].astype(bfloat)
    lane = lax.broadcasted_iota(jnp.int32, rope_grads[0].shape, 1)
    both = jnp.where(lane < ROPE, rope_grads[0], rope_grads[1])
    grad_rope[...] = (both * cos[...] - half_swap(both) * sin[...]).astype(bfloat)
    grad_key_rope[...] = rope_sum[...]


def whole(shape):
    return pl.BlockSpec(shape, lambda pair: (0,) * len(shape))


def pair_specs(tokens, key_rows, prompt_mask, cont_mask):
    nope_blocks = HEADS * NOPE // (2 * ROPE)
    return [
        pl.BlockSpec(memory_space=pltpu.SMEM),
        pl.BlockSpec((tokens, 2 * NOPE), lambda pair: (0, pair)),
        pl.BlockSpec((tokens, 2 * ROPE), lambda pair: (0, nope_blocks + pair)),
        whole((tokens, 2 * ROPE)),
        whole((tokens, 2 * ROPE)),
        pl.BlockSpec((key_rows, 2 * NOPE), lambda pair: (0, pair)),
        pl.BlockSpec((key_rows, 2 * VDIM), lambda pair: (0, HEADS // 2 + pair)),
        whole((key_rows, 2 * ROPE)),
        whole(prompt_mask),
        whole(cont_mask),
    ]


def attend(rows, scale, link, query_pre, cos, sin, kv, key_rope, prompt_mask, cont_mask):
    tokens = query_pre.shape[0]
    key_rows = kv.shape[0]
    work = 2 * (rows[0] * PROMPT * PROMPTS + rows[1] * (PROMPT + CONTS * CONT_LEN)) * HEADS
    return pl.pallas_call(
        functools.partial(attend_kernel, rows, scale),
        grid=(HEADS // 2,),
        in_specs=pair_specs(tokens, key_rows, prompt_mask.shape, cont_mask.shape),
        out_specs=[
            pl.BlockSpec((tokens, 2 * VDIM), lambda pair: (0, pair)),
            whole((tokens, 128)),
        ],
        out_shape=[
            jax.ShapeDtypeStruct((tokens, HEADS * VDIM), bfloat),
            jax.ShapeDtypeStruct((tokens, 128), single),
        ],
        compiler_params=pltpu.CompilerParams(vmem_limit_bytes=40 * 2**20),
        cost_estimate=pl.CostEstimate(
            flops=work * 384, bytes_accessed=2 * kv.size + 6 * query_pre.size, transcendentals=work // 2
        ),
    )(link, query_pre, query_pre, cos, sin, kv, kv, key_rope, prompt_mask, cont_mask)


def attend_back(
    rows, scale, link, query_pre, cos, sin, kv, key_rope, prompt_mask, cont_mask, lse, grad
):
    tokens = query_pre.shape[0]
    key_rows = kv.shape[0]
    work = 2 * (rows[0] * PROMPT * PROMPTS + rows[1] * (PROMPT + CONTS * CONT_LEN)) * HEADS
    return pl.pallas_call(
        functools.partial(attend_back_kernel, rows, scale),
        grid=(HEADS // 2,),
        in_specs=pair_specs(tokens, key_rows, prompt_mask.shape, cont_mask.shape)
        + [
            pl.BlockSpec((None, 2, tokens), lambda pair: (pair, 0, 0)),
            pl.BlockSpec((tokens, 2 * VDIM), lambda pair: (0, pair)),
        ],
        out_specs=[
            pl.BlockSpec((tokens, 2 * NOPE), lambda pair: (0, pair)),
            pl.BlockSpec((tokens, 2 * ROPE), lambda pair: (0, pair)),
            pl.BlockSpec((key_rows, 2 * NOPE), lambda pair: (0, pair)),
            pl.BlockSpec((key_rows, 2 * VDIM), lambda pair: (0, pair)),
            whole((key_rows, 2 * ROPE)),
        ],
        out_shape=[
            jax.ShapeDtypeStruct((tokens, HEADS * NOPE), bfloat),
            jax.ShapeDtypeStruct((tokens, HEADS * ROPE), bfloat),
            jax.ShapeDtypeStruct((key_rows, HEADS * NOPE), bfloat),
            jax.ShapeDtypeStruct((key_rows, HEADS * VDIM), bfloat),
            jax.ShapeDtypeStruct((key_rows, 2 * ROPE), single),
        ],
        scratch_shapes=[
            pltpu.VMEM((key_rows, NOPE), single),
            pltpu.VMEM((key_rows, VDIM), single),
            pltpu.VMEM((key_rows, 2 * ROPE), single),
        ],
        compiler_params=pltpu.CompilerParams(vmem_limit_bytes=48 * 2**20),
        cost_estimate=pl.CostEstimate(
            flops=work * 1152, bytes_accessed=4 * kv.size + 10 * query_pre.size, transcendentals=work // 2
        ),
    )(link, query_pre, query_pre, cos, sin, kv, kv, key_rope, prompt_mask, cont_mask, lse, grad)


def expert_kernel(
    first_row,
    experts,
    expert,
    mine,
    theirs,
    grad_mine,
    grad_theirs,
    gate,
    up,
    down,
    *refs,
):
    back_mine, back_theirs, out_mine, out_theirs = refs[-21:-17]
    all_rows, all_grads, all_act, all_gate, all_up = refs[-17:-12]
    rows, grads, gate_w, up_w, down_w, act, grad_gate, grad_up, back, out = refs[-12:-2]
    in_sems, out_sems = refs[-2:]
    count = mine.shape[0]
    hidden, width = gate.shape
    lane = lax.broadcasted_iota(jnp.int32, (count, EXTRA), 1)
    here = lane == expert[0]
    loads = [
        pltpu.make_async_copy(source, target, in_sems.at[i])
        for i, (source, target) in enumerate(
            [
                (theirs, rows.at[1]),
                (gate, gate_w),
                (up, up_w),
                (grad_theirs, grads.at[1]),
                (down, down_w),
                (mine, rows.at[0]),
                (grad_mine, grads.at[0]),
            ]
        )
    ]
    for load in loads:
        load.start()

    def store(half, which):
        span = pl.ds(first_row + half * count, count)
        pairs = [
            (rows.at[half, :, pl.ds(0, width)], all_rows.at[span, :]),
            (grads.at[half], all_grads.at[span, :]),
            (act.at[half], all_act.at[span, :]),
            (grad_gate.at[half], all_gate.at[span, :]),
            (grad_up.at[half], all_up.at[span, :]),
            (back.at[half], (back_mine, back_theirs)[half]),
            (out.at[half], (out_mine, out_theirs)[half]),
        ]
        source, target = pairs[which]
        return pltpu.make_async_copy(source, target, out_sems.at[half, which])

    def one_half(turn, carry):
        half = 1 - turn

        def await_loads(first, second):
            for when, which in enumerate((first, second)):
                if which:

                    @pl.when(turn == when)
                    def _(which=which):
                        for i in which:
                            loads[i].wait()

        def start_stores(which):
            for when in range(2):

                @pl.when(turn == when)
                def _(when=when):
                    for i in which:
                        store(1 - when, i).start()

        await_loads((0, 1), (5,))
        start_stores((0,))
        extra = rows[half, :, width:].astype(single)
        slot_weight = jnp.sum(
            jnp.where(here | (lane == expert[0] + experts), extra, 0.0), axis=1, keepdims=True
        )
        total = jnp.zeros((count, 1), single)
        for lo in range(0, hidden, 256):
            hi = min(lo + 256, hidden)
            gate_pre = product(rows[half, :, :width], gate_w[lo:hi, :], NT)
            if lo == 0:
                await_loads((2,), ())
            up_pre = product(rows[half, :, :width], up_w[lo:hi, :], NT)
            if lo == 0:
                await_loads((3, 4), (6,))
                start_stores((1,))
            grad_act = product(grads[half], down_w[lo:hi, :], NT)
            sigmoid = 1.0 / (1.0 + jnp.exp(-gate_pre))
            silu = gate_pre * sigmoid
            value = silu * up_pre
            total = total + jnp.sum(
                value.astype(bfloat).astype(single) * grad_act, axis=1, keepdims=True
            )
            grad_act = grad_act * slot_weight
            act[half, :, lo:hi] = (value * slot_weight).astype(bfloat)
            grad_gate[half, :, lo:hi] = (
                grad_act * up_pre * sigmoid * (1.0 + gate_pre * (1.0 - sigmoid))
            ).astype(bfloat)
            grad_up[half, :, lo:hi] = (grad_act * silu).astype(bfloat)
        start_stores((2, 3, 4))
        back[half, :, width:] = jnp.where(here, total, 0.0).astype(bfloat)
        step = min(512, width)
        for lo in range(0, width, step):
            hi = lo + step
            part = matmul(grad_gate[half], gate_w[:, lo:hi])
            part = part + matmul(grad_up[half], up_w[:, lo:hi])
            back[half, :, lo:hi] = part.astype(bfloat)
        start_stores((5,))
        for lo in range(0, width, step):
            hi = lo + step
            out[half, :, lo:hi] = matmul(act[half], down_w[:, lo:hi]).astype(bfloat)
        start_stores((6,))
        return carry

    lax.fori_loop(0, 2, one_half, 0)
    for half in range(2):
        for which in range(7):
            store(half, which).wait()


def expert_call(
    step, steps, experts, expert, mine, theirs, grad_mine, grad_theirs, gate, up, down, kept
):
    count, wide = mine.shape
    hidden, width = gate.shape
    anywhere = pl.BlockSpec(memory_space=pl.ANY)
    back_shape = jax.ShapeDtypeStruct((count, wide), bfloat)
    out_shape = jax.ShapeDtypeStruct((count, width), bfloat)
    kept_shapes = [
        jax.ShapeDtypeStruct((steps * 2 * count, columns), bfloat)
        for columns in (width, width, hidden, hidden, hidden)
    ]
    outs = pl.pallas_call(
        functools.partial(expert_kernel, step * 2 * count, experts),
        in_specs=[pl.BlockSpec(memory_space=pltpu.SMEM)] + [anywhere] * (7 + len(kept)),
        out_specs=[anywhere] * 9,
        out_shape=[back_shape] * 2 + [out_shape] * 2 + kept_shapes,
        input_output_aliases={8 + i: 4 + i for i in range(len(kept))},
        scratch_shapes=[
            pltpu.VMEM((2, count, wide), bfloat),
            pltpu.VMEM((2, count, width), bfloat),
        ]
        + [pltpu.VMEM((hidden, width), bfloat)] * 3
        + [pltpu.VMEM((2, count, hidden), bfloat)] * 3
        + [pltpu.VMEM((2, count, wide), bfloat), pltpu.VMEM((2, count, width), bfloat)]
        + [pltpu.SemaphoreType.DMA((7,)), pltpu.SemaphoreType.DMA((2, 7))],
        compiler_params=pltpu.CompilerParams(vmem_limit_bytes=56 * 2**20),
        cost_estimate=pl.CostEstimate(
            flops=2 * 6 * 2 * count * width * hidden,
            bytes_accessed=2 * (12 * count * width + 3 * hidden * width + 6 * count * hidden),
            transcendentals=2 * count * hidden,
        ),
    )(expert, mine, theirs, grad_mine, grad_theirs, gate, up, down, *kept)
    return outs[:4], list(outs[4:])


def ring_next(value):
    size = lax.axis_size("ctx")
    return lax.ppermute(value, "ctx", [(i, (i + 1) % size) for i in range(size)])


def to_chips(value):
    size = lax.axis_size("fsdp")
    return lax.all_to_all(
        value,
        "fsdp",
        split_axis=0,
        concat_axis=0,
        tiled=True,
        axis_index_groups=[list(range(core, size, 2)) for core in range(2)],
    )


def to_core(value):
    size = lax.axis_size("fsdp")
    return lax.ppermute(value, "fsdp", [(i, i ^ 1) for i in range(size)])


def gather_rows(value):
    return lax.all_gather(value, "fsdp", axis=0, tiled=True)


def scatter_rows(value):
    return lax.psum_scatter(value.astype(bfloat), "fsdp", scatter_dimension=0, tiled=True)


def along_ctx(value, shift):
    size = lax.axis_size("ctx")
    return lax.ppermute(value, "ctx", [(i, (i + shift) % size) for i in range(size)])


def column_shares(value, device):
    size = lax.axis_size("ctx")
    count = value.shape[1] // size

    def share(owner):
        return lax.dynamic_slice_in_dim(value, owner % size * count, count, axis=1)

    return [share(device)] + [along_ctx(share(device + k), k) for k in range(1, size)]


def all_columns_of(part, device):
    pieces = [part] + [along_ctx(part, shift) for shift in range(1, lax.axis_size("ctx"))]
    return in_order([piece.astype(single) for piece in pieces], device, 1)


def ctx_spread(part, device):
    pieces = [part] + [along_ctx(part, shift) for shift in range(1, lax.axis_size("ctx"))]
    return in_order([piece.astype(single) for piece in pieces], device)


def sum_ctx(value):
    device = lax.axis_index("ctx")
    return ctx_spread(ctx_total(value, device).astype(bfloat), device)


def in_order(pieces, device, axis=0):
    size = len(pieces)
    count = pieces[0].shape[axis]
    shape = list(pieces[0].shape)
    shape[axis] = size * count
    result = jnp.zeros(shape, pieces[0].dtype)
    for shift, piece in enumerate(pieces):
        owner = (device - shift + size) % size
        result = lax.dynamic_update_slice_in_dim(result, piece, owner * count, axis=axis)
    return result


def together(*values):
    return lax.optimization_barrier(values)


def ctx_total(group, device):
    size = lax.axis_size("ctx")
    count = group.shape[0] // size

    def share(owner):
        return lax.dynamic_slice_in_dim(group, owner % size * count, count, axis=0)

    total = share(device).astype(single)
    for shift in range(1, size):
        total = total + along_ctx(share(device + shift), shift).astype(single)
    return total


def rank_table(route_block, experts, capacity):
    tokens = route_block.shape[0]
    expert_ids = jnp.arange(experts, dtype=jnp.int32)
    named = jnp.any(route_block[:, :, None] == expert_ids[None, None, :], axis=1)
    order = jnp.arange(tokens, dtype=jnp.int32)
    earlier = (order[:, None] > order[None, :]).astype(bfloat)
    rank = matmul(earlier, named.astype(bfloat)).astype(jnp.int32)
    return jnp.where(named & (rank < capacity), rank, -1)


def dispatch(rows):
    mine = to_chips(rows)
    return mine, to_core(mine)


def add_halves(mine, theirs):
    return (mine.astype(single) + to_core(theirs).astype(single)).astype(bfloat)


def local(
    layer_input,
    grad_output,
    routes,
    continuation_prompt,
    block_order,
    query_weight,
    latent_down,
    latent_up,
    output_weight,
    router_weight,
    shared_gate,
    shared_up,
    shared_down,
    attn_gain,
    latent_gain,
    ffn_gain,
    expert_gate,
    expert_up,
    expert_down,
):
    ctx_size = lax.axis_size("ctx")
    fsdp_size = lax.axis_size("fsdp")
    chips = fsdp_size // 2
    device = lax.axis_index("ctx")
    tokens = layer_input.shape[1]
    model_width = layer_input.shape[2]
    experts = router_weight.shape[1]
    group_tok = tokens * ctx_size
    block_len = PROMPT // (2 * ctx_size)
    cont_dev = CONTS * CONT_LEN // ctx_size
    capacity = (5 * tokens * TOP + 4 * experts - 1) // (4 * experts)
    slots = (capacity + 7) // 8 * 8
    score_scale = (NOPE + ROPE) ** (-0.5)
    shard_rows = latent_down.shape[0]
    down_width = latent_down.shape[1]
    hidden_dev = shared_down.shape[0] // ctx_size

    def hidden_columns(weight):
        parts = weight.reshape(shard_rows, fsdp_size, ctx_size, hidden_dev)
        return lax.dynamic_index_in_dim(parts, device, axis=2, keepdims=False).reshape(
            shard_rows, fsdp_size * hidden_dev
        )

    hidden_part = fsdp_size * hidden_dev
    part_down = lax.dynamic_slice_in_dim(shared_down, device * hidden_dev, hidden_dev, axis=0)
    part_shared = jnp.concatenate([hidden_columns(shared_gate), hidden_columns(shared_up)], axis=1)

    own_rows = jnp.arange(tokens, dtype=jnp.int32)
    link_table = continuation_prompt[0]
    own_seq, own_pos, own_link, own_rotary = row_layout(
        device, own_rows, block_order, link_table, block_len, cont_dev
    )
    prompt_rows = 2 * block_len
    first_cont = PROMPTS * prompt_rows
    link = lookup(link_table, (device * cont_dev // CONT_LEN)[None])
    key_pos = (block_order[:, None] * block_len + jnp.arange(block_len, dtype=jnp.int32)).reshape(-1)
    prompt_mask = jnp.where(key_pos[None, :] <= own_pos[:prompt_rows, None], 0.0, masked_score)
    cont_rows = device * cont_dev + jnp.arange(cont_dev, dtype=jnp.int32)
    cont_ids = jnp.arange(CONTS * CONT_LEN, dtype=jnp.int32)
    cont_mask = jnp.where(
        (cont_ids[None, :] // CONT_LEN == cont_rows[:, None] // CONT_LEN)
        & (cont_ids[None, :] <= cont_rows[:, None]),
        0.0,
        masked_score,
    )
    cos_table, sin_table = rotary_tables(own_rotary.astype(single))
    pair_cos = jnp.concatenate([cos_table] * 4, axis=1)
    pair_sin = jnp.concatenate([-sin_table, sin_table] * 2, axis=1)

    def by_sequence(group):
        blocks = group.reshape(ctx_size, tokens, -1)
        parts = [
            blocks[:, p * prompt_rows : (p + 1) * prompt_rows].reshape(PROMPT, -1)
            for p in range(PROMPTS)
        ]
        return jnp.concatenate(parts + [blocks[:, first_cont:].reshape(CONTS * CONT_LEN, -1)])

    def by_block(group):
        parts = [
            group[p * PROMPT : (p + 1) * PROMPT].reshape(ctx_size, prompt_rows, -1)
            for p in range(PROMPTS)
        ]
        last = group[PROMPTS * PROMPT :].reshape(ctx_size, cont_dev, -1)
        return jnp.concatenate(parts + [last], axis=1).reshape(group_tok, -1)

    plane_experts = device * chips + jnp.arange(chips, dtype=jnp.int32)
    chosen_here = plane_experts[:, None] == jnp.arange(experts, dtype=jnp.int32)[None, :]
    def here(table):
        return jnp.sum(jnp.where(chosen_here[:, None, :], table[None], 0), axis=2)

    slot_ids = jnp.arange(slots, dtype=jnp.int32)

    def pick_rows(step, rows):
        return jnp.einsum(
            "jrt,td->jrd", slot_pick[step], rows, preferred_element_type=single
        ).astype(bfloat)

    def put_rows(step, results):
        return jnp.einsum("jrt,jrd->td", slot_pick[step], results, preferred_element_type=single)

    def add_slots(route_block):
        ranks = rank_table(route_block, experts, capacity)
        match = here(ranks)[:, None, :] == slot_ids[None, :, None]
        slot_pick.append(match.astype(bfloat))
        return ranks

    slot_pick = []
    own_ranks = add_slots(routes[0])
    packed = gather_rows(
        jnp.concatenate(
            [
                latent_down,
                router_weight,
                attn_gain[:, None],
                ffn_gain[:, None],
                jnp.pad(latent_gain, (0, shard_rows - latent_gain.shape[0]))[:, None],
            ],
            axis=1,
        )
    )
    route_ring = [along_ctx(routes[0], s) for s in range(1, ctx_size)]
    grad_ring = [grad_output[0]]
    grad_next = ring_next(grad_ring[0])
    grad_mine = [to_chips(pick_rows(0, grad_ring[0]))]
    grad_theirs = []
    packed, query_shard, route_ring, grad_next, grad_mine[0] = together(
        packed, query_weight, route_ring, grad_next, grad_mine[0]
    )

    for route_block in route_ring:
        add_slots(route_block)
    full_down = packed[:, :down_width]
    full_router = packed[:, down_width : down_width + experts]
    gain_attn = packed[:, down_width + experts].astype(single)
    gain_ffn = packed[:, down_width + experts + 1].astype(single)
    gain_latent = (
        packed[:, down_width + experts + 2]
        .reshape(fsdp_size, shard_rows)[:, : latent_gain.shape[0]]
        .reshape(-1)
        .astype(single)
    )
    inputs_full = layer_input[0].astype(single)
    normed, attn_normal, attn_inverse = rms_forward(inputs_full, gain_attn)
    normed_low = normed.astype(bfloat)
    latent_pre = matmul(normed_low, full_down)
    latent, latent_normal, latent_inverse = rms_forward(latent_pre[:, :KV_RANK], gain_latent)
    latent_low = latent.astype(bfloat)
    key_rope_own = rotate(latent_pre[:, KV_RANK:], cos_table, sin_table).astype(bfloat)
    key_own = jnp.concatenate([latent_low, key_rope_own], axis=1)

    def more_grad_rows():
        step = len(grad_mine)
        grad_ring.append(grad_next)
        following = ring_next(grad_next) if step + 1 < ctx_size else grad_next
        theirs = to_core(grad_mine[-1])
        return following, theirs, to_chips(pick_rows(step, grad_ring[step]))

    full_query = gather_rows(query_shard)
    key_pieces = [key_own] + [along_ctx(key_own, s) for s in range(1, ctx_size)]
    grad_next, theirs, mine = more_grad_rows()
    full_query, up_shard, key_pieces, grad_next, theirs, mine = together(
        full_query, latent_up, key_pieces, grad_next, theirs, mine
    )
    grad_theirs.append(theirs)
    grad_mine.append(mine)

    full_up = gather_rows(up_shard)
    query_pre = matmul(normed_low, full_query)
    grad_next, theirs, mine = more_grad_rows()
    full_up, output_shard, query_pre, grad_next, theirs, mine = together(
        full_up, output_weight, query_pre, grad_next, theirs, mine
    )
    grad_theirs.append(theirs)
    grad_mine.append(mine)

    full_output = gather_rows(output_shard)
    key_group = by_sequence(in_order(key_pieces, device))
    latent_group = key_group[:, :KV_RANK]
    rope_pair = jnp.concatenate([key_group[:, KV_RANK:]] * 2, axis=1)
    kv_group = matmul(latent_group, full_up).astype(bfloat)
    rows_here = (prompt_rows, cont_dev)
    attended_low, log_total = attend(
        rows_here,
        score_scale,
        link,
        query_pre,
        pair_cos,
        pair_sin,
        kv_group,
        rope_pair,
        prompt_mask,
        cont_mask,
    )
    while len(grad_mine) < ctx_size:
        grad_next, theirs, mine = more_grad_rows()
        grad_theirs.append(theirs)
        grad_mine.append(mine)
    grad_group = jnp.concatenate(grad_ring)
    (
        full_output,
        shared_shard,
        down_shard,
        attended_low,
        grad_mine,
        grad_theirs,
        grad_group,
    ) = together(
        full_output,
        part_shared,
        part_down,
        attended_low,
        grad_mine,
        grad_theirs,
        grad_group,
    )
    grad_theirs.append(to_core(grad_mine[-1]))

    part_down = gather_rows(down_shard)
    hidden = inputs_full + matmul(attended_low, full_output)
    ffn_in, ffn_normal, ffn_inverse = rms_forward(hidden, gain_ffn)
    ffn_low = ffn_in.astype(bfloat)
    logits = matmul(ffn_low, full_router)
    router_exps = jnp.exp(logits - jnp.max(logits, axis=1, keepdims=True))
    router = router_exps / jnp.sum(router_exps, axis=1, keepdims=True)
    route_match = jnp.any(
        routes[0][:, :, None] == jnp.arange(experts, dtype=jnp.int32)[None, None, :], axis=1
    )
    chosen_total = jnp.sum(jnp.where(route_match, router, 0.0), axis=1, keepdims=True)
    gates = jnp.where(route_match, router, 0.0) / chosen_total
    pair_weight = jnp.where(own_ranks >= 0, gates, 0.0)

    weight_high = pair_weight.astype(bfloat)
    weight_low = (pair_weight - weight_high.astype(single)).astype(bfloat)
    ffn_wide = jnp.concatenate(
        [
            ffn_low,
            weight_high,
            weight_low,
            jnp.zeros((tokens, EXTRA - 2 * experts), bfloat),
        ],
        axis=1,
    )
    own_expert = (device * chips + lax.axis_index("fsdp") // 2)[None].astype(jnp.int32)
    kept = []
    out_sends = []

    def flat(rows):
        return rows.reshape(-1, rows.shape[-1])

    def expert_step(step, mine, theirs):
        results, kept[:] = expert_call(
            step,
            ctx_size,
            experts,
            own_expert,
            flat(mine),
            flat(theirs),
            flat(grad_mine[step]),
            flat(grad_theirs[step]),
            expert_gate[0].T,
            expert_up[0].T,
            expert_down[0],
            kept,
        )
        return [rows.reshape(chips, slots, -1) for rows in results]

    def shared_step(rows, grad_act):
        gate_pre = matmul(rows, part_gate)
        up_pre = matmul(rows, part_up)
        act = (jax.nn.silu(gate_pre) * up_pre).astype(bfloat)
        grad_gate, grad_up = silu_grads(grad_act, gate_pre, up_pre)
        back = jnp.einsum("tf,df->td", grad_gate, part_gate, preferred_element_type=single)
        back = back + jnp.einsum("tf,df->td", grad_up, part_up, preferred_element_type=single)
        return act, grad_gate, grad_up, back

    def shared_grads():
        group = jnp.concatenate(groups)
        act, grad_gate, grad_up = [
            jnp.concatenate([part[i] for part in shared]) for i in range(3)
        ]
        pieces = [
            jnp.einsum("ta,tb->ab", left, right, preferred_element_type=single).astype(bfloat)
            for left, right in ((group, grad_gate), (group, grad_up), (act, grad_group))
        ]
        return pieces

    last = ctx_size - 1
    ffn_ring = [ffn_wide]
    attended_ring = [attended_low]
    mines, theirs, backs, added, returned, out_added, out_steps = ({} for _ in range(7))
    shared, groups = [], []
    together_blocks = 4
    moving = None

    def of_block(which, step):
        first = step % together_blocks * tokens
        return shared[step // together_blocks][which][first : first + tokens]

    def block_part(step):
        part = put_rows(step, returned[step])
        return part + jnp.pad(of_block(3, step), ((0, 0), (0, EXTRA)))

    def hop(step):
        part = block_part(step)
        if moving is not None:
            part = part + moving.astype(single)
        return ring_next(part.astype(bfloat))

    for tick in range(ctx_size + 5):
        sent = {}
        if tick <= last:
            sent["mine"] = to_chips(pick_rows(tick, ffn_ring[tick]))
        if tick < last:
            sent["ring"] = ring_next(ffn_ring[tick])
        if 0 <= tick - 1 <= last:
            sent["theirs"] = to_core(mines[tick - 1])
        if 0 <= tick - 2 <= last:
            sent["back"] = expert_step(tick - 2, mines[tick - 2], theirs[tick - 2])
        if 0 <= tick - 3 <= last:
            sent["added"] = add_halves(*backs[tick - 3])
        if 0 <= tick - 4 <= last:
            sent["returned"] = to_chips(added[tick - 4])
        first = tick - 4
        if 0 <= first <= last and first % together_blocks == 0:
            sent["group"] = jnp.concatenate(
                [
                    block[:, :model_width]
                    for block in ffn_ring[first : first + together_blocks]
                ]
            )
        first = tick - 5
        if 0 <= first <= last and first % together_blocks == 0:
            rows = groups[-1].shape[0]
            shared.append(
                shared_step(groups[-1], grad_act[first * tokens : first * tokens + rows])
            )
            sent["shared"] = shared[-1]
        if 1 <= tick - 5 <= last:
            sent["moving"] = hop(tick - 5)
        if tick == 0:
            sent["grads"] = grad_theirs[-1]
        if tick == 0:
            sent["shard"] = shared_shard
        if tick == 3:
            sent["weights"] = part_shared
        if tick == 1:
            sent["down"] = part_down
            sent["grad_act"] = jnp.einsum(
                "td,fd->tf", grad_group, part_down, preferred_element_type=single
            )
        if tick == ctx_size + 2:
            sent["shared_all"] = (shared, groups, grad_group)
        if tick == ctx_size + 3:
            sent["shared_grads"] = shared_grads()
            sent["out"] = add_halves(*out_sends[1])
        if tick == ctx_size + 4:
            sent["shared_packed"] = jnp.concatenate(
                shared_pieces[:2] + [shared_pieces[2].reshape(model_width, hidden_part)], axis=1
            )
            sent["out_step"] = to_chips(out_added[1])
        if last <= tick < 2 * last:
            sent["attended"] = ring_next(attended_ring[-1])
        if tick == ctx_size + 4:
            sent["out"] = add_halves(*out_sends[2])
            sent["out_third"] = add_halves(*out_sends[3])
        names = sorted(sent)
        sent = dict(zip(names, together(*(sent[name] for name in names))))
        if "mine" in sent:
            mines[tick] = sent["mine"]
        if "ring" in sent:
            ffn_ring.append(sent["ring"])
        if "theirs" in sent:
            theirs[tick - 1] = sent["theirs"]
        if "back" in sent:
            backs[tick - 2] = sent["back"][:2]
            out_sends.append(sent["back"][2:])
        if "added" in sent:
            added[tick - 3] = sent["added"]
        if "returned" in sent:
            returned[tick - 4] = sent["returned"]
        if "group" in sent:
            groups.append(sent["group"])
        if "shared" in sent:
            shared[-1] = sent["shared"]
        if "shared_grads" in sent:
            shared_pieces = list(sent["shared_grads"])
        if "shared_all" in sent:
            shared, groups, grad_group = sent["shared_all"]
        if "attended" in sent:
            attended_ring.append(sent["attended"])
        if "out" in sent:
            out_added[tick - ctx_size - 2] = sent["out"]
        if "out_third" in sent:
            out_added[3] = sent["out_third"]
        if "out_step" in sent:
            out_steps[1] = sent["out_step"]
        moving = sent.get("moving", moving)
        if tick == 0:
            grad_theirs[-1] = sent["grads"]
        if "shard" in sent:
            part_shared = gather_rows(sent["shard"])
        if "down" in sent:
            part_down = sent["down"]
            grad_act = sent["grad_act"]
        if "weights" in sent:
            part_gate = sent["weights"][:, :hidden_part]
            part_up = sent["weights"][:, hidden_part:]

    while len(attended_ring) < ctx_size:
        attended_ring.append(ring_next(attended_ring[-1]))
    shared_part = scatter_rows(sent["shared_packed"])
    first_part = block_part(0)

    def next_out(step):
        ahead = (step + 1) % ctx_size
        return to_chips(out_added[step]), add_halves(*out_sends[ahead]) if step else out_added[step]

    grad_wide = moving.astype(single) + first_part
    grad_ffn = grad_wide[:, :model_width]
    grad_gate_pair = jnp.where(
        own_ranks >= 0, grad_wide[:, model_width : model_width + experts], 0.0
    )

    grad_low = grad_output[0]
    grad_top = grad_low.astype(single)
    grad_chosen = (
        grad_gate_pair - jnp.sum(grad_gate_pair * gates, axis=1, keepdims=True)
    ) / chosen_total
    grad_router = jnp.where(route_match, grad_chosen, 0.0)
    grad_logits = (
        router * (grad_router - jnp.sum(router * grad_router, axis=1, keepdims=True))
    ).astype(bfloat)
    grad_w_router = jnp.einsum("td,te->de", ffn_low, grad_logits, preferred_element_type=single)
    grad_ffn = grad_ffn + jnp.einsum(
        "te,de->td", grad_logits, full_router, preferred_element_type=single
    )
    grad_hidden_norm, grad_gain_ffn = rms_backward(grad_ffn, ffn_normal, ffn_inverse, gain_ffn)
    grad_hidden = grad_top + grad_hidden_norm
    grad_attn_low = grad_hidden.astype(bfloat)

    def out_hop(step, moving):
        part = put_rows(step, out_steps[step]) + matmul(of_block(0, step), part_down)
        if moving is not None:
            part = part + moving.astype(single)
        return ring_next(part.astype(bfloat))

    grad_attended = jnp.einsum(
        "td,vd->tv", grad_attn_low, full_output, preferred_element_type=single
    ).astype(bfloat)
    out_steps[2] = to_chips(out_added[2])
    out_moving = out_hop(2, out_hop(1, None))
    att_shares = column_shares(grad_attn_low, device)
    grad_attended, out_sends = together(grad_attended, out_sends)

    def weight_grad(left, right):
        return jnp.einsum("ra,rb->ab", left, right, preferred_element_type=single)

    grad_w_output = weight_grad(jnp.concatenate(attended_ring), jnp.concatenate(att_shares))

    out_steps[3] = to_chips(out_added[3])
    out_added[4 % ctx_size] = add_halves(*out_sends[4 % ctx_size])

    log_rows = log_total[:, :HEADS].T.reshape(HEADS // 2, 2, tokens)
    grad_nope, grad_rope, grad_key_part, grad_value_part, rope_pair_grad = attend_back(
        rows_here,
        score_scale,
        link,
        query_pre,
        pair_cos,
        pair_sin,
        kv_group,
        rope_pair,
        prompt_mask.T,
        cont_mask.T,
        log_rows,
        grad_attended,
    )
    (
        grad_nope,
        grad_rope,
        grad_key_part,
        grad_value_part,
        rope_pair_grad,
        out_steps[2],
        out_steps[3],
        out_added[4 % ctx_size],
        out_moving,
        shared_part,
        grad_w_output,
    ) = together(
        grad_nope,
        grad_rope,
        grad_key_part,
        grad_value_part,
        rope_pair_grad,
        out_steps[2],
        out_steps[3],
        out_added[4 % ctx_size],
        out_moving,
        shared_part,
        grad_w_output,
    )
    out_next = next_out(4 % ctx_size)
    output_part = scatter_rows(grad_w_output)
    grad_key_rope = rope_pair_grad[:, :ROPE] + rope_pair_grad[:, ROPE:]
    keys_width = HEADS * NOPE
    grad_latent_group = jnp.einsum(
        "tk,ck->tc", grad_key_part, full_up[:, :keys_width], preferred_element_type=single
    ) + jnp.einsum(
        "tk,ck->tc", grad_value_part, full_up[:, keys_width:], preferred_element_type=single
    )
    grad_query_pre = jnp.concatenate([grad_nope, grad_rope], axis=1)
    grad_w_query = weight_grad(normed_low, grad_query_pre)
    grad_keys_own = ctx_total(
        by_block(jnp.concatenate([grad_latent_group, grad_key_rope], axis=1).astype(bfloat)), device
    )
    grad_keys_own, output_part, grad_w_query, out_next, out_moving = together(
        grad_keys_own, output_part, grad_w_query, out_next, out_moving
    )
    out_steps[4 % ctx_size], out_added[5] = out_next
    for step in range(3, ctx_size):
        if step > 4:
            out_steps[step], out_added[(step + 1) % ctx_size] = next_out(step)
        out_moving = out_hop(step, out_moving)
    if ctx_size > 4:
        out_steps[0] = to_chips(out_added[0])
    query_part = scatter_rows(grad_w_query)
    shared_ring = [shared_part, ring_next(shared_part)]
    shared_ring.append(ring_next(shared_ring[-1]))
    sum_output = all_columns_of(output_part, device)
    grad_w_up = jnp.concatenate(
        [
            weight_grad(latent_group, part).astype(bfloat).reshape(model_width, -1)
            for part in (grad_key_part, grad_value_part)
        ],
        axis=1,
    )
    grad_latent = grad_keys_own[:, :KV_RANK]
    grad_rope_own = grad_keys_own[:, KV_RANK:]
    grad_latent_in, grad_gain_latent = rms_backward(
        grad_latent, latent_normal, latent_inverse, gain_latent
    )
    grad_rope_in = rotate(grad_rope_own, cos_table, -sin_table)
    grad_latent_pre = jnp.concatenate([grad_latent_in, grad_rope_in], axis=1).astype(bfloat)
    grad_w_down = jnp.einsum(
        "td,tk->dk",
        normed_low,
        jnp.pad(grad_latent_pre, ((0, 0), (0, -down_width % 128))),
        preferred_element_type=single,
    )
    grad_normed = jnp.einsum(
        "tq,dq->td", grad_query_pre, full_query, preferred_element_type=single
    ) + jnp.einsum("tk,dk->td", grad_latent_pre, full_down, preferred_element_type=single)
    grad_x_norm, grad_gain_attn = rms_backward(grad_normed, attn_normal, attn_inverse, gain_attn)
    grad_input = (grad_hidden + grad_x_norm).astype(bfloat)

    padded_latent = jnp.pad(
        grad_gain_latent.reshape(fsdp_size, -1),
        ((0, 0), (0, shard_rows - latent_gain.shape[0])),
    ).reshape(-1)
    up_width = grad_w_up.shape[1]
    small = jnp.concatenate(
        [
            grad_w_router,
            grad_gain_attn[:, None],
            grad_gain_ffn[:, None],
            padded_latent[:, None],
        ],
        axis=1,
    ).astype(bfloat)
    packed_grads = jnp.concatenate(
        [
            grad_w_up,
            grad_w_down.astype(bfloat),
            jnp.pad(small, ((0, 0), (0, -small.shape[1] % 128))),
        ],
        axis=1,
    )
    (
        query_part,
        packed_grads,
        shared_ring,
        kept,
        out_moving,
        out_steps[0],
        sum_output,
    ) = together(
        query_part, packed_grads, shared_ring, kept, out_moving, out_steps[0], sum_output
    )
    packed_part = scatter_rows(with_layout_constraint(packed_grads, by_rows))
    all_rows, all_grads, all_act, all_gate, all_up = kept
    grad_piece_down = weight_grad(all_act, all_grads)
    grad_piece_gate = weight_grad(all_rows, all_gate)
    sum_query = sum_ctx(query_part)
    packed_part, sum_query, grad_piece_down, grad_piece_gate, kept = together(
        packed_part, sum_query, grad_piece_down, grad_piece_gate, kept
    )
    all_rows, all_grads, all_act, all_gate, all_up = kept
    grad_piece_up = weight_grad(all_rows, all_up)
    while len(shared_ring) < ctx_size:
        shared_ring.append(ring_next(shared_ring[-1]))
    first_out = put_rows(0, out_steps[0]) + matmul(of_block(0, 0), part_down)
    layer_output = (hidden + out_moving.astype(single) + first_out).astype(bfloat)
    sum_packed = with_layout_constraint(
        sum_ctx(with_layout_constraint(packed_part, by_rows)), by_rows
    )
    sum_up = jnp.concatenate(
        [
            part.reshape(latent_up.shape[0], -1)
            for part in (sum_packed[:, : up_width // 2], sum_packed[:, up_width // 2 : up_width])
        ],
        axis=1,
    )
    sum_down = sum_packed[:, up_width : up_width + down_width]
    sum_small = sum_packed[:, up_width + grad_w_down.shape[1] :]
    sum_router = sum_small[:, :experts]
    sum_gain_attn = sum_small[:, experts]
    sum_gain_ffn = sum_small[:, experts + 1]
    sum_gain_latent = sum_small[: latent_gain.shape[0], experts + 2]

    shared_blocks = in_order([piece[None] for piece in shared_ring], device)

    def all_columns(blocks):
        blocks = blocks.reshape(ctx_size, shard_rows, fsdp_size, hidden_dev)
        return blocks.transpose(1, 2, 0, 3).reshape(shard_rows, -1).astype(single)

    sum_sh_gate = all_columns(shared_blocks[:, :, :hidden_part])
    sum_sh_up = all_columns(shared_blocks[:, :, hidden_part : 2 * hidden_part])
    sum_sh_down = shared_blocks[:, :, 2 * hidden_part :].reshape(shared_down.shape).astype(single)
    return (
        layer_output[None],
        grad_input[None],
        sum_query,
        sum_down,
        sum_up,
        sum_output,
        sum_router,
        sum_sh_gate,
        sum_sh_up,
        sum_sh_down,
        sum_gain_attn,
        sum_gain_latent,
        sum_gain_ffn,
        grad_piece_gate[None],
        grad_piece_up[None],
        grad_piece_down[None],
    )


def solution(mesh):
    in_specs = (
        P("fsdp", "ctx", None),
        P("fsdp", "ctx", None),
        P("fsdp", "ctx", None),
        P("fsdp", None),
        P(),
        P("fsdp", None),
        P("fsdp", None),
        P("fsdp", None),
        P("fsdp", None),
        P("fsdp", None),
        P("fsdp", None),
        P("fsdp", None),
        P("fsdp", None),
        P("fsdp"),
        P("fsdp"),
        P("fsdp"),
        P(("ctx", "fsdp"), None, None),
        P(("ctx", "fsdp"), None, None),
        P(("ctx", "fsdp"), None, None),
    )
    out_specs = (
        P("fsdp", "ctx", None),
        P("fsdp", "ctx", None),
        P("fsdp", None),
        P("fsdp", None),
        P("fsdp", None),
        P("fsdp", None),
        P("fsdp", None),
        P("fsdp", None),
        P("fsdp", None),
        P("fsdp", None),
        P("fsdp"),
        P("fsdp"),
        P("fsdp"),
        P(("ctx", "fsdp"), None, None),
        P(("ctx", "fsdp"), None, None),
        P(("ctx", "fsdp"), None, None),
    )
    return jax.shard_map(local, mesh=mesh, in_specs=in_specs, out_specs=out_specs, check_vma=False)
```
